256 devices in a mesh: dp: 4 (over y_lo, core), tensor: 64 (over y_hi, x, z).
Axes of the slice: x: 4, y: 4 (y_hi: 2, y_lo: 2; y = y_hi * 2 + y_lo), z: 8, core: 2. Of those that a mesh axis runs over, the one named last changes fastest.
Arguments:
- hidden: bfloat16 [1024, 5120], P('dp'), may hold values from -12 to 12, as said below
- head_weight: bfloat16 [5120, 81920], P('dp', 'tensor'), as said below
- prompt_ids: int32 [64, 32], P('dp'), may hold values from 0 to 81919, as said below
- prompt_counts: int32 [64, 32], P('dp'), may hold values from 1 to 8
- sampled_ids: int32 [64, 16], P('dp'), may hold values from 0 to 81919, as said below
- token_mask: int32 [64, 16], P('dp'), may hold values 0 or 1
- rewards: float32 [64], P('dp'), may hold values from -4 to 4
Outputs:
- logprobs: float32 [64, 16], P('dp')
- grad_hidden: bfloat16 [1024, 5120], P('dp')
- grad_weight: bfloat16 [5120, 81920], P('dp', 'tensor')
The draws below stay inside these ranges and needn't reach their ends.
Inputs may be any that keep to these rules, and one draw needn't show every extreme that they name: `hidden`: activations entering the head. `head_weight`: weights of the head. `prompt_ids`: ids counted in a row's prompt; an id may stand in several slots of a row, and its counts then add. `sampled_ids`: ids sampled at a row's positions.
All inputs are finite; a program needn't handle non-finite values. No bound on the sum of `token_mask` on one device may be relied on, other than what follows from the above.
Results may differ from the reference program's by a relative error of at most 0.009.
Values may be sent and summed in bfloat16 or wider, within the bound.
A program may use at most 128 MiB of HBM per device.

```python
import math
import jax
import jax.numpy as jnp
from jax import lax

D = 5120
V = 81920
RESP = 16
GROUP = 8
PSLOTS = 32
ROWS = 64
TOKENS = 1024
N_DP = 4


pool_width = 8


def shared_pool(key):
    return jax.random.randint(jax.random.fold_in(key, 201), (ROWS, pool_width), 0, V)


def anchor_vector(key):
    return jnp.clip(jax.random.normal(jax.random.fold_in(key, 101), (D,), jnp.float32), -6.0, 6.0)


def pin_extremes(token_ids, key):
    flattened = token_ids.reshape(-1)
    position = jax.random.randint(key, (), 0, flattened.shape[0] - 1)
    flattened = flattened.at[position].set(V - 1)
    flattened = flattened.at[position + 1].set(0)
    return flattened.reshape(token_ids.shape)


def pick_ids(pool_rows, key, slots):
    subkeys = jax.random.split(key, 4)
    pool_slot = jax.random.randint(subkeys[0], (ROWS, slots), 0, pool_width)
    from_pool = jnp.take_along_axis(pool_rows, pool_slot, axis=1)
    uniform_ids = jax.random.randint(subkeys[1], (ROWS, slots), 0, V)
    source_flag = jax.random.randint(subkeys[2], (ROWS, slots), 0, 2)
    token_ids = jnp.where(source_flag == 0, from_pool, uniform_ids)
    return pin_extremes(token_ids, subkeys[3])


def draw_prompt_ids(key, part):
    pool_rows = shared_pool(key)
    key = jax.random.fold_in(key, 11)
    return pick_ids(pool_rows, key, PSLOTS)


def draw_sampled_ids(key, part):
    pool_rows = shared_pool(key)
    key = jax.random.fold_in(key, 13)
    return pick_ids(pool_rows, key, RESP)


def draw_hidden(key, part):
    anchor = anchor_vector(key)
    key = jax.random.fold_in(key, 21)
    subkeys = jax.random.split(key, 1)
    values = jnp.clip(jax.random.normal(subkeys[0], (TOKENS, D), jnp.float32), -6.0, 6.0)
    strengths = jnp.array([0.8, 1.2, 1.6, 1.0], jnp.float32)
    values = values.at[TOKENS - 4:].set(strengths[:, None] * anchor[None, :])
    return values.astype(jnp.bfloat16)


def draw_head_weight(key, part):
    anchor = anchor_vector(key)
    key = jax.random.fold_in(key, 31)
    subkeys = jax.random.split(key, 3)
    factor = 3.0 / math.sqrt(D)
    aligned_factor = 150.0 / D
    column_scale = 1.0 + 0.075 * jnp.arange(V, dtype=jnp.float32) / V
    values = jnp.clip(jax.random.normal(subkeys[0], (D, V), jnp.float32), -6.0, 6.0) * column_scale[None, :] * factor
    lead_column = jax.random.randint(subkeys[1], (), 0, V)
    twin_column = (lead_column + V // 2 + 1) % V
    partner = jnp.clip(0.99 * anchor + 0.05 * jax.random.normal(subkeys[2], (D,), jnp.float32), -6.0, 6.0)
    values = values.at[:, lead_column].set(anchor * aligned_factor)
    values = values.at[:, twin_column].set(partner * aligned_factor)
    return values.astype(jnp.bfloat16)


def plant(drawn, key, low, largest):
    shape = drawn.shape
    spot = [jax.random.randint(jax.random.fold_in(key, axis), (), 0, shape[axis]) for axis in range(len(shape))]
    drawn = drawn.at[tuple(spot)].set(low)
    longest = shape.index(max(shape))
    spot[longest] = (spot[longest] + 1) % shape[longest]
    return drawn.at[tuple(spot)].set(largest)


def levels(stream_key, extent, shards, smallest, high):
    factor_of = 1.0
    for dim, parts in shards:
        draws = jax.random.uniform(jax.random.fold_in(jax.random.fold_in(stream_key, 6), dim), (parts,), jnp.float32, smallest / len(shards), high / len(shards))
        factor_of = factor_of * jnp.repeat(jnp.exp(draws), extent[dim] // parts).reshape((-1,) + (1,) * (len(extent) - 1 - dim))
    return factor_of


def scatter_about(rng, shape, deviation, limit, shards=(), kind=jnp.bfloat16):
    level = levels(rng, shape, shards, -0.22, 0.18) if shards else 1.0
    drawn = jax.random.normal(rng, shape, jnp.float32) * deviation * level
    return jnp.minimum(jnp.maximum(drawn, -limit), limit).astype(kind)


def setup_inputs(seed: int = 0) -> dict:
    streams_of = jax.random.split(jax.random.key(seed), 8)
    hidden = draw_hidden(jax.random.fold_in(streams_of[7], 71), 0)
    head_weight = draw_head_weight(jax.random.fold_in(streams_of[7], 71), 0)
    prompt_ids = draw_prompt_ids(jax.random.fold_in(streams_of[7], 71), 0)
    prompt_counts = plant(jax.random.randint(streams_of[3], (ROWS, PSLOTS), 1, 9), jax.random.fold_in(streams_of[3], 1), 1, 8).astype(jnp.int32)
    sampled_ids = draw_sampled_ids(jax.random.fold_in(streams_of[7], 71), 0)
    token_mask = plant((jax.random.randint(streams_of[5], (ROWS, RESP), 0, 4) < 3).astype(jnp.int32), jax.random.fold_in(streams_of[5], 1), 0, 1)
    rewards = scatter_about(streams_of[6], (ROWS,), 1.0, 4.0, ((0, 4),), jnp.float32)
    return dict(hidden=hidden, head_weight=head_weight, prompt_ids=prompt_ids, prompt_counts=prompt_counts, sampled_ids=sampled_ids, token_mask=token_mask, rewards=rewards)


recurrence_deduction = 0.4
presence_deduction = 0.6
division_coolness = 0.8


def reference(hidden, head_weight, prompt_ids, prompt_counts, sampled_ids, token_mask, rewards):
    lexicon_scores = jnp.dot(hidden, head_weight, preferred_element_type=jnp.float32)
    row_index = jnp.arange(ROWS, dtype=jnp.int32)[:, None]
    prompt_tile = jnp.zeros((ROWS, V), jnp.float32).at[row_index, prompt_ids].add(prompt_counts.astype(jnp.float32))
    vocab_ids = jnp.arange(V, dtype=jnp.int32)
    chosen_indicator = (sampled_ids[:, :, None] == vocab_ids[None, None, :]).astype(jnp.float32)
    prior = jnp.cumsum(chosen_indicator, axis=1) - chosen_indicator
    symbol_repeat_tally = (prompt_tile[:, None, :] + prior).reshape(TOKENS, V)
    chosen_indicator = chosen_indicator.reshape(TOKENS, V)
    symbol_present_marker = (symbol_repeat_tally > 0.0).astype(jnp.float32)
    cooled_scores = (lexicon_scores - recurrence_deduction * symbol_repeat_tally - presence_deduction * symbol_present_marker) / division_coolness
    row_top = jnp.max(cooled_scores, axis=1)
    row_total = jnp.sum(jnp.exp(cooled_scores - row_top[:, None]), axis=1)
    normalizer = row_top + jnp.log(row_total)
    picked = jnp.sum(chosen_indicator * cooled_scores, axis=1)
    logprobs = (picked - normalizer).reshape(ROWS, RESP)
    normalized_chances = jnp.exp(cooled_scores - normalizer[:, None])
    reward_groups = rewards.reshape(-1, GROUP)
    advantage = (reward_groups - jnp.mean(reward_groups, axis=1, keepdims=True)).reshape(-1)
    position_multiplier = (-(advantage[:, None] * token_mask.astype(jnp.float32))).reshape(-1)
    score_derivative = (position_multiplier[:, None] / division_coolness * (chosen_indicator - normalized_chances)).astype(jnp.bfloat16)
    grad_hidden = lax.dot_general(score_derivative, head_weight, (((1,), (1,)), ((), ())),
                                  preferred_element_type=jnp.float32).astype(jnp.bfloat16)
    block_tokens = TOKENS // N_DP
    weight_acc = jnp.zeros((D, V), jnp.float32)
    for block_index in range(N_DP):
        rows_part = hidden[block_index * block_tokens:(block_index + 1) * block_tokens]
        grad_part = score_derivative[block_index * block_tokens:(block_index + 1) * block_tokens]
        partial_term = lax.dot_general(rows_part, grad_part, (((0,), (0,)), ((), ())),
                                       preferred_element_type=jnp.float32).astype(jnp.bfloat16)
        partial_term = lax.optimization_barrier(partial_term)
        weight_acc = weight_acc + partial_term.astype(jnp.float32)
    return logprobs, grad_hidden, weight_acc.astype(jnp.bfloat16)
```

```python
import functools

import jax
import jax.numpy as jnp
from jax import lax
from jax.experimental import pallas as pl
from jax.experimental.pallas import tpu as pltpu
from jax.sharding import PartitionSpec as P

GROUP = 8
NX, NZ, NY = 4, 8, 4
MESH = pl.DeviceIdType.MESH
F32, BF16 = jnp.float32, jnp.bfloat16

recurrence_deduction = 0.4
presence_deduction = 0.6
division_coolness = 0.8


class Place:
    def __init__(self):
        dp, t = lax.axis_index("dp"), lax.axis_index("tensor")
        self.ylo, self.c = dp // 2, dp % 2
        self.yhi, self.x, self.z = t // 32, (t // 8) % 4, t % 8
        self.dp = dp

    def peer(self, x=0, y=0, z=0, c=0):
        yy = (self.yhi * 2 + self.ylo + y) % NY
        xx, zz, cc = (self.x + x) % NX, (self.z + z) % NZ, (self.c + c) % 2
        return ((yy % 2) * 2 + cc, (yy // 2) * 32 + xx * 8 + zz)


def meet(peers):
    barrier = pltpu.get_barrier_semaphore()
    for who in peers:
        pl.semaphore_signal(barrier, inc=1, device_id=who, device_id_type=MESH)
    pl.semaphore_wait(barrier, len(peers))


def send(src, dst, ssem, rsem, who):
    copy = pltpu.make_async_remote_copy(
        src_ref=src, dst_ref=dst, send_sem=ssem, recv_sem=rsem, device_id=who, device_id_type=MESH
    )
    copy.start()
    return copy


Z_PEERS = [dict(z=i) for i in range(1, NZ)]
XY_PEERS = [dict(x=i, y=j) for i in range(NX) for j in (0, 2) if (i, j) != (0, 0)]


def merge(m, l, p, others):
    top = m
    for o in others:
        top = jnp.maximum(top, o[0:2])
    l = l * jnp.exp(m - top)
    for o in others:
        l = l + o[2:4] * jnp.exp(o[0:2] - top)
        p = p + o[4:6]
    return top, l, p


def stats_kernel(s_ref, o_ref, mine, land, ssem, rsem):
    me = Place()
    meet([me.peer(**s) for s in Z_PEERS + XY_PEERS])
    m, l, p = s_ref[0:2], s_ref[2:4], s_ref[4:6]
    done = []
    for stage, peers in enumerate((Z_PEERS, XY_PEERS)):
        mine[stage] = jnp.concatenate([m, l, p, jnp.zeros_like(p)], axis=0)
        copies = []
        for i, s in enumerate(peers):
            k = stage * 7 + i
            copies.append(send(mine.at[stage], land.at[k], ssem.at[k], rsem.at[k], me.peer(**s)))
        for copy in copies:
            copy.wait_recv()
        done += copies
        m, l, p = merge(m, l, p, [land[stage * 7 + i] for i in range(7)])
    o_ref[...] = jnp.concatenate([m, l, p, jnp.zeros_like(p)], axis=0)
    for copy in done:
        copy.wait_send()


def combine_stats(stats):
    return pl.pallas_call(
        stats_kernel,
        out_shape=jax.ShapeDtypeStruct((8, 128), F32),
        in_specs=[pl.BlockSpec(memory_space=pltpu.VMEM)],
        out_specs=pl.BlockSpec(memory_space=pltpu.VMEM),
        scratch_shapes=[
            pltpu.VMEM((2, 8, 128), F32),
            pltpu.VMEM((14, 8, 128), F32),
            pltpu.SemaphoreType.DMA((14,)),
            pltpu.SemaphoreType.DMA((14,)),
        ],
        compiler_params=pltpu.CompilerParams(collective_id=0, has_side_effects=True),
        name="stats",
    )(stats)


CHAINS = [(1, 0, True), (-1, 1, True), (1, 1, False), (-1, 0, False)]


class Ring:
    def __init__(self, n, at, get, out, land, ssem, rsem, ahead, behind):
        self.n, self.at, self.get, self.out, self.land = n, at, get, out, land
        self.ssem, self.rsem, self.toward = ssem, rsem, {1: ahead, -1: behind}
        self.slots, self.copies = {}, {}
        for i, (d, half, far) in enumerate(CHAINS):
            for h in range(n // 2 - (0 if far else 1)):
                self.slots[i, h] = len(self.slots)

    def hops(self, i):
        return self.n // 2 - (0 if CHAINS[i][2] else 1)

    def step(self, h):
        for i, (d, half, far) in enumerate(CHAINS):
            if h >= self.hops(i):
                continue
            chunk = (self.at + d * (self.hops(i) - h) + self.n) % self.n
            term = self.get(half, chunk)
            if h:
                self.copies[i, h - 1].wait_recv()
                term = term + self.land[self.slots[i, h - 1]].astype(F32)
            k = self.slots[i, h]
            self.out[k] = term.astype(BF16)
            self.copies[i, h] = send(
                self.out.at[k], self.land.at[k], self.ssem.at[k], self.rsem.at[k], self.toward[d]
            )

    def total(self, half):
        term = self.get(half, self.at)
        for i, (d, hf, far) in enumerate(CHAINS):
            if hf == half:
                self.copies[i, self.hops(i) - 1].wait_recv()
                term = term + self.land[self.slots[i, self.hops(i) - 1]].astype(F32)
        return term

    def finish(self):
        for copy in self.copies.values():
            copy.wait_send()


def spread_ring(n, at, rows_of, out, ssem, rsem, ahead, behind):
    copies, k = {}, 0
    toward = {1: ahead, -1: behind}
    for h in range(n // 2):
        for i, (d, half, far) in enumerate(CHAINS):
            hops = n // 2 - (0 if far else 1)
            if h >= hops:
                continue
            if h:
                copies[i, h - 1].wait_recv()
            part = rows_of((at - d * h + n) % n, half)
            copies[i, h] = send(part(out), part(out), ssem.at[k], rsem.at[k], toward[d])
            k += 1
    for i, (d, half, far) in enumerate(CHAINS):
        copies[i, n // 2 - (0 if far else 1) - 1].wait_recv()
    for copy in copies.values():
        copy.wait_send()


X_PEERS = [dict(x=i) for i in range(1, NX)]
Y_PEERS = [dict(y=i, c=j) for i in range(NY) for j in range(2) if (i, j) != (0, 0)]


def grad_hidden_kernel(
    g_ref, w_ref, o_ref, part, zout, zland, xout, xland, z2, x2, z2land, x2land, ysum, yland,
    zs, zr, xs, xr, z2s, z2r, x2s, x2r, ys, yr, as_, ar, bs, br,
):
    me = Place()
    meet([me.peer(**s) for s in Z_PEERS + X_PEERS + Y_PEERS])

    @pl.loop(0, 4)
    def _(j):
        part[j] = lax.dot_general(
            g_ref[j], w_ref[...], (((1,), (1,)), ((), ())), preferred_element_type=F32
        )

    def z_get(half, chunk):
        return part[2 * half, pl.ds(pl.multiple_of(chunk * 32, 32), 32), :]

    def x_get(half, chunk):
        return part[2 * half + 1, pl.ds(pl.multiple_of(chunk * 64, 64), 64), :]

    zring = Ring(NZ, me.z, z_get, zout, zland, zs, zr, me.peer(z=1), me.peer(z=-1))
    xring = Ring(NX, me.x, x_get, xout, xland, xs, xr, me.peer(x=1), me.peer(x=-1))
    zring.step(0)
    xring.step(0)
    xring.step(1)
    zring.step(1)

    def cut(ref, at):
        rows = pl.ds(pl.multiple_of((at // 2) * 16, 16), 16)
        return ref.at[:, rows, pl.ds(pl.multiple_of((at % 2) * 640, 128), 640)]

    later = []
    for half in range(2):
        x2[half] = xring.total(half).astype(BF16)
    x_copies = []
    for i in range(1, NZ):
        x_copies.append(
            send(cut(x2, (me.z + i) % NZ), x2land.at[i - 1], x2s.at[i - 1], x2r.at[i - 1], me.peer(z=i))
        )
    zring.step(2)
    zring.step(3)
    for half in range(2):
        z2[half] = zring.total(half).astype(BF16)
    z_copies = []
    for i in range(1, NX):
        z_copies.append(
            send(cut(z2, (me.x + i) % NX), z2land.at[i - 1], z2s.at[i - 1], z2r.at[i - 1], me.peer(x=i))
        )
    for core, (own, land, copies) in enumerate(
        ((cut(z2, me.x), z2land, z_copies), (cut(x2, me.z), x2land, x_copies))
    ):
        for copy in copies:
            copy.wait_recv()
        term = own[...].astype(F32)
        for i in range(len(copies)):
            term = term + land[i].astype(F32)
        ysum[core] = term.astype(BF16)
        later += copies

    y_copies = {}
    for i, s in enumerate(Y_PEERS):
        piece = ysum.at[(me.c + s["c"]) % 2, (me.ylo + s["y"]) % 2]
        y_copies[s["y"], s["c"]] = send(piece, yland.at[i], ys.at[i], yr.at[i], me.peer(**s))
    row = jnp.where(me.c == 0, 32 * me.z + 16 * (me.x // 2), 64 * me.x + 16 * (me.z // 2))
    col = jnp.where(me.c == 0, me.x % 2, me.z % 2) * 640
    row, col = pl.multiple_of(row, 16), pl.multiple_of(col, 128)
    for dc in range(2):
        for dy in range(2):
            pair = []
            for y in (dy, dy + 2):
                if (y, dc) == (0, 0):
                    pair.append(ysum[me.c, me.ylo].astype(F32))
                else:
                    mirror = ((NY - y) % NY, dc)
                    y_copies[mirror].wait_recv()
                    pair.append(yland[Y_PEERS.index(dict(y=mirror[0], c=mirror[1]))].astype(F32))
            owner = ((me.ylo + dy) % 2) * 2 + (me.c + dc) % 2
            o_ref[owner, pl.ds(row, 16), pl.ds(col, 640)] = (pair[0] + pair[1]).astype(BF16)
    later += list(y_copies.values())

    def place(ref, r, n, cl, w):
        return ref.at[:, pl.ds(pl.multiple_of(r, 16), n), pl.ds(pl.multiple_of(cl, 128), w)]

    @pl.when(me.c == 0)
    def _():
        copies = []
        for i in range(1, NX):
            mine = place(o_ref, row, 16, col, 640)
            copies.append(send(mine, mine, as_.at[i - 1], ar.at[i - 1], me.peer(x=i)))
        for copy in copies:
            copy.wait_recv()
        spread_ring(
            NZ, me.z, lambda chunk, half: lambda ref: place(ref, 32 * chunk + 16 * half, 16, 0, 1280),
            o_ref, bs, br, me.peer(z=1), me.peer(z=-1),
        )
        for copy in copies:
            copy.wait_send()

    @pl.when(me.c == 1)
    def _():
        copies = []
        for i in range(1, NZ):
            mine = place(o_ref, row, 16, col, 640)
            copies.append(send(mine, mine, as_.at[i - 1], ar.at[i - 1], me.peer(z=i)))
        for copy in copies:
            copy.wait_recv()
        spread_ring(
            NX, me.x, lambda chunk, half: lambda ref: place(ref, 64 * chunk + 32 * half, 32, 0, 1280),
            o_ref, bs, br, me.peer(x=1), me.peer(x=-1),
        )
        for copy in copies:
            copy.wait_send()

    zring.finish()
    xring.finish()
    for copy in later:
        copy.wait_send()


def grad_hidden_of(grads, head_weight):
    vmem = pl.BlockSpec(memory_space=pltpu.VMEM)
    dma = lambda n: pltpu.SemaphoreType.DMA((n,))
    out = pl.pallas_call(
        grad_hidden_kernel,
        out_shape=jax.ShapeDtypeStruct((4, 256, 1280), BF16),
        in_specs=[vmem, vmem],
        out_specs=vmem,
        scratch_shapes=[
            pltpu.VMEM((4, 256, 1280), F32),
            pltpu.VMEM((14, 32, 1280), BF16),
            pltpu.VMEM((14, 32, 1280), BF16),
            pltpu.VMEM((6, 64, 1280), BF16),
            pltpu.VMEM((6, 64, 1280), BF16),
            pltpu.VMEM((2, 32, 1280), BF16),
            pltpu.VMEM((2, 64, 1280), BF16),
            pltpu.VMEM((3, 2, 16, 640), BF16),
            pltpu.VMEM((7, 2, 16, 640), BF16),
            pltpu.VMEM((2, 2, 16, 640), BF16),
            pltpu.VMEM((7, 16, 640), BF16),
            dma(14), dma(14), dma(6), dma(6), dma(3), dma(3), dma(7), dma(7), dma(7), dma(7),
            dma(7), dma(7), dma(14), dma(14),
        ],
        compiler_params=pltpu.CompilerParams(
            collective_id=1, has_side_effects=True, vmem_limit_bytes=50 << 20
        ),
        name="grad_hidden",
    )(grads.reshape(4, 256, 1280), head_weight)
    return jnp.transpose(out, (1, 0, 2)).reshape(256, 5120)


def penalty_tile(prompt_ids, prompt_counts, sampled_ids, vocab_offset, vocab_width):
    columns = vocab_offset + jnp.arange(vocab_width, dtype=jnp.int32)
    prompt_hits = prompt_ids[:, :, None] == columns[None, None, :]
    prompt_tile = jnp.sum(jnp.where(prompt_hits, prompt_counts[:, :, None], 0), axis=1).astype(F32)
    chosen_indicator = (sampled_ids[:, :, None] == columns[None, None, :]).astype(F32)
    resp_len = sampled_ids.shape[1]
    positions = jnp.arange(resp_len, dtype=jnp.int32)
    earlier = (positions[None, :] < positions[:, None]).astype(F32)
    prior = jnp.einsum("kq,rqv->rkv", earlier, chosen_indicator, precision=lax.Precision.HIGHEST)
    symbol_repeat_tally = prompt_tile[:, None, :] + prior
    return (symbol_repeat_tally.reshape(-1, vocab_width), chosen_indicator.reshape(-1, vocab_width))


def shards(hidden, head_weight, prompt_ids, prompt_counts, sampled_ids, token_mask, rewards):
    vocab_width = head_weight.shape[1]
    vocab_offset = lax.axis_index("tensor") * vocab_width
    symbol_repeat_tally, chosen_indicator = penalty_tile(
        prompt_ids, prompt_counts, sampled_ids, vocab_offset, vocab_width
    )
    group_slices = lax.all_to_all(hidden, "dp", split_axis=1, concat_axis=0, tiled=True)
    lexicon_scores = lax.psum_scatter(
        jnp.dot(group_slices, head_weight, preferred_element_type=F32),
        "dp",
        scatter_dimension=0,
        tiled=True,
    )
    symbol_present_marker = (symbol_repeat_tally > 0.0).astype(F32)
    cooled_scores = (
        lexicon_scores
        - recurrence_deduction * symbol_repeat_tally
        - presence_deduction * symbol_present_marker
    ) / division_coolness
    own_top = jnp.max(cooled_scores, axis=1)
    picked_local = jnp.sum(chosen_indicator * cooled_scores, axis=1)
    own_total = jnp.sum(jnp.exp(cooled_scores - own_top[:, None]), axis=1)
    stats = jnp.concatenate([own_top, own_total, picked_local, jnp.zeros_like(own_top)]).reshape(8, 128)
    stats = combine_stats(stats).reshape(4, 256)
    normalizer = stats[0] + jnp.log(stats[1])
    logprobs = (stats[2] - normalizer).reshape(sampled_ids.shape)
    normalized_chances = jnp.exp(cooled_scores - normalizer[:, None])
    reward_groups = rewards.reshape(-1, GROUP)
    advantage = (reward_groups - jnp.mean(reward_groups, axis=1, keepdims=True)).reshape(-1)
    position_multiplier = (-(advantage[:, None] * token_mask.astype(F32))).reshape(-1)
    score_derivative = (
        position_multiplier[:, None] / division_coolness * (chosen_indicator - normalized_chances)
    ).astype(BF16)
    portion = lax.all_gather(score_derivative, "dp", axis=0, tiled=True)
    grad_weight = lax.dot_general(
        group_slices, portion, (((0,), (0,)), ((), ())), preferred_element_type=F32
    ).astype(BF16)
    grad_hidden = grad_hidden_of(portion, head_weight)
    return (logprobs, grad_hidden, grad_weight)


def solution(mesh):
    return jax.shard_map(
        shards,
        mesh=mesh,
        in_specs=(
            P("dp", None),
            P("dp", "tensor"),
            P("dp", None),
            P("dp", None),
            P("dp", None),
            P("dp", None),
            P("dp"),
        ),
        out_specs=(P("dp", None), P("dp", None), P("dp", "tensor")),
        check_vma=False,
    )
```

```python
import functools

import jax
import jax.numpy as jnp
from jax import lax
from jax.experimental import pallas as pl
from jax.experimental.pallas import tpu as pltpu
from jax.sharding import PartitionSpec as P

GROUP = 8
NX, NZ, NY = 4, 8, 4
MESH = pl.DeviceIdType.MESH
F32, BF16 = jnp.float32, jnp.bfloat16

recurrence_deduction = 0.4
presence_deduction = 0.6
division_coolness = 0.8


class Place:
    def __init__(self):
        dp, t = lax.axis_index("dp"), lax.axis_index("tensor")
        self.ylo, self.c = dp // 2, dp % 2
        self.yhi, self.x, self.z = t // 32, (t // 8) % 4, t % 8
        self.dp = dp

    def peer(self, x=0, y=0, z=0, c=0):
        yy = (self.yhi * 2 + self.ylo + y + NY) % NY
        xx, zz, cc = (self.x + x + NX) % NX, (self.z + z + NZ) % NZ, (self.c + c) % 2
        return ((yy % 2) * 2 + cc, (yy // 2) * 32 + xx * 8 + zz)


def meet(peers):
    barrier = pltpu.get_barrier_semaphore()
    for who in peers:
        pl.semaphore_signal(barrier, inc=1, device_id=who, device_id_type=MESH)
    pl.semaphore_wait(barrier, len(peers))


def send(src, dst, ssem, rsem, who):
    copy = pltpu.make_async_remote_copy(
        src_ref=src, dst_ref=dst, send_sem=ssem, recv_sem=rsem, device_id=who, device_id_type=MESH
    )
    copy.start()
    return copy


Z_PEERS = [dict(z=i) for i in range(1, NZ)]
X_PEERS = [dict(x=i) for i in range(1, NX)]
Y_PEERS = [dict(y=i, c=j) for i in range(NY) for j in range(2) if (i, j) != (0, 0)]
XY_PEERS = [dict(x=i, y=j) for i in range(NX) for j in (0, 2) if (i, j) != (0, 0)]
ALL_PEERS = Z_PEERS + X_PEERS + Y_PEERS + [dict(x=i, y=2) for i in range(1, NX)]

WIDE, VOCAB, OWN, ALL = 1280, 1280, 256, 1024
STEP, STEPS = 32, 8
DIRECT = (1, 3)
EARLY, LATE = 0, 1
CHAINS = [(1, EARLY, True), (-1, LATE, True), (1, LATE, False), (-1, EARLY, False)]


def al(i, n):
    return pl.multiple_of(i, n)


class Ring:
    def __init__(self, n, at, get, out, land, ssem, rsem, ahead, behind):
        self.n, self.at, self.get, self.out, self.land = n, at, get, out, land
        self.ssem, self.rsem, self.toward = ssem, rsem, {1: ahead, -1: behind}
        self.slots, self.copies = {}, {}
        for i in range(len(CHAINS)):
            for h in range(self.hops(i)):
                self.slots[i, h] = len(self.slots)

    def hops(self, i):
        return self.n // 2 - (0 if CHAINS[i][2] else 1)

    def step(self, h, halves=(EARLY, LATE)):
        for i, (d, half, far) in enumerate(CHAINS):
            if h >= self.hops(i) or half not in halves:
                continue
            chunk = (self.at + d * (self.hops(i) - h) + self.n) % self.n
            term = self.get(half, chunk)
            if h:
                self.copies[i, h - 1].wait_recv()
                term = term + self.land[self.slots[i, h - 1]].astype(F32)
            k = self.slots[i, h]
            self.out[k] = term.astype(BF16)
            self.copies[i, h] = send(
                self.out.at[k], self.land.at[k], self.ssem.at[k], self.rsem.at[k], self.toward[d]
            )

    def total(self, half):
        term = self.get(half, self.at)
        for i, (d, hf, far) in enumerate(CHAINS):
            if hf == half:
                self.copies[i, self.hops(i) - 1].wait_recv()
                term = term + self.land[self.slots[i, self.hops(i) - 1]].astype(F32)
        return term

    def finish(self):
        for copy in self.copies.values():
            copy.wait_send()


def spread_ring(n, at, part, ssem, rsem, ahead, behind, between):
    copies, k = {}, 0
    toward = {1: ahead, -1: behind}
    for h in range(n // 2):
        for i, (d, half, far) in enumerate(CHAINS):
            hops = n // 2 - (0 if far else 1)
            if h >= hops:
                continue
            if h:
                copies[i, h - 1].wait_recv()
            piece = part((at - d * h + n) % n, half)
            copies[i, h] = send(piece, piece, ssem.at[k], rsem.at[k], toward[d])
            k += 1
        between(h)
    for i, (d, half, far) in enumerate(CHAINS):
        copies[i, n // 2 - (0 if far else 1) - 1].wait_recv()
    for copy in copies.values():
        copy.wait_send()


def merge(m, l, p, others):
    top = m
    for o in others:
        top = jnp.maximum(top, o[0:1])
    l = l * jnp.exp(m - top)
    for o in others:
        l = l + o[1:2] * jnp.exp(o[0:1] - top)
        p = p + o[2:3]
    return top, l, p


def rows_of(i, n):
    return pl.ds(al(i, n), n)


def kernel(
    hid_ref, w_hbm, pen_hbm, ids_ref, tw_ref, lp_ref, gh_ref, gw_ref,
    w_ref, pen_ref, hd, lex, pout, pland, xout, xland, lout, lland, chosen_ref, st, mine, sland,
    gr, part, zout, zland, xrout, xrland, z2, x2, z2land, x2land, ysum, yland, gather,
    loc, hs, hr, cs, cr, ps, pr, xs, xr, ls, lr, ss, sr, gs, grs,
    zs, zr, xrs, xrr, z2s, z2r, x2s, x2r, ys, yr, as_, ar, bs, br,
):
    me = Place()
    toward = 1 - 2 * me.ylo
    mate, across = me.peer(c=1), me.peer(y=toward)
    other = 2 * (1 - me.ylo)
    own, mates = me.dp, 2 * me.ylo + 1 - me.c

    copy_w = pltpu.make_async_copy(w_hbm, w_ref, loc.at[0])
    copy_h = pltpu.make_async_copy(
        hid_ref.at[:, pl.ds(al(own * WIDE, 128), WIDE)], hd.at[rows_of(own * OWN, OWN)], loc.at[1]
    )
    copy_p = pltpu.make_async_copy(pen_hbm, pen_ref, loc.at[2])
    copy_w.start()
    copy_h.start()
    copy_p.start()
    meet([me.peer(**s) for s in ALL_PEERS])

    def hidden_copy(rel, step, way):
        who = me.peer(y=way, c=rel)
        to = other + (me.c + rel) % 2
        k = rel * STEPS + step
        return pltpu.make_async_remote_copy(
            src_ref=hid_ref.at[rows_of(step * STEP, STEP), pl.ds(al(to * WIDE, 128), WIDE)],
            dst_ref=hd.at[rows_of(own * OWN + step * STEP, STEP)],
            send_sem=hs.at[k],
            recv_sem=hr.at[k],
            device_id=who,
            device_id_type=MESH,
        )

    to_mate = send(
        hid_ref.at[:, pl.ds(al(mates * WIDE, 128), WIDE)], hd.at[rows_of(own * OWN, OWN)],
        cs.at[0], cr.at[0], mate,
    )
    wrapped = [s for s in range(STEPS) if s not in DIRECT]
    hidden = {}
    for s in range(STEPS):
        for rel in range(2):
            hidden[rel, s] = hidden_copy(rel, s, toward if s in DIRECT else -toward)
    ahead = 2
    for s in DIRECT[:1] + tuple(wrapped[:ahead]) + DIRECT[1:]:
        for rel in range(2):
            hidden[rel, s].start()

    copy_w.wait()
    copy_h.wait()
    to_mate.wait_recv()

    @pl.loop(0, 4)
    def _(i):
        at = rows_of(mates * OWN + i * 64, 64)
        pout[rows_of(i * 64, 64)] = jnp.dot(hd[at, :], w_ref[...], preferred_element_type=F32)

    to_mate_part = send(pout, pland, ps.at[0], pr.at[0], mate)
    mine_of, mates_of = other + me.c, other + 1 - me.c
    exchanged, crossed = [], []
    for s in range(STEPS):
        for rel in range(2):
            hidden[rel, s].wait_recv()
        both = jnp.concatenate(
            [hd[rows_of(mates_of * OWN + s * STEP, STEP), :], hd[rows_of(mine_of * OWN + s * STEP, STEP), :]], axis=0
        )
        term = jnp.dot(both, w_ref[...], preferred_element_type=F32)
        xout[s] = term[:STEP]
        exchanged.append(send(xout.at[s], xland.at[s], xs.at[s], xr.at[s], mate))
        if s in wrapped:
            i = wrapped.index(s) + ahead
            if i < len(wrapped):
                for rel in range(2):
                    hidden[rel, wrapped[i]].start()
        exchanged[s].wait_recv()
        lout[s] = term[STEP:] + xland[s]
        crossed.append(send(lout.at[s], lland.at[s], ls.at[s], lr.at[s], across))
        if s == 1:

            @pl.loop(0, 4)
            def _(i):
                lex[rows_of(i * 64, 64)] = jnp.dot(
                    hd[rows_of(own * OWN + i * 64, 64), :], w_ref[...], preferred_element_type=F32
                )

    copy_p.wait()
    to_mate_part.wait_recv()
    lane = lax.broadcasted_iota(jnp.int32, (STEP, 128), 1)
    column = lax.broadcasted_iota(jnp.int32, (STEP, VOCAB), 1)
    for s in range(STEPS):
        crossed[s].wait_recv()
        at = pl.ds(s * STEP, STEP)
        scaled = (lex[at, :] + pland[at, :] + lland[s] - pen_ref[at, :]) * 1.25
        lex[at, :] = scaled
        chosen = column == ids_ref[at, :]
        m = jnp.max(scaled, axis=1, keepdims=True)
        l = jnp.sum(jnp.exp(scaled - m), axis=1, keepdims=True)
        p = jnp.sum(jnp.where(chosen, scaled, 0.0), axis=1, keepdims=True)
        st[at, :] = jnp.where(lane == 0, m, jnp.where(lane == 1, l, jnp.where(lane == 2, p, 0.0)))
    across_rows = st[...].T[0:8]
    m, l, p = across_rows[0:1], across_rows[1:2], across_rows[2:3]
    stats = []
    for stage, peers in enumerate((Z_PEERS, XY_PEERS)):
        mine[stage] = across_rows
        copies = []
        for i, s in enumerate(peers):
            k = stage * 7 + i
            copies.append(send(mine.at[stage], sland.at[k], ss.at[k], sr.at[k], me.peer(**s)))
        for copy in copies:
            copy.wait_recv()
        stats += copies
        m, l, p = merge(m, l, p, [sland[stage * 7 + i] for i in range(7)])
        across_rows = jnp.concatenate([m, l, p, jnp.zeros((5, OWN), F32)], axis=0)
    norm = m + jnp.log(l)
    lp_ref[...] = jnp.broadcast_to(p - norm, (8, OWN))
    st[...] = jnp.broadcast_to(norm, (128, OWN)).T

    for s in range(STEPS):
        at = pl.ds(s * STEP, STEP)
        chosen = jnp.where(column == ids_ref[at, :], 1.0, 0.0)
        g = tw_ref[at, :] * (chosen - jnp.exp(lex[at, :] - st[at, 0:1]))
        gr[rows_of(own * OWN + s * STEP, STEP)] = g.astype(BF16)
    grads = {}

    def grad_send(k, j, half, who):
        at = rows_of(j * OWN + half * 128, 128)
        grads[k] = send(gr.at[at], gr.at[at], gs.at[k], grs.at[k], who)

    for half in range(2):
        grad_send(half, own, half, across)
    for half in range(2):
        grad_send(2 + half, own, half, mate)

    def product(j):
        part[j] = lax.dot_general(
            gr[rows_of(j * OWN, OWN), :], w_ref[...], (((1,), (1,)), ((), ())), preferred_element_type=F32
        )

    def relay(half):
        grads[half].wait_recv()
        grad_send(4 + half, mine_of, half, mate)

    def z_get(half, chunk):
        ylo = me.ylo if half == EARLY else 1 - me.ylo
        return part[2 * ylo, rows_of(chunk * 32, 32), :]

    def x_get(half, chunk):
        ylo = me.ylo if half == EARLY else 1 - me.ylo
        return part[2 * ylo + 1, rows_of(chunk * 64, 64), :]

    zring = Ring(NZ, me.z, z_get, zout, zland, zs, zr, me.peer(z=1), me.peer(z=-1))
    xring = Ring(NX, me.x, x_get, xrout, xrland, xrs, xrr, me.peer(x=1), me.peer(x=-1))
    grads[2].wait_recv()
    grads[3].wait_recv()

    @pl.loop(0, 2)
    def _(i):
        product(2 * me.ylo + i)

    E, L = (EARLY,), (LATE,)
    zring.step(0, E)
    xring.step(0, E)
    zring.step(1, E)
    xring.step(1, E)
    relay(0)
    zring.step(2, E)
    relay(1)
    zring.step(3, E)
    grads[4].wait_recv()
    grads[5].wait_recv()

    @pl.loop(0, 2)
    def _(i):
        product(other + i)

    zring.step(0, L)
    xring.step(0, L)
    zring.step(1, L)
    xring.step(1, L)
    zring.step(2, L)

    def weight_tiles(lo, hi):
        @pl.loop(lo, hi)
        def _(i):
            cols = pl.ds(al(i * 128, 128), 128)
            gw_ref[cols, :] = lax.dot_general(
                hd[:, cols], gr[...], (((0,), (0,)), ((), ())), preferred_element_type=F32
            ).astype(BF16)

    def cut(ref, at):
        rows = rows_of((at // 2) * 16, 16)
        return ref.at[:, rows, pl.ds(al((at % 2) * 640, 128), 640)]

    later = []
    x2[me.ylo] = xring.total(EARLY).astype(BF16)
    x2[1 - me.ylo] = xring.total(LATE).astype(BF16)
    x_copies = []
    for i in range(1, NZ):
        x_copies.append(
            send(cut(x2, (me.z + i) % NZ), x2land.at[i - 1], x2s.at[i - 1], x2r.at[i - 1], me.peer(z=i))
        )
    zring.step(3, L)
    z2[me.ylo] = zring.total(EARLY).astype(BF16)
    z2[1 - me.ylo] = zring.total(LATE).astype(BF16)
    z_copies = []
    for i in range(1, NX):
        z_copies.append(
            send(cut(z2, (me.x + i) % NX), z2land.at[i - 1], z2s.at[i - 1], z2r.at[i - 1], me.peer(x=i))
        )
    weight_tiles(0, 2)
    for core, (ours, land, copies) in enumerate(
        ((cut(z2, me.x), z2land, z_copies), (cut(x2, me.z), x2land, x_copies))
    ):
        for copy in copies:
            copy.wait_recv()
        term = ours[...].astype(F32)
        for i in range(len(copies)):
            term = term + land[i].astype(F32)
        ysum[core] = term.astype(BF16)
        later += copies

    y_copies = {}
    for i, s in enumerate(Y_PEERS):
        piece = ysum.at[(me.c + s["c"]) % 2, (me.ylo + s["y"]) % 2]
        y_copies[s["y"], s["c"]] = send(piece, yland.at[i], ys.at[i], yr.at[i], me.peer(**s))
    weight_tiles(2, 4)
    row = jnp.where(me.c == 0, 32 * me.z + 16 * (me.x // 2), 64 * me.x + 16 * (me.z // 2))
    col = jnp.where(me.c == 0, me.x % 2, me.z % 2) * 640
    kept = lambda: (slice(None), rows_of(row, 16), pl.ds(al(col, 128), 640))
    for dc in range(2):
        for dy in range(2):
            pair = []
            for y in (dy, dy + 2):
                if (y, dc) == (0, 0):
                    pair.append(ysum[me.c, me.ylo].astype(F32))
                else:
                    mirror = ((NY - y) % NY, dc)
                    y_copies[mirror].wait_recv()
                    pair.append(yland[Y_PEERS.index(dict(y=mirror[0], c=mirror[1]))].astype(F32))
            owner = ((me.ylo + dy) % 2) * 2 + (me.c + dc) % 2
            gather[owner, rows_of(row, 16), pl.ds(al(col, 128), 640)] = (pair[0] + pair[1]).astype(BF16)
    later += list(y_copies.values())

    def gather_all(first, first_sems, ring, n, at, part_of, ahead, behind):
        copies = []
        for i, s in enumerate(first):
            piece = gather.at[kept()]
            copies.append(send(piece, piece, as_.at[i], ar.at[i], me.peer(**s)))
        weight_tiles(4, 6)
        for copy in copies:
            copy.wait_recv()
        spread_ring(n, at, part_of, bs, br, ahead, behind, lambda h: weight_tiles(6 + 2 * h, 8 + 2 * h) if h < 2 else None)
        for copy in copies:
            copy.wait_send()

    @pl.when(me.c == 0)
    def _():
        gather_all(
            X_PEERS, None, None, NZ, me.z,
            lambda chunk, half: gather.at[:, rows_of(32 * chunk + 16 * half, 16), :],
            me.peer(z=1), me.peer(z=-1),
        )

    @pl.when(me.c == 1)
    def _():
        gather_all(
            Z_PEERS, None, None, NX, me.x,
            lambda chunk, half: gather.at[:, rows_of(64 * chunk + 32 * half, 32), :],
            me.peer(x=1), me.peer(x=-1),
        )

    outs = []
    for s in range(4):
        copy = pltpu.make_async_copy(gather.at[s], gh_ref.at[:, pl.ds(s * WIDE, WIDE)], loc.at[3 + s])
        copy.start()
        outs.append(copy)
    zring.finish()
    xring.finish()
    to_mate.wait_send()
    to_mate_part.wait_send()
    for copy in later + exchanged + crossed + stats + list(hidden.values()) + list(grads.values()):
        copy.wait_send()
    for copy in outs:
        copy.wait()


def fused(hidden, head_weight, penalty, ids, weight):
    vmem = pl.BlockSpec(memory_space=pltpu.VMEM)
    hbm = pl.BlockSpec(memory_space=pl.ANY)
    dma = lambda n: pltpu.SemaphoreType.DMA((n,))
    buf = lambda *shape: pltpu.VMEM(shape, BF16)
    wide = lambda *shape: pltpu.VMEM(shape, F32)
    return pl.pallas_call(
        kernel,
        out_shape=(
            jax.ShapeDtypeStruct((8, OWN), F32),
            jax.ShapeDtypeStruct((OWN, 4 * WIDE), BF16),
            jax.ShapeDtypeStruct((WIDE, VOCAB), BF16),
        ),
        in_specs=[hbm, hbm, hbm, vmem, vmem],
        out_specs=(vmem, hbm, vmem),
        scratch_shapes=[
            buf(WIDE, VOCAB), wide(OWN, VOCAB), buf(ALL, WIDE), wide(OWN, VOCAB), wide(OWN, VOCAB), wide(OWN, VOCAB),
            wide(STEPS, STEP, VOCAB), wide(STEPS, STEP, VOCAB), wide(STEPS, STEP, VOCAB), wide(STEPS, STEP, VOCAB),
            wide(8, 128), wide(OWN, 128), wide(2, 8, OWN), wide(14, 8, OWN),
            buf(ALL, VOCAB), wide(4, OWN, WIDE),
            buf(14, 32, 1280), buf(14, 32, 1280), buf(6, 64, 1280), buf(6, 64, 1280),
            buf(2, 32, 1280), buf(2, 64, 1280), buf(3, 2, 16, 640), buf(7, 2, 16, 640), buf(2, 2, 16, 640),
            buf(7, 16, 640), buf(4, OWN, WIDE),
            dma(7), dma(16), dma(16), dma(1), dma(1), dma(1), dma(1), dma(8), dma(8), dma(8), dma(8),
            dma(14), dma(14), dma(6), dma(6),
            dma(14), dma(14), dma(6), dma(6), dma(3), dma(3), dma(7), dma(7), dma(7), dma(7),
            dma(7), dma(7), dma(14), dma(14),
        ],
        compiler_params=pltpu.CompilerParams(
            collective_id=0, has_side_effects=True, vmem_limit_bytes=56 << 20
        ),
        name="fused",
    )(hidden, head_weight, penalty, ids, weight)


def penalties(prompt_ids, prompt_counts, sampled_ids, vocab_offset, vocab_width):
    columns = vocab_offset + jnp.arange(vocab_width, dtype=jnp.int32)
    prompt_hits = prompt_ids[:, :, None] == columns[None, None, :]
    prompt_tile = jnp.sum(jnp.where(prompt_hits, prompt_counts[:, :, None], 0), axis=1).astype(F32)
    chosen = (sampled_ids[:, :, None] == columns[None, None, :]).astype(F32)
    positions = jnp.arange(sampled_ids.shape[1], dtype=jnp.int32)
    earlier = (positions[None, :] < positions[:, None]).astype(F32)
    prior = jnp.einsum("kq,rqv->rkv", earlier, chosen, precision=lax.Precision.HIGHEST)
    tally = (prompt_tile[:, None, :] + prior).reshape(-1, vocab_width)
    return recurrence_deduction * tally + presence_deduction * (tally > 0.0).astype(F32)


def shards(hidden, head_weight, prompt_ids, prompt_counts, sampled_ids, token_mask, rewards):
    vocab_width = head_weight.shape[1]
    vocab_offset = lax.axis_index("tensor") * vocab_width
    penalty = penalties(prompt_ids, prompt_counts, sampled_ids, vocab_offset, vocab_width)
    reward_groups = rewards.reshape(-1, GROUP)
    advantage = (reward_groups - jnp.mean(reward_groups, axis=1, keepdims=True)).reshape(-1)
    weight = (-(advantage[:, None] * token_mask.astype(F32))).reshape(-1, 1) / division_coolness
    ids = (sampled_ids - vocab_offset).reshape(-1, 1)
    logprobs, grad_hidden, grad_weight = fused(hidden, head_weight, penalty, ids, weight)
    return (logprobs[0].reshape(sampled_ids.shape), grad_hidden, grad_weight)


def solution(mesh):
    return jax.shard_map(
        shards,
        mesh=mesh,
        in_specs=(
            P("dp", None),
            P("dp", "tensor"),
            P("dp", None),
            P("dp", None),
            P("dp", None),
            P("dp", None),
            P("dp"),
        ),
        out_specs=(P("dp", None), P("dp", None), P("dp", "tensor")),
        check_vma=False,
    )
```

```python
import functools

import jax
import jax.numpy as jnp
from jax import lax
from jax.experimental import pallas as pl
from jax.experimental.pallas import tpu as pltpu
from jax.sharding import PartitionSpec as P

GROUP = 8
NX, NZ, NY = 4, 8, 4
MESH = pl.DeviceIdType.MESH
F32, BF16 = jnp.float32, jnp.bfloat16

recurrence_deduction = 0.4
presence_deduction = 0.6

class Place:
    def __init__(self):
        dp, t = lax.axis_index("dp"), lax.axis_index("tensor")
        self.ylo, self.c = dp // 2, dp % 2
        self.yhi, self.x, self.z = t // 32, (t // 8) % 4, t % 8
        self.dp = dp

    def peer(self, x=0, y=0, z=0, c=0):
        yy = (self.yhi * 2 + self.ylo + y + NY) % NY
        xx, zz, cc = (self.x + x + NX) % NX, (self.z + z + NZ) % NZ, (self.c + c) % 2
        return ((yy % 2) * 2 + cc, (yy // 2) * 32 + xx * 8 + zz)


def arrive(barrier, peers):
    for who in peers:
        pl.semaphore_signal(barrier, inc=1, device_id=who, device_id_type=MESH)


def send(src, dst, ssem, rsem, who):
    copy = pltpu.make_async_remote_copy(
        src_ref=src, dst_ref=dst, send_sem=ssem, recv_sem=rsem, device_id=who, device_id_type=MESH
    )
    copy.start()
    return copy


Z_PEERS = [dict(z=i) for i in range(1, NZ)]
X_PEERS = [dict(x=i) for i in range(1, NX)]
Y_PEERS = [dict(y=i, c=j) for i in range(NY) for j in range(2) if (i, j) != (0, 0)]
XY_PEERS = [dict(x=i, y=j) for i in range(NX) for j in (0, 2) if (i, j) != (0, 0)]
ALL_PEERS = Z_PEERS + X_PEERS + Y_PEERS + [dict(x=i, y=2) for i in range(1, NX)]

WIDE, VOCAB, OWN, ALL = 1280, 1280, 256, 1024
STEP, STEPS = 32, 8
DIRECT = (1, 3)
EARLY, LATE = 0, 1
CHAINS = [(d, half, sub, (d == 1) == (sub == 0)) for half in (EARLY, LATE) for sub in range(2) for d in (1, -1)]


def al(i, n):
    return pl.multiple_of(i, n)


class Ring:
    def __init__(self, n, at, get, out, land, ssem, rsem, ahead, behind):
        self.n, self.at, self.get, self.out, self.land = n, at, get, out, land
        self.ssem, self.rsem, self.toward = ssem, rsem, {1: ahead, -1: behind}
        self.slots, self.copies = {}, {}
        for i in range(len(CHAINS)):
            for h in range(self.hops(i)):
                self.slots[i, h] = len(self.slots)

    def hops(self, i):
        return self.n // 2 - (0 if CHAINS[i][3] else 1)

    def step(self, half, h):
        for i, (d, hf, sub, far) in enumerate(CHAINS):
            if h >= self.hops(i) or hf != half:
                continue
            chunk = (self.at + d * (self.hops(i) - h) + self.n) % self.n
            term = self.get(half, sub, chunk)
            if h:
                self.copies[i, h - 1].wait_recv()
                term = term + self.land[self.slots[i, h - 1]].astype(F32)
            k = self.slots[i, h]
            self.out[k] = term.astype(BF16)
            self.copies[i, h] = send(
                self.out.at[k], self.land.at[k], self.ssem.at[k], self.rsem.at[k], self.toward[d]
            )

    def total(self, half, sub):
        term = self.get(half, sub, self.at)
        for i, (d, hf, sb, far) in enumerate(CHAINS):
            if (hf, sb) == (half, sub):
                self.copies[i, self.hops(i) - 1].wait_recv()
                term = term + self.land[self.slots[i, self.hops(i) - 1]].astype(F32)
        return term

    def finish(self):
        for copy in self.copies.values():
            copy.wait_send()


def merge(m, l, p, others):
    top = m
    for o in others:
        top = jnp.maximum(top, o[0:1])
    l = l * jnp.exp(m - top)
    for o in others:
        l = l + o[1:2] * jnp.exp(o[0:1] - top)
        p = p + o[2:3]
    return top, l, p


def rows_of(i, n):
    return pl.ds(al(i, n), n)


def kernel(
    hid_ref, w_hbm, pid_ref, pc_ref, sid_ref, mask_ref, rew_ref, lp_ref, gh_ref, gw_ref,
    w_ref, hd, lex, pout, pland, xout, xland, lout, lland, prompt, id_ref, tw_ref, st, mine, sland, tab, cols,
    raw, gr, part, zout, zland, xrout, xrland, z2, x2, z2land, x2land, ysum, yland, gather,
    loc, hs, hr, cs, cr, ps, pr, xs, xr, ls, lr, ss, sr, gs, grs, ts, tr,
    zs, zr, xrs, xrr, z2s, z2r, x2s, x2r, ys, yr, as_, ar, bs, br,
):
    me = Place()
    toward = 1 - 2 * me.ylo
    mate, across, across_mate = me.peer(c=1), me.peer(y=toward), me.peer(y=toward, c=1)
    other = 2 * (1 - me.ylo)
    own, mates = me.dp, 2 * me.ylo + 1 - me.c
    mine_of, mates_of = other + me.c, other + 1 - me.c

    copy_w = pltpu.make_async_copy(w_hbm, w_ref, loc.at[0])
    copy_h = pltpu.make_async_copy(
        hid_ref.at[:, pl.ds(al(own * WIDE, 128), WIDE)], hd.at[rows_of(own * OWN, OWN)], loc.at[1]
    )
    copy_w.start()
    copy_h.start()
    peers = [me.peer(**s) for s in ALL_PEERS]
    barrier = pltpu.get_barrier_semaphore()
    arrive(barrier, peers)

    offset = (me.yhi * 32 + me.x * 8 + me.z) * VOCAB
    column = lax.broadcasted_iota(jnp.int32, (16, VOCAB), 1) + offset
    tile = jnp.zeros((16, VOCAB), F32)
    pid, pc = pid_ref[...], pc_ref[...].astype(F32)
    for j in range(pid.shape[1]):
        tile = tile + jnp.where(pid[:, j : j + 1] == column, pc[:, j : j + 1], 0.0)
    prompt[...] = tile
    diagonal = lax.broadcasted_iota(jnp.int32, (16, 16), 0) == lax.broadcasted_iota(jnp.int32, (16, 16), 1)
    which = lax.broadcasted_iota(jnp.int32, (16, 16), 0)
    advantage = jnp.zeros((16, 16), F32)
    for g in range(16 // GROUP):
        rewards = [rew_ref[g * GROUP + r] for r in range(GROUP)]
        mean = sum(rewards[1:], rewards[0]) * (1.0 / GROUP)
        for r in range(GROUP):
            advantage = jnp.where(which == g * GROUP + r, rewards[r] - mean, advantage)
    weight = -(advantage * mask_ref[...].astype(F32)) * 1.25
    sampled = sid_ref[...].astype(F32)
    for r in range(16):
        at = pl.ds(r * 16, 16)
        for ref, rows in ((id_ref, sampled), (tw_ref, weight)):
            turned = jnp.sum(jnp.where(diagonal, rows[r : r + 1, :], 0.0), axis=1, keepdims=True)
            ref[at, :] = jnp.broadcast_to(turned, (16, 128))
    pl.semaphore_wait(barrier, len(peers))

    def hidden_copy(rel, step, way):
        who = me.peer(y=way, c=rel)
        to = other + (me.c + rel) % 2
        k = rel * STEPS + step
        return pltpu.make_async_remote_copy(
            src_ref=hid_ref.at[rows_of(step * STEP, STEP), pl.ds(al(to * WIDE, 128), WIDE)],
            dst_ref=hd.at[rows_of(own * OWN + step * STEP, STEP)],
            send_sem=hs.at[k],
            recv_sem=hr.at[k],
            device_id=who,
            device_id_type=MESH,
        )

    wrapped = [s for s in range(STEPS) if s not in DIRECT]
    hidden = {}
    for s in range(STEPS):
        for rel in range(2):
            hidden[rel, s] = hidden_copy(rel, s, toward if s in DIRECT else -toward)
    ahead = 2
    for s in (wrapped[0],) + DIRECT[:1]:
        for rel in range(2):
            hidden[rel, s].start()
    to_mate = send(
        hid_ref.at[:, pl.ds(al(mates * WIDE, 128), WIDE)], hd.at[rows_of(own * OWN, OWN)],
        cs.at[0], cr.at[0], mate,
    )
    for s in tuple(wrapped[1:ahead]) + DIRECT[1:]:
        for rel in range(2):
            hidden[rel, s].start()

    copy_w.wait()
    copy_h.wait()
    to_mate.wait_recv()

    @pl.loop(0, 4)
    def _(i):
        at = rows_of(mates * OWN + i * 64, 64)
        pout[rows_of(i * 64, 64)] = jnp.dot(hd[at, :], w_ref[...], preferred_element_type=F32)

    to_mate_part = send(pout, pland, ps.at[0], pr.at[0], mate)
    exchanged, crossed = [], []
    for s in range(STEPS):
        for rel in range(2):
            hidden[rel, s].wait_recv()
        both = jnp.concatenate(
            [hd[rows_of(mates_of * OWN + s * STEP, STEP), :], hd[rows_of(mine_of * OWN + s * STEP, STEP), :]], axis=0
        )
        term = jnp.dot(both, w_ref[...], preferred_element_type=F32)
        xout[s] = term[:STEP]
        exchanged.append(send(xout.at[s], xland.at[s], xs.at[s], xr.at[s], mate))
        if s in wrapped:
            i = wrapped.index(s) + ahead
            if i < len(wrapped):
                for rel in range(2):
                    hidden[rel, wrapped[i]].start()
        exchanged[s].wait_recv()
        lout[s] = term[STEP:] + xland[s]
        crossed.append(send(lout.at[s], lland.at[s], ls.at[s], lr.at[s], across))
        if s == 1:

            @pl.loop(0, 4)
            def _(i):
                lex[rows_of(i * 64, 64)] = jnp.dot(
                    hd[rows_of(own * OWN + i * 64, 64), :], w_ref[...], preferred_element_type=F32
                )

    grads = {}

    def grad_send(k, src, j, lo, n, who):
        grads[k] = send(src, gr.at[rows_of(j * OWN + lo, n)], gs.at[k], grs.at[k], who)

    to_mate_part.wait_recv()
    lane = lax.broadcasted_iota(jnp.int32, (STEP, 128), 1)
    vocab = (lax.broadcasted_iota(jnp.int32, (STEP, VOCAB), 1) + offset).astype(F32)
    k_of = lax.broadcasted_iota(jnp.int32, (STEP, STEP), 0)
    q_of = lax.broadcasted_iota(jnp.int32, (STEP, STEP), 1)
    earlier = jnp.where((q_of < k_of) & (q_of // 16 == k_of // 16), 1.0, 0.0).astype(BF16)
    for s in range(STEPS):
        crossed[s].wait_recv()
        at = pl.ds(s * STEP, STEP)
        chosen = vocab == id_ref[at, 0:1]
        tally = jnp.dot(earlier, jnp.where(chosen, 1.0, 0.0).astype(BF16), preferred_element_type=F32)
        tally = tally + jnp.concatenate(
            [jnp.broadcast_to(prompt[2 * s + i : 2 * s + i + 1, :], (16, VOCAB)) for i in range(2)], axis=0
        )
        penalty = recurrence_deduction * tally + jnp.where(tally > 0.0, presence_deduction, 0.0)
        scaled = (lex[at, :] + pland[at, :] + lland[s] - penalty) * 1.25
        m = jnp.max(scaled, axis=1, keepdims=True)
        raised = jnp.exp(scaled - m)
        l = jnp.sum(raised, axis=1, keepdims=True)
        p = jnp.sum(jnp.where(chosen, scaled, 0.0), axis=1, keepdims=True)
        raw[at, :] = raised.astype(BF16)
        table = jnp.zeros((STEP, 128), F32)
        for i, v in enumerate((m, l, p, id_ref[at, 0:1], tw_ref[at, 0:1])):
            table = jnp.where(lane == i, v, table)
        st[at, :] = table
        if s % 2:
            lo, n = (s - 1) * STEP, 2 * STEP
            grad_send(s // 2, raw.at[pl.ds(lo, n)], own, lo, n, across)
        if s % 4 == 3:
            lo, n = (s - 3) * STEP, 4 * STEP
            grad_send(4 + s // 4, raw.at[pl.ds(lo, n)], own, lo, n, mate)
    first = st[...].T[0:8]
    m, l, p, chosen_id, weight = [first[i : i + 1] for i in range(5)]
    own_m, across_rows = m, first
    stats = []
    for stage, where in enumerate((Z_PEERS, XY_PEERS)):
        mine[stage] = across_rows
        copies = []
        for i, s in enumerate(where):
            k = stage * 7 + i
            copies.append(send(mine.at[stage], sland.at[k], ss.at[k], sr.at[k], me.peer(**s)))
        for copy in copies:
            copy.wait_recv()
        stats += copies
        m, l, p = merge(m, l, p, [sland[stage * 7 + i] for i in range(7)])
        across_rows = jnp.concatenate([m, l, p, jnp.zeros((5, OWN), F32)], axis=0)
    norm = m + jnp.log(l)
    logp = p - norm
    lp_ref[...] = jnp.concatenate([logp[:, 16 * r : 16 * r + 16] for r in range(16)], axis=0)

    tab[own] = jnp.concatenate(
        [weight * jnp.exp(own_m - norm), weight * (1.0 - jnp.exp(logp)), chosen_id, jnp.zeros((5, OWN), F32)], axis=0
    )
    tables = [send(tab.at[own], tab.at[own], ts.at[i], tr.at[i], who) for i, who in enumerate((mate, across, across_mate))]

    def turn(j, src, base):
        wide_rows = jnp.concatenate([tab[j], jnp.zeros((120, OWN), F32)], axis=0)
        cols[...] = wide_rows.T

        @pl.loop(0, OWN // STEP)
        def _(i):
            at, to = rows_of(i * STEP, STEP), rows_of(j * OWN + i * STEP, STEP)
            g = jnp.where(
                vocab == cols[at, 2:3], cols[at, 1:2], -cols[at, 0:1] * src[rows_of(base + i * STEP, STEP), :].astype(F32)
            )
            gr[to, :] = g.astype(BF16)

        part[j] = lax.dot_general(
            gr[rows_of(j * OWN, OWN), :], w_ref[...], (((1,), (1,)), ((), ())), preferred_element_type=F32
        )

    def relay(i):
        grads[i].wait_recv()
        grad_send(6 + i, gr.at[rows_of(mine_of * OWN + i * 64, 64)], mine_of, i * 64, 64, mate)

    def z_get(half, sub, chunk):
        ylo = me.ylo if half == EARLY else 1 - me.ylo
        return part[2 * ylo, rows_of(chunk * 32 + sub * 16, 16), :]

    def x_get(half, sub, chunk):
        ylo = me.ylo if half == EARLY else 1 - me.ylo
        return part[2 * ylo + 1, rows_of(chunk * 64 + sub * 32, 32), :]

    zring = Ring(NZ, me.z, z_get, zout, zland, zs, zr, me.peer(z=1), me.peer(z=-1))
    xring = Ring(NX, me.x, x_get, xrout, xrland, xrs, xrr, me.peer(x=1), me.peer(x=-1))
    relay(0)
    relay(1)
    turn(own, raw, 0)
    grads[4].wait_recv()
    grads[5].wait_recv()
    tables[0].wait_recv()
    turn(mates, gr, mates * OWN)
    zring.step(EARLY, 0)
    xring.step(EARLY, 0)
    relay(2)
    zring.step(EARLY, 1)
    relay(3)
    xring.step(EARLY, 1)
    for copy in tables[1:]:
        copy.wait_recv()
    for i in range(4):
        grads[6 + i].wait_recv()
        grads[6 + i].wait_send()

    @pl.loop(0, 2)
    def _(i):
        turn(other + i, gr, (other + i) * OWN)

    def weight_tiles(lo, hi):
        @pl.loop(lo, hi)
        def _(i):
            at = pl.ds(al(i * 128, 128), 128)
            gw_ref[at, :] = lax.dot_general(
                hd[:, at], gr[...], (((0,), (0,)), ((), ())), preferred_element_type=F32
            ).astype(BF16)

    zring.step(LATE, 0)
    xring.step(LATE, 0)
    zring.step(EARLY, 2)
    weight_tiles(0, 1)
    zring.step(LATE, 1)
    xring.step(LATE, 1)
    zring.step(EARLY, 3)
    weight_tiles(1, 2)

    def cut(ref, at):
        rows = rows_of((at // 2) * 16, 16)
        return ref.at[:, rows, pl.ds(al((at % 2) * 640, 128), 640)]

    later = []
    zring.step(LATE, 2)
    for half, ylo in ((EARLY, me.ylo), (LATE, 1 - me.ylo)):
        for sub in range(2):
            x2[ylo, pl.ds(sub * 32, 32)] = xring.total(half, sub).astype(BF16)
    x_copies = []
    for i in range(1, NZ):
        x_copies.append(
            send(cut(x2, (me.z + i) % NZ), x2land.at[i - 1], x2s.at[i - 1], x2r.at[i - 1], me.peer(z=i))
        )
    weight_tiles(2, 3)
    zring.step(LATE, 3)
    weight_tiles(3, 5)
    for half, ylo in ((EARLY, me.ylo), (LATE, 1 - me.ylo)):
        for sub in range(2):
            z2[ylo, pl.ds(sub * 16, 16)] = zring.total(half, sub).astype(BF16)
    z_copies = []
    for i in range(1, NX):
        z_copies.append(
            send(cut(z2, (me.x + i) % NX), z2land.at[i - 1], z2s.at[i - 1], z2r.at[i - 1], me.peer(x=i))
        )
    weight_tiles(5, 7)
    for core, (ours, land, copies) in enumerate(
        ((cut(z2, me.x), z2land, z_copies), (cut(x2, me.z), x2land, x_copies))
    ):
        for copy in copies:
            copy.wait_recv()
        term = ours[...].astype(F32)
        for i in range(len(copies)):
            term = term + land[i].astype(F32)
        ysum[core] = term.astype(BF16)
        later += copies

    y_copies = {}
    for i, s in enumerate(Y_PEERS):
        piece = ysum.at[(me.c + s["c"]) % 2, (me.ylo + s["y"]) % 2]
        y_copies[s["y"], s["c"]] = send(piece, yland.at[i], ys.at[i], yr.at[i], me.peer(**s))
    weight_tiles(7, 10)
    row = jnp.where(me.c == 0, 32 * me.z + 16 * (me.x // 2), 64 * me.x + 16 * (me.z // 2))
    col = jnp.where(me.c == 0, me.x % 2, me.z % 2) * 640
    for dc in range(2):
        for dy in range(2):
            pair = []
            for y in (dy, dy + 2):
                if (y, dc) == (0, 0):
                    pair.append(ysum[me.c, me.ylo].astype(F32))
                else:
                    mirror = ((NY - y) % NY, dc)
                    y_copies[mirror].wait_recv()
                    pair.append(yland[Y_PEERS.index(dict(y=mirror[0], c=mirror[1]))].astype(F32))
            owner = ((me.ylo + dy) % 2) * 2 + (me.c + dc) % 2
            gather[owner, rows_of(row, 16), pl.ds(al(col, 128), 640)] = (pair[0] + pair[1]).astype(BF16)
    later += list(y_copies.values())

    def gather_all(where, order, n, piece, ahead, behind):
        mine = piece(0, 0)
        firsts = [send(mine, mine, as_.at[i], ar.at[i], me.peer(**s)) for i, s in enumerate(where)]
        toward, copies = {1: ahead, -1: behind}, {}
        hops = lambda q, d: n // 2 - (0 if (d == 1) == (q % 2 == 0) else 1)
        for h in range(n // 2):
            for q in order:
                if h == 0 and q:
                    firsts[q - 1].wait_recv()
                for d in (1, -1):
                    if h >= hops(q, d):
                        continue
                    if h:
                        copies[q, d, h - 1].wait_recv()
                    part_of, k = piece(q, -d * h), len(copies)
                    copies[q, d, h] = send(part_of, part_of, bs.at[k], br.at[k], toward[d])
        for q in order:
            for d in (1, -1):
                copies[q, d, hops(q, d) - 1].wait_recv()
        for copy in firsts + list(copies.values()):
            copy.wait_send()

    def owned(row, at):
        return gather.at[:, rows_of(row + 16 * (at // 2), 16), pl.ds(al((at % 2) * 640, 128), 640)]

    @pl.when(me.c == 0)
    def _():
        piece = lambda q, far: owned(32 * ((me.z + far + NZ) % NZ), (me.x - q + NX) % NX)
        gather_all(X_PEERS, (0, 1, 3, 2), NZ, piece, me.peer(z=1), me.peer(z=-1))

    @pl.when(me.c == 1)
    def _():
        piece = lambda q, far: owned(64 * ((me.x + far + NX) % NX), (me.z - q + NZ) % NZ)
        gather_all(Z_PEERS, (0, 1, 7, 2, 6, 3, 5, 4), NX, piece, me.peer(x=1), me.peer(x=-1))

    outs = []
    for s in range(4):
        copy = pltpu.make_async_copy(gather.at[s], gh_ref.at[:, pl.ds(s * WIDE, WIDE)], loc.at[2 + s])
        copy.start()
        outs.append(copy)
    zring.finish()
    xring.finish()
    to_mate.wait_send()
    to_mate_part.wait_send()
    for copy in later + exchanged + crossed + stats + tables + list(hidden.values()) + [grads[i] for i in range(6)]:
        copy.wait_send()
    for copy in outs:
        copy.wait()


def fused(hidden, head_weight, prompt_ids, prompt_counts, sampled_ids, token_mask, rewards):
    vmem = pl.BlockSpec(memory_space=pltpu.VMEM)
    smem = pl.BlockSpec(memory_space=pltpu.SMEM)
    hbm = pl.BlockSpec(memory_space=pl.ANY)
    dma = lambda n: pltpu.SemaphoreType.DMA((n,))
    buf = lambda *shape: pltpu.VMEM(shape, BF16)
    wide = lambda *shape: pltpu.VMEM(shape, F32)
    return pl.pallas_call(
        kernel,
        out_shape=(
            jax.ShapeDtypeStruct((16, 16), F32),
            jax.ShapeDtypeStruct((OWN, 4 * WIDE), BF16),
            jax.ShapeDtypeStruct((WIDE, VOCAB), BF16),
        ),
        in_specs=[hbm, hbm, vmem, vmem, vmem, vmem, smem],
        out_specs=(vmem, hbm, vmem),
        scratch_shapes=[
            buf(WIDE, VOCAB), buf(ALL, WIDE), wide(OWN, VOCAB), wide(OWN, VOCAB), wide(OWN, VOCAB),
            wide(STEPS, STEP, VOCAB), wide(STEPS, STEP, VOCAB), wide(STEPS, STEP, VOCAB), wide(STEPS, STEP, VOCAB),
            wide(16, VOCAB), wide(OWN, 128), wide(OWN, 128), wide(OWN, 128), wide(2, 8, OWN), wide(14, 8, OWN),
            wide(4, 8, OWN), wide(OWN, 128),
            buf(OWN, VOCAB), buf(ALL, VOCAB), wide(4, OWN, WIDE),
            buf(28, 16, 1280), buf(28, 16, 1280), buf(12, 32, 1280), buf(12, 32, 1280),
            buf(2, 32, 1280), buf(2, 64, 1280), buf(3, 2, 16, 640), buf(7, 2, 16, 640), buf(2, 2, 16, 640),
            buf(7, 16, 640), buf(4, OWN, WIDE),
            dma(6), dma(16), dma(16), dma(1), dma(1), dma(1), dma(1), dma(8), dma(8), dma(8), dma(8),
            dma(14), dma(14), dma(10), dma(10), dma(3), dma(3),
            dma(28), dma(28), dma(12), dma(12), dma(3), dma(3), dma(7), dma(7), dma(7), dma(7),
            dma(7), dma(7), dma(28), dma(28),
        ],
        compiler_params=pltpu.CompilerParams(
            collective_id=0, has_side_effects=True, vmem_limit_bytes=56 << 20
        ),
        name="fused",
    )(hidden, head_weight, prompt_ids, prompt_counts, sampled_ids, token_mask, rewards)


def solution(mesh):
    return jax.shard_map(
        fused,
        mesh=mesh,
        in_specs=(
            P("dp", None),
            P("dp", "tensor"),
            P("dp", None),
            P("dp", None),
            P("dp", None),
            P("dp", None),
            P("dp"),
        ),
        out_specs=(P("dp", None), P("dp", None), P("dp", "tensor")),
        check_vma=False,
    )
```

```python
import functools

import jax
import jax.numpy as jnp
from jax import lax
from jax.experimental import pallas as pl
from jax.experimental.pallas import tpu as pltpu
from jax.sharding import PartitionSpec as P

GROUP = 8
NX, NZ, NY = 4, 8, 4
MESH = pl.DeviceIdType.MESH
F32, BF16 = jnp.float32, jnp.bfloat16

recurrence_deduction = 0.4
presence_deduction = 0.6

class Place:
    def __init__(self):
        dp, t = lax.axis_index("dp"), lax.axis_index("tensor")
        self.ylo, self.c = dp // 2, dp % 2
        self.yhi, self.x, self.z = t // 32, (t // 8) % 4, t % 8
        self.dp = dp

    def peer(self, x=0, y=0, z=0, c=0):
        yy = (self.yhi * 2 + self.ylo + y + NY) % NY
        xx, zz, cc = (self.x + x + NX) % NX, (self.z + z + NZ) % NZ, (self.c + c) % 2
        return ((yy % 2) * 2 + cc, (yy // 2) * 32 + xx * 8 + zz)

    def same_column(self, ylo, yhi, c):
        return (ylo * 2 + c, yhi * 32 + self.x * 8 + self.z)


def arrive(barrier, peers):
    for who in peers:
        pl.semaphore_signal(barrier, inc=1, device_id=who, device_id_type=MESH)


def transfer(src, dst, ssem, rsem, who):
    return pltpu.make_async_remote_copy(
        src_ref=src, dst_ref=dst, send_sem=ssem, recv_sem=rsem, device_id=who, device_id_type=MESH
    )


def send(src, dst, ssem, rsem, who):
    copy = transfer(src, dst, ssem, rsem, who)
    copy.start()
    return copy


Z_PEERS = [dict(z=i) for i in range(1, NZ)]
X_PEERS = [dict(x=i) for i in range(1, NX)]
Y_PEERS = [dict(y=i, c=j) for i in range(NY) for j in range(2) if (i, j) != (0, 0)]
XY_PEERS = [dict(x=i, y=j) for i in range(NX) for j in (0, 2) if (i, j) != (0, 0)]
ALL_PEERS = Z_PEERS + X_PEERS + Y_PEERS + [dict(x=i, y=2) for i in range(1, NX)]

WIDE, VOCAB, OWN, ALL = 1280, 1280, 256, 1024
STEP, STEPS = 32, 8
DIRECT = (1, 3)
EARLY, LATE = 0, 1
PART = 128

def al(i, n):
    return pl.multiple_of(i, n)


def merge(m, l, p, others):
    top = m
    for o in others:
        top = jnp.maximum(top, o[0:1])
    l = l * jnp.exp(m - top)
    for o in others:
        l = l + o[1:2] * jnp.exp(o[0:1] - top)
        p = p + o[2:3]
    return top, l, p


def rows_of(i, n):
    return pl.ds(al(i, n), n)


def kernel(
    hid_ref, w_hbm, pid_ref, pc_ref, sid_ref, mask_ref, rew_ref, lp_ref, gh_ref, gw_ref,
    w_ref, hd, lex, pout, pland, xout, xland, lout, lland, prompt, id_ref, tw_ref, st, mine, sland, tab, cols,
    raw, gr, part, z1land, x1land, s1z, s1x, z2land, x2land, s2, yland, gather,
    loc, hs, hr, cs, cr, ps, pr, xs, xr, ls, lr, ss, sr, gs, grs, ts, tr,
    z1s, z1r, x1s, x1r, z2s, z2r, x2s, x2r, ys, yr, as_, ar, bs, br,
):
    me = Place()
    toward = 1 - 2 * me.ylo
    mate, across, across_mate = me.peer(c=1), me.peer(y=toward), me.peer(y=toward, c=1)
    other = 2 * (1 - me.ylo)
    own, mates = me.dp, 2 * me.ylo + 1 - me.c
    mine_of, mates_of = other + me.c, other + 1 - me.c

    copy_w = pltpu.make_async_copy(w_hbm, w_ref, loc.at[0])
    copy_h = pltpu.make_async_copy(
        hid_ref.at[:, pl.ds(al(own * WIDE, 128), WIDE)], hd.at[rows_of(own * OWN, OWN)], loc.at[1]
    )
    copy_w.start()
    copy_h.start()
    peers = [me.peer(**s) for s in ALL_PEERS]
    barrier = pltpu.get_barrier_semaphore()
    arrive(barrier, peers)

    offset = (me.yhi * 32 + me.x * 8 + me.z) * VOCAB
    column = lax.broadcasted_iota(jnp.int32, (16, VOCAB), 1) + offset
    tile = jnp.zeros((16, VOCAB), F32)
    pid, pc = pid_ref[...], pc_ref[...].astype(F32)
    for j in range(pid.shape[1]):
        tile = tile + jnp.where(pid[:, j : j + 1] == column, pc[:, j : j + 1], 0.0)
    prompt[...] = tile
    diagonal = lax.broadcasted_iota(jnp.int32, (16, 16), 0) == lax.broadcasted_iota(jnp.int32, (16, 16), 1)
    which = lax.broadcasted_iota(jnp.int32, (16, 16), 0)
    advantage = jnp.zeros((16, 16), F32)
    for g in range(16 // GROUP):
        rewards = [rew_ref[g * GROUP + r] for r in range(GROUP)]
        mean = sum(rewards[1:], rewards[0]) * (1.0 / GROUP)
        for r in range(GROUP):
            advantage = jnp.where(which == g * GROUP + r, rewards[r] - mean, advantage)
    weight = -(advantage * mask_ref[...].astype(F32)) * 1.25
    sampled = sid_ref[...].astype(F32)
    for r in range(16):
        at = pl.ds(r * 16, 16)
        for ref, rows in ((id_ref, sampled), (tw_ref, weight)):
            turned = jnp.sum(jnp.where(diagonal, rows[r : r + 1, :], 0.0), axis=1, keepdims=True)
            ref[at, :] = jnp.broadcast_to(turned, (16, 128))
    pl.semaphore_wait(barrier, len(peers))

    def hidden_copy(rel, step, way):
        who = me.peer(y=way, c=rel)
        to = other + (me.c + rel) % 2
        k = rel * STEPS + step
        return pltpu.make_async_remote_copy(
            src_ref=hid_ref.at[rows_of(step * STEP, STEP), pl.ds(al(to * WIDE, 128), WIDE)],
            dst_ref=hd.at[rows_of(own * OWN + step * STEP, STEP)],
            send_sem=hs.at[k],
            recv_sem=hr.at[k],
            device_id=who,
            device_id_type=MESH,
        )

    wrapped = [s for s in range(STEPS) if s not in DIRECT]
    hidden = {}
    for s in range(STEPS):
        for rel in range(2):
            hidden[rel, s] = hidden_copy(rel, s, toward if s in DIRECT else -toward)
    ahead = 2
    for s in (wrapped[0],) + DIRECT[:1]:
        for rel in range(2):
            hidden[rel, s].start()
    to_mate = send(
        hid_ref.at[:, pl.ds(al(mates * WIDE, 128), WIDE)], hd.at[rows_of(own * OWN, OWN)],
        cs.at[0], cr.at[0], mate,
    )
    for s in tuple(wrapped[1:ahead]) + DIRECT[1:]:
        for rel in range(2):
            hidden[rel, s].start()

    copy_w.wait()
    copy_h.wait()
    to_mate.wait_recv()

    @pl.loop(0, 4)
    def _(i):
        at = rows_of(mates * OWN + i * 64, 64)
        pout[rows_of(i * 64, 64)] = jnp.dot(hd[at, :], w_ref[...], preferred_element_type=F32)

    to_mate_part = send(pout, pland, ps.at[0], pr.at[0], mate)
    exchanged, crossed = [], []
    for s in range(STEPS):
        for rel in range(2):
            hidden[rel, s].wait_recv()
        both = jnp.concatenate(
            [hd[rows_of(mates_of * OWN + s * STEP, STEP), :], hd[rows_of(mine_of * OWN + s * STEP, STEP), :]], axis=0
        )
        term = jnp.dot(both, w_ref[...], preferred_element_type=F32)
        xout[s] = term[:STEP]
        exchanged.append(send(xout.at[s], xland.at[s], xs.at[s], xr.at[s], mate))
        if s in wrapped:
            i = wrapped.index(s) + ahead
            if i < len(wrapped):
                for rel in range(2):
                    hidden[rel, wrapped[i]].start()
        exchanged[s].wait_recv()
        lout[s] = term[STEP:] + xland[s]
        crossed.append(send(lout.at[s], lland.at[s], ls.at[s], lr.at[s], across))
        if s == 1:

            @pl.loop(0, 4)
            def _(i):
                lex[rows_of(i * 64, 64)] = jnp.dot(
                    hd[rows_of(own * OWN + i * 64, 64), :], w_ref[...], preferred_element_type=F32
                )

    grads = {}
    lane = lax.broadcasted_iota(jnp.int32, (STEP, 128), 1)
    vocab = (lax.broadcasted_iota(jnp.int32, (STEP, VOCAB), 1) + offset).astype(F32)
    k_of = lax.broadcasted_iota(jnp.int32, (STEP, STEP), 0)
    q_of = lax.broadcasted_iota(jnp.int32, (STEP, STEP), 1)
    earlier = jnp.where((q_of < k_of) & (q_of // 16 == k_of // 16), 1.0, 0.0).astype(BF16)

    def grad_send(k, src, j, lo, n, who):
        grads[k] = send(src, gr.at[rows_of(j * OWN + lo, n)], gs.at[k], grs.at[k], who)

    def local(s):
        crossed[s].wait_recv()
        at = pl.ds(s * STEP, STEP)
        chosen = vocab == id_ref[at, 0:1]
        tally = jnp.dot(earlier, jnp.where(chosen, 1.0, 0.0).astype(BF16), preferred_element_type=F32)
        tally = tally + jnp.concatenate(
            [jnp.broadcast_to(prompt[2 * s + i : 2 * s + i + 1, :], (16, VOCAB)) for i in range(2)], axis=0
        )
        penalty = recurrence_deduction * tally + jnp.where(tally > 0.0, presence_deduction, 0.0)
        scaled = (lex[at, :] + pland[at, :] + lland[s] - penalty) * 1.25
        m = jnp.max(scaled, axis=1, keepdims=True)
        raised = jnp.exp(scaled - m)
        l = jnp.sum(raised, axis=1, keepdims=True)
        p = jnp.sum(jnp.where(chosen, scaled, 0.0), axis=1, keepdims=True)
        raw[at, :] = raised.astype(BF16)
        table = jnp.zeros((STEP, 128), F32)
        for i, v in enumerate((m, l, p, id_ref[at, 0:1], tw_ref[at, 0:1])):
            table = jnp.where(lane == i, v, table)
        st[at, :] = table
        if s % 2:
            lo, n = (s - 1) * STEP, 2 * STEP
            grad_send(s // 2, raw.at[pl.ds(lo, n)], own, lo, n, across)
        if s % 4 == 3:
            lo, n = (s - 3) * STEP, PART
            grad_send(4 + s // 4, raw.at[pl.ds(lo, n)], own, lo, n, mate)

    stats, held, tables = {}, {}, {}

    def stats_send(t, stage, rows):
        mine[t, stage] = rows
        for i, s in enumerate((Z_PEERS, XY_PEERS)[stage]):
            k = (t * 2 + stage) * 7 + i
            stats[k] = send(mine.at[t, stage], sland.at[k], ss.at[k], sr.at[k], me.peer(**s))

    def stats_merge(t, stage, m, l, p):
        ks = [(t * 2 + stage) * 7 + i for i in range(7)]
        for k in ks:
            stats[k].wait_recv()
        return merge(m, l, p, [sland[k] for k in ks])

    def stats_begin(t):
        first = st[pl.ds(t * PART, PART), :].T[0:8]
        held[t] = [first[i : i + 1] for i in range(5)]
        stats_send(t, 0, first)

    def stats_middle(t):
        m, l, p = stats_merge(t, 0, *held[t][:3])
        held[t] += [m, l, p]
        stats_send(t, 1, jnp.concatenate([m, l, p, jnp.zeros((5, PART), F32)], axis=0))

    def stats_end(t):
        own_m, _, _, chosen_id, weight, m, l, p = held[t]
        m, l, p = stats_merge(t, 1, m, l, p)
        norm = m + jnp.log(l)
        logp = p - norm
        lp_ref[pl.ds(t * 8, 8), :] = jnp.concatenate([logp[:, 16 * r : 16 * r + 16] for r in range(8)], axis=0)
        tab[own, t] = jnp.concatenate(
            [weight * jnp.exp(own_m - norm), weight * (1.0 - jnp.exp(logp)), chosen_id, jnp.zeros((5, PART), F32)],
            axis=0,
        )
        for i, who in enumerate((mate, across, across_mate)):
            k = t * 3 + i
            tables[k] = send(tab.at[own, t], tab.at[own, t], ts.at[k], tr.at[k], who)

    def turn(j, t, source, base):
        cols[...] = jnp.concatenate([tab[j, t], jnp.zeros((120, PART), F32)], axis=0).T

        @pl.loop(0, PART // STEP)
        def _(i):
            at, lo = rows_of(i * STEP, STEP), t * PART + i * STEP
            e = source[rows_of(base + lo, STEP), :].astype(F32)
            g = jnp.where(vocab == cols[at, 2:3], cols[at, 1:2], -cols[at, 0:1] * e)
            gr[rows_of(j * OWN + lo, STEP)] = g.astype(BF16)

        part[j, pl.ds(t * PART, PART)] = lax.dot_general(
            gr[rows_of(j * OWN + t * PART, PART), :], w_ref[...], (((1,), (1,)), ((), ())),
            preferred_element_type=F32,
        ).astype(BF16)

    def relay(i):
        grads[i].wait_recv()
        grad_send(6 + i, gr.at[rows_of(mine_of * OWN + i * 64, 64)], mine_of, i * 64, 64, mate)

    def turn_early(t):
        turn(own, t, raw, 0)
        grads[4 + t].wait_recv()
        tables[t * 3].wait_recv()
        turn(mates, t, gr, mates * OWN)

    def turn_late(t):
        for k in (1, 2):
            tables[t * 3 + k].wait_recv()
        for i in (2 * t, 2 * t + 1):
            grads[6 + i].wait_recv()
            grads[6 + i].wait_send()

        @pl.loop(0, 2)
        def _(i):
            turn(other + i, t, gr, (other + i) * OWN)

    one, two, column_y = {}, {}, {}
    ylo_of = {EARLY: me.ylo, LATE: 1 - me.ylo}

    def z_rows(t, half, q):
        return part.at[2 * ylo_of[half], rows_of(t * PART + 16 * q, 16)]

    def x_rows(t, half, q):
        return part.at[2 * ylo_of[half] + 1, rows_of(t * PART + 32 * q, 32)]

    def one_send(t, half):
        for i in (4, 3, 5, 2, 6, 1, 7):
            k = (t * 2 + half) * 7 + i - 1
            one["z", k] = send(
                z_rows(t, half, (me.z + i) % NZ), z1land.at[k], z1s.at[k], z1r.at[k], me.peer(z=i)
            )
        for i in (2, 1, 3):
            k = (t * 2 + half) * 3 + i - 1
            one["x", k] = send(
                x_rows(t, half, (me.x + i) % NX), x1land.at[k], x1s.at[k], x1r.at[k], me.peer(x=i)
            )

    def one_total(axis, t, half):
        n, land = (7, z1land) if axis == "z" else (3, x1land)
        term = (z_rows(t, half, me.z) if axis == "z" else x_rows(t, half, me.x))[...].astype(F32)
        for i in range(n):
            k = (t * 2 + half) * n + i
            one[axis, k].wait_recv()
            term = term + land[k].astype(F32)
        return term.astype(BF16)

    def half_cols(i):
        return pl.ds(al((i % 2) * 640, 128), 640)

    def z_cut(t, x):
        return s1z.at[t, x // 2, :, half_cols(x)]

    def x_cut(t, z):
        return s1x.at[t, (z // 2) % 2, rows_of((z // 4) * 16, 16), half_cols(z)]

    def two_send_x(t):
        for half in (EARLY, LATE):
            s1x[t, ylo_of[half]] = one_total("x", t, half)
        for i in (4, 3, 5, 2, 6, 1, 7):
            k = t * 7 + i - 1
            two["x", k] = send(x_cut(t, (me.z + i) % NZ), x2land.at[k], x2s.at[k], x2r.at[k], me.peer(z=i))

    def two_send_z(t):
        for half in (EARLY, LATE):
            s1z[t, ylo_of[half]] = one_total("z", t, half)
        for i in (2, 1, 3):
            k = t * 3 + i - 1
            two["z", k] = send(z_cut(t, (me.x + i) % NX), z2land.at[k], z2s.at[k], z2r.at[k], me.peer(x=i))

    slot = (me.yhi * 2 + me.ylo) * 2 + me.c
    kept_by = (me.x // 2, (me.z // 2) % 2)
    keeps = ((me.c == 0) & (kept_by[0] == me.ylo)) | ((me.c == 1) & (kept_by[1] == me.ylo))

    def y_copy(t, core, yhi):
        k = t * 4 + core * 2 + yhi
        to = me.same_column(kept_by[core], yhi, core)
        return transfer(s2.at[t, core], yland.at[t, slot], ys.at[k], yr.at[t * 8 + slot], to)

    def y_each(t, act):
        for core in range(2):
            for yhi in range(2):

                @pl.when((me.c != core) | (me.ylo != kept_by[core]) | (me.yhi != yhi))
                def _():
                    act(y_copy(t, core, yhi))

    def y_send(t):
        for core, (axis, ours, land, n) in enumerate(
            (("z", z_cut(t, me.x), z2land, 3), ("x", x_cut(t, me.z), x2land, 7))
        ):
            term = ours[...].astype(F32)
            for i in range(n):
                k = t * n + i
                two[axis, k].wait_recv()
                term = term + land[k].astype(F32)
            s2[t, core] = term.astype(BF16)
        y_each(t, lambda copy: copy.start())

        @pl.when(keeps)
        def _():
            yland[t, slot] = s2[t, me.c]

    def piece(t, x, z):
        row = jnp.where(me.c == 0, 16 * z, 32 * x + 16 * (z // 4))
        col = jnp.where(me.c == 0, x % 2, z % 2) * 640
        return gather.at[:, rows_of(t * PART + row, 16), pl.ds(al(col, 128), 640)]

    def first_out(t, core, i):
        at, k = piece(t, me.x, me.z), t * 7 + i - 1
        return transfer(at, at, as_.at[k], ar.at[k], me.peer(x=i) if core == 0 else me.peer(z=i))

    def first_in(t, core, i):
        x, z = ((me.x - i + NX) % NX, me.z) if core == 0 else (me.x, (me.z - i + NZ) % NZ)
        at, k = piece(t, x, z), t * 7 + i - 1
        return transfer(at, at, as_.at[k], ar.at[k], me.peer(x=-i) if core == 0 else me.peer(z=-i))

    def y_take(t):
        @pl.when(keeps)
        def _():
            for k in range(8):

                @pl.when(k != slot)
                def _():
                    transfer(
                        s2.at[t, 0], yland.at[t, k], ys.at[t * 4], yr.at[t * 8 + k], mate
                    ).wait_recv()

            mine_at = piece(t, me.x, me.z)
            for s in range(4):
                k = (s // 2) * 2 + s % 2
                pair = yland[t, k].astype(F32) + yland[t, k + 4].astype(F32)
                mine_at.at[s][...] = pair.astype(BF16)

            for core in range(2):

                @pl.when(me.c == core)
                def _():
                    for i in ((2, 1, 3), (4, 3, 5, 2, 6, 1, 7))[core]:
                        first_out(t, core, i).start()

    def z_rows_of(t, z, halves=None):
        at = gather.at[:, rows_of(t * PART + 16 * ((z + NZ) % NZ), 16)]
        return at if halves is None else at.at[:, :, pl.ds(halves * 640, 640)]

    def x_rows_of(t, x):
        return gather.at[:, rows_of(t * PART + 32 * ((x + NX) % NX), 32)]

    Z_STEPS = [(2, 2, None), (-2, -2, None), (1, 1, None), (-1, -1, None), (1, 3, None), (-1, -3, None), (2, 4, 0), (-2, -4, 1)]

    def z_out(t, k):
        away, origin, halves = Z_STEPS[k]
        at = z_rows_of(t, me.z - (origin - away), halves)
        return transfer(at, at, bs.at[t * 8 + k], br.at[t * 8 + k], me.peer(z=away))

    def z_in(t, k):
        away, origin, halves = Z_STEPS[k]
        at = z_rows_of(t, me.z - origin, halves)
        return transfer(at, at, bs.at[t * 8 + k], br.at[t * 8 + k], me.peer(z=-away))

    X_STEPS = [2, 1, -1]

    def x_out(t, k):
        at = x_rows_of(t, me.x)
        return transfer(at, at, bs.at[t * 8 + k], br.at[t * 8 + k], me.peer(x=X_STEPS[k]))

    def x_in(t, k):
        at = x_rows_of(t, me.x - X_STEPS[k])
        return transfer(at, at, bs.at[t * 8 + k], br.at[t * 8 + k], me.peer(x=-X_STEPS[k]))

    def gather_begin(t):
        for core in range(2):

            @pl.when(me.c == core)
            def _():
                for i in ((1, 3, 2), (1, 7, 2, 6, 3, 5, 4))[core]:
                    far = (me.x - i + NX) % NX // 2 if core == 0 else (me.z - i + NZ) % NZ // 2 % 2

                    @pl.when(far == me.ylo)
                    def _():
                        first_in(t, core, i).wait_recv()

                for k in range(4 if core == 0 else 3):
                    (z_out if core == 0 else x_out)(t, k).start()

    def gather_middle(t):
        @pl.when(me.c == 0)
        def _():
            z_in(t, 0).wait_recv()
            z_out(t, 4).start()
            z_out(t, 6).start()
            z_in(t, 1).wait_recv()
            z_out(t, 5).start()
            z_out(t, 7).start()

    def gather_end(t):
        @pl.when(me.c == 0)
        def _():
            for k in range(2, 8):
                z_in(t, k).wait_recv()

        @pl.when(me.c == 1)
        def _():
            for k in range(3):
                x_in(t, k).wait_recv()

        for s in range(4):
            out_copy(t, s).start()

    def out_copy(t, s):
        at = pl.ds(t * PART, PART)
        return pltpu.make_async_copy(
            gather.at[s, at], gh_ref.at[at, pl.ds(s * WIDE, WIDE)], loc.at[2 + t * 4 + s]
        )

    def gather_drain(t):
        @pl.when(keeps)
        def _():
            for core in range(2):

                @pl.when(me.c == core)
                def _():
                    for i in range(1, NX if core == 0 else NZ):
                        first_out(t, core, i).wait_send()

        @pl.when(me.c == 0)
        def _():
            for k in range(8):
                z_out(t, k).wait_send()

        @pl.when(me.c == 1)
        def _():
            for k in range(3):
                x_out(t, k).wait_send()

    def weight_tiles(lo, hi):
        @pl.loop(lo, hi)
        def _(i):
            at = pl.ds(al(i * 128, 128), 128)
            gw_ref[at, :] = lax.dot_general(
                hd[:, at], gr[...], (((0,), (0,)), ((), ())), preferred_element_type=F32
            ).astype(BF16)

    to_mate_part.wait_recv()
    for s in range(4):
        local(s)
    stats_begin(0)
    local(4)
    local(5)
    stats_middle(0)
    local(6)
    stats_end(0)
    local(7)
    stats_begin(1)
    turn_early(0)
    one_send(0, EARLY)
    relay(0)
    stats_middle(1)
    relay(1)
    turn_late(0)
    one_send(0, LATE)
    stats_end(1)
    relay(2)
    turn_early(1)
    one_send(1, EARLY)
    two_send_x(0)
    relay(3)
    turn_late(1)
    one_send(1, LATE)
    two_send_z(0)
    weight_tiles(0, 2)
    y_send(0)
    weight_tiles(2, 3)
    two_send_x(1)
    y_take(0)
    weight_tiles(3, 4)
    two_send_z(1)
    gather_begin(0)
    weight_tiles(4, 6)
    y_send(1)
    gather_middle(0)
    weight_tiles(6, 8)
    y_take(1)
    weight_tiles(8, 10)
    gather_begin(1)
    gather_end(0)
    gather_middle(1)
    to_mate.wait_send()
    to_mate_part.wait_send()
    for copy in (
        exchanged + crossed + list(hidden.values()) + [grads[i] for i in range(6)] + list(stats.values())
        + list(tables.values()) + list(one.values()) + list(two.values())
    ):
        copy.wait_send()
    for t in range(2):
        y_each(t, lambda copy: copy.wait_send())
    gather_end(1)
    for t in range(2):
        gather_drain(t)
    for t in range(2):
        for s in range(4):
            out_copy(t, s).wait()


def fused(hidden, head_weight, prompt_ids, prompt_counts, sampled_ids, token_mask, rewards):
    vmem = pl.BlockSpec(memory_space=pltpu.VMEM)
    smem = pl.BlockSpec(memory_space=pltpu.SMEM)
    hbm = pl.BlockSpec(memory_space=pl.ANY)
    dma = lambda n: pltpu.SemaphoreType.DMA((n,))
    buf = lambda *shape: pltpu.VMEM(shape, BF16)
    wide = lambda *shape: pltpu.VMEM(shape, F32)
    return pl.pallas_call(
        kernel,
        out_shape=(
            jax.ShapeDtypeStruct((16, 16), F32),
            jax.ShapeDtypeStruct((OWN, 4 * WIDE), BF16),
            jax.ShapeDtypeStruct((WIDE, VOCAB), BF16),
        ),
        in_specs=[hbm, hbm, vmem, vmem, vmem, vmem, smem],
        out_specs=(vmem, hbm, vmem),
        scratch_shapes=[
            buf(WIDE, VOCAB), buf(ALL, WIDE), wide(OWN, VOCAB), wide(OWN, VOCAB), wide(OWN, VOCAB),
            wide(STEPS, STEP, VOCAB), wide(STEPS, STEP, VOCAB), wide(STEPS, STEP, VOCAB), wide(STEPS, STEP, VOCAB),
            wide(16, VOCAB), wide(OWN, 128), wide(OWN, 128), wide(OWN, 128), wide(2, 2, 8, PART), wide(28, 8, PART),
            wide(4, 2, 8, PART), wide(PART, 128),
            buf(OWN, VOCAB), buf(ALL, VOCAB), buf(4, OWN, WIDE),
            buf(28, 16, WIDE), buf(12, 32, WIDE), buf(2, 2, 16, WIDE), buf(2, 2, 32, WIDE),
            buf(6, 16, 640), buf(14, 16, 640), buf(2, 2, 16, 640), buf(2, 8, 16, 640), buf(4, OWN, WIDE),
            dma(10), dma(16), dma(16), dma(1), dma(1), dma(1), dma(1), dma(8), dma(8), dma(8), dma(8),
            dma(28), dma(28), dma(10), dma(10), dma(6), dma(6),
            dma(28), dma(28), dma(12), dma(12), dma(6), dma(6), dma(14), dma(14), dma(8), dma(16),
            dma(14), dma(14), dma(16), dma(16),
        ],
        compiler_params=pltpu.CompilerParams(
            collective_id=0, has_side_effects=True, vmem_limit_bytes=56 << 20
        ),
        name="fused",
    )(hidden, head_weight, prompt_ids, prompt_counts, sampled_ids, token_mask, rewards)


def solution(mesh):
    return jax.shard_map(
        fused,
        mesh=mesh,
        in_specs=(
            P("dp", None),
            P("dp", "tensor"),
            P("dp", None),
            P("dp", None),
            P("dp", None),
            P("dp", None),
            P("dp"),
        ),
        out_specs=(P("dp", None), P("dp", None), P("dp", "tensor")),
        check_vma=False,
    )
```

```python
import functools

import jax
import jax.numpy as jnp
from jax import lax
from jax.experimental import pallas as pl
from jax.experimental.pallas import tpu as pltpu
from jax.sharding import PartitionSpec as P

GROUP = 8
NX, NZ, NY = 4, 8, 4
MESH = pl.DeviceIdType.MESH
F32, BF16 = jnp.float32, jnp.bfloat16

recurrence_deduction = 0.4
presence_deduction = 0.6

class Place:
    def __init__(self):
        dp, t = lax.axis_index("dp"), lax.axis_index("tensor")
        self.ylo, self.c = dp // 2, dp % 2
        self.yhi, self.x, self.z = t // 32, (t // 8) % 4, t % 8
        self.dp = dp

    def peer(self, x=0, y=0, z=0, c=0):
        yy = (self.yhi * 2 + self.ylo + y + NY) % NY
        xx, zz, cc = (self.x + x + NX) % NX, (self.z + z + NZ) % NZ, (self.c + c) % 2
        return ((yy % 2) * 2 + cc, (yy // 2) * 32 + xx * 8 + zz)


def arrive(barrier, peers):
    for who in peers:
        pl.semaphore_signal(barrier, inc=1, device_id=who, device_id_type=MESH)


def send(src, dst, ssem, rsem, who):
    copy = pltpu.make_async_remote_copy(
        src_ref=src, dst_ref=dst, send_sem=ssem, recv_sem=rsem, device_id=who, device_id_type=MESH
    )
    copy.start()
    return copy


Z_PEERS = [dict(z=i) for i in range(1, NZ)]
X_PEERS = [dict(x=i) for i in range(1, NX)]
Y_PEERS = [dict(y=i, c=j) for i in range(NY) for j in range(2) if (i, j) != (0, 0)]
XY_PEERS = [dict(x=i, y=j) for i in range(NX) for j in (0, 2) if (i, j) != (0, 0)]
ALL_PEERS = Z_PEERS + X_PEERS + Y_PEERS + [dict(x=i, y=2) for i in range(1, NX)]

WIDE, VOCAB, OWN, ALL = 1280, 1280, 256, 1024
STEP, STEPS = 32, 8
DIRECT = (1, 3)
EARLY, LATE = 0, 1
PART = 128
CHAINS = [(d, half, sub, (d == 1) == (sub == 0)) for half in (EARLY, LATE) for sub in range(2) for d in (1, -1)]


def al(i, n):
    return pl.multiple_of(i, n)


class Ring:
    def __init__(self, n, at, get, out, land, ssem, rsem, ahead, behind):
        self.n, self.at, self.get, self.out, self.land = n, at, get, out, land
        self.ssem, self.rsem, self.toward = ssem, rsem, {1: ahead, -1: behind}
        self.slots, self.copies = {}, {}
        for i in range(len(CHAINS)):
            for h in range(self.hops(i)):
                self.slots[i, h] = len(self.slots)

    def hops(self, i):
        return self.n // 2 - (0 if CHAINS[i][3] else 1)

    def step(self, half, sub, h):
        for i, (d, hf, sb, far) in enumerate(CHAINS):
            if h >= self.hops(i) or (hf, sb) != (half, sub):
                continue
            chunk = (self.at + d * (self.hops(i) - h) + self.n) % self.n
            term = self.get(half, sub, chunk)
            if h:
                self.copies[i, h - 1].wait_recv()
                term = term + self.land[self.slots[i, h - 1]].astype(F32)
            k = self.slots[i, h]
            self.out[k] = term.astype(BF16)
            self.copies[i, h] = send(
                self.out.at[k], self.land.at[k], self.ssem.at[k], self.rsem.at[k], self.toward[d]
            )

    def total(self, half, sub):
        term = self.get(half, sub, self.at)
        for i, (d, hf, sb, far) in enumerate(CHAINS):
            if (hf, sb) == (half, sub):
                self.copies[i, self.hops(i) - 1].wait_recv()
                term = term + self.land[self.slots[i, self.hops(i) - 1]].astype(F32)
        return term

    def finish(self):
        for copy in self.copies.values():
            copy.wait_send()


def merge(m, l, p, others):
    top = m
    for o in others:
        top = jnp.maximum(top, o[0:1])
    l = l * jnp.exp(m - top)
    for o in others:
        l = l + o[1:2] * jnp.exp(o[0:1] - top)
        p = p + o[2:3]
    return top, l, p


def rows_of(i, n):
    return pl.ds(al(i, n), n)


def kernel(
    hid_ref, w_hbm, pid_ref, pc_ref, sid_ref, mask_ref, rew_ref, lp_ref, gh_ref, gw_ref,
    w_ref, wt_ref, hd, lex, pout, pland, xout, xland, lout, lland, prompt, sids, id_ref, tw_ref, st, mine, sland, tab, cols,
    raw, gr, part, plain, gw_tiles, zout, zland, xrout, xrland, z2, x2, z2land, x2land, ysum, yland, gather,
    loc, is_, ir, hs, hr, cs, cr, ps, pr, xs, xr, ls, lr, ss, sr, gs, grs, ts, tr,
    zs, zr, xrs, xrr, z2s, z2r, x2s, x2r, ys, yr, as_, ar, bs, br,
):
    me = Place()
    toward = 1 - 2 * me.ylo
    mate, across, across_mate = me.peer(c=1), me.peer(y=toward), me.peer(y=toward, c=1)
    other = 2 * (1 - me.ylo)
    own, mates = me.dp, 2 * me.ylo + 1 - me.c
    mine_of, mates_of = other + me.c, other + 1 - me.c

    copy_w = pltpu.make_async_copy(w_hbm, w_ref, loc.at[0])
    copy_h = pltpu.make_async_copy(
        hid_ref.at[:, pl.ds(al(own * WIDE, 128), WIDE)], hd.at[rows_of(own * OWN, OWN)], loc.at[1]
    )
    copy_w.start()
    copy_h.start()
    peers = [me.peer(**s) for s in ALL_PEERS]
    barrier = pltpu.get_barrier_semaphore()
    arrive(barrier, peers)

    offset = (me.yhi * 32 + me.x * 8 + me.z) * VOCAB
    column = lax.broadcasted_iota(jnp.int32, (16, VOCAB), 1) + offset
    tile = jnp.zeros((16, VOCAB), F32)
    pid, pc = pid_ref[...], pc_ref[...].astype(F32)
    for j in range(pid.shape[1]):
        tile = tile + jnp.where(pid[:, j : j + 1] == column, pc[:, j : j + 1], 0.0)
    prompt[...] = tile
    its_lane = lax.broadcasted_iota(jnp.int32, (OWN, 16), 1) == lax.broadcasted_iota(jnp.int32, (OWN, 16), 0) % 16

    def as_column(rows):
        wide_rows = jnp.concatenate([jnp.broadcast_to(rows[r : r + 1, :], (16, 16)) for r in range(16)], axis=0)
        return jnp.broadcast_to(jnp.sum(jnp.where(its_lane, wide_rows, 0.0), axis=1, keepdims=True), (OWN, 128))

    which = lax.broadcasted_iota(jnp.int32, (16, 16), 0)
    advantage = jnp.zeros((16, 16), F32)
    for g in range(16 // GROUP):
        rewards = [rew_ref[g * GROUP + r] for r in range(GROUP)]
        mean = sum(rewards[1:], rewards[0]) * (1.0 / GROUP)
        for r in range(GROUP):
            advantage = jnp.where(which == g * GROUP + r, rewards[r] - mean, advantage)
    weight = -(advantage * mask_ref[...].astype(F32)) * 1.25
    sids[own] = sid_ref[...]
    id_ref[rows_of(own * OWN, OWN)] = as_column(sid_ref[...].astype(F32))
    tw_ref[...] = as_column(weight)
    pl.semaphore_wait(barrier, len(peers))

    def hidden_copy(rel, step, way):
        who = me.peer(y=way, c=rel)
        to = other + (me.c + rel) % 2
        k = rel * STEPS + step
        return pltpu.make_async_remote_copy(
            src_ref=hid_ref.at[rows_of(step * STEP, STEP), pl.ds(al(to * WIDE, 128), WIDE)],
            dst_ref=hd.at[rows_of(own * OWN + step * STEP, STEP)],
            send_sem=hs.at[k],
            recv_sem=hr.at[k],
            device_id=who,
            device_id_type=MESH,
        )

    wrapped = [s for s in range(STEPS) if s not in DIRECT]
    hidden = {}
    for s in range(STEPS):
        for rel in range(2):
            hidden[rel, s] = hidden_copy(rel, s, toward if s in DIRECT else -toward)
    ahead = 2
    for s in (wrapped[0],) + DIRECT[:1]:
        for rel in range(2):
            hidden[rel, s].start()
    to_mate = send(
        hid_ref.at[:, pl.ds(al(mates * WIDE, 128), WIDE)], hd.at[rows_of(own * OWN, OWN)],
        cs.at[0], cr.at[0], mate,
    )
    for s in tuple(wrapped[1:ahead]) + DIRECT[1:]:
        for rel in range(2):
            hidden[rel, s].start()

    id_copies = [
        send(sids.at[own], sids.at[own], is_.at[i], ir.at[i], who) for i, who in enumerate((mate, across, across_mate))
    ]
    copy_w.wait()

    @pl.loop(0, 10)
    def _(i):
        at = pl.ds(al(i * 128, 128), 128)
        wt_ref[:, at] = w_ref[at, :].T

    copy_h.wait()
    to_mate.wait_recv()

    @pl.loop(0, 4)
    def _(i):
        at = rows_of(mates * OWN + i * 64, 64)
        pout[rows_of(i * 64, 64)] = jnp.dot(hd[at, :], w_ref[...], preferred_element_type=F32)

    to_mate_part = send(pout, pland, ps.at[0], pr.at[0], mate)
    exchanged, crossed = [], []
    vocab = (lax.broadcasted_iota(jnp.int32, (STEP, VOCAB), 1) + offset).astype(F32)
    vocab_wide = (lax.broadcasted_iota(jnp.int32, (64, VOCAB), 1) + offset).astype(F32)

    def sampled_rows(j):
        @pl.loop(0, 4)
        def _(i):
            chosen = jnp.where(vocab_wide == id_ref[rows_of(j * OWN + i * 64, 64), 0:1], 1.0, 0.0)
            part[j, rows_of(i * 64, 64)] = jnp.dot(chosen.astype(BF16), wt_ref[...], preferred_element_type=F32)

    for s in range(STEPS):
        for rel in range(2):
            hidden[rel, s].wait_recv()
        both = jnp.concatenate(
            [hd[rows_of(mates_of * OWN + s * STEP, STEP), :], hd[rows_of(mine_of * OWN + s * STEP, STEP), :]], axis=0
        )
        term = jnp.dot(both, w_ref[...], preferred_element_type=F32)
        xout[s] = term[:STEP]
        exchanged.append(send(xout.at[s], xland.at[s], xs.at[s], xr.at[s], mate))
        if s in wrapped:
            i = wrapped.index(s) + ahead
            if i < len(wrapped):
                for rel in range(2):
                    hidden[rel, wrapped[i]].start()
        exchanged[s].wait_recv()
        lout[s] = term[STEP:] + xland[s]
        crossed.append(send(lout.at[s], lland.at[s], ls.at[s], lr.at[s], across))
        if s == 1:

            @pl.loop(0, 4)
            def _(i):
                lex[rows_of(i * 64, 64)] = jnp.dot(
                    hd[rows_of(own * OWN + i * 64, 64), :], w_ref[...], preferred_element_type=F32
                )

        if s == 2:
            for copy in id_copies:
                copy.wait_recv()
            for i in range(1, 4):
                j = (own + i) % 4
                id_ref[rows_of(j * OWN, OWN)] = as_column(sids[j].astype(F32))
        if 3 <= s < 7:
            sampled_rows(s - 3)

    grads = {}

    def grad_send(k, src, j, lo, n, who):
        grads[k] = send(src, gr.at[rows_of(j * OWN + lo, n)], gs.at[k], grs.at[k], who)

    to_mate_part.wait_recv()
    lane = lax.broadcasted_iota(jnp.int32, (STEP, 128), 1)
    k_of = lax.broadcasted_iota(jnp.int32, (STEP, STEP), 0)
    q_of = lax.broadcasted_iota(jnp.int32, (STEP, STEP), 1)
    earlier = jnp.where((q_of < k_of) & (q_of // 16 == k_of // 16), 1.0, 0.0).astype(BF16)
    for s in range(STEPS):
        crossed[s].wait_recv()
        at = pl.ds(s * STEP, STEP)
        ids = id_ref[rows_of(own * OWN + s * STEP, STEP), 0:1]
        chosen = vocab == ids
        tally = jnp.dot(earlier, jnp.where(chosen, 1.0, 0.0).astype(BF16), preferred_element_type=F32)
        tally = tally + jnp.concatenate(
            [jnp.broadcast_to(prompt[2 * s + i : 2 * s + i + 1, :], (16, VOCAB)) for i in range(2)], axis=0
        )
        penalty = recurrence_deduction * tally + jnp.where(tally > 0.0, presence_deduction, 0.0)
        scaled = (lex[at, :] + pland[at, :] + lland[s] - penalty) * 1.25
        m = jnp.max(scaled, axis=1, keepdims=True)
        raised = jnp.exp(scaled - m)
        l = jnp.sum(raised, axis=1, keepdims=True)
        p = jnp.sum(jnp.where(chosen, scaled, 0.0), axis=1, keepdims=True)
        raw[at, :] = jnp.where(chosen, 0.0, raised).astype(BF16)
        table = jnp.zeros((STEP, 128), F32)
        for i, v in enumerate((m, l, p, tw_ref[at, 0:1])):
            table = jnp.where(lane == i, v, table)
        st[at, :] = table
        if s % 2:
            lo, n = (s - 1) * STEP, 2 * STEP
            grad_send(s // 2, raw.at[pl.ds(lo, n)], own, lo, n, across)
        if s % 4 == 3:
            lo, n = (s - 3) * STEP, 4 * STEP
            grad_send(4 + s // 4, raw.at[pl.ds(lo, n)], own, lo, n, mate)
    first = st[...].T[0:8]
    m, l, p, weight = [first[i : i + 1] for i in range(4)]
    own_m, across_rows = m, first
    stats = []

    def product(j, lo, n, src, base):
        plain[rows_of(j * OWN + lo, n)] = jnp.dot(
            src[rows_of(base + lo, n), :], wt_ref[...], preferred_element_type=F32
        )

    def relay(i):
        grads[i].wait_recv()
        grad_send(6 + i, gr.at[rows_of(mine_of * OWN + i * 64, 64)], mine_of, i * 64, 64, mate)

    for stage, where in enumerate((Z_PEERS, XY_PEERS)):
        mine[stage] = across_rows
        copies = []
        for i, s in enumerate(where):
            k = stage * 7 + i
            copies.append(send(mine.at[stage], sland.at[k], ss.at[k], sr.at[k], me.peer(**s)))
        if stage == 0:
            product(own, 0, OWN, raw, 0)
        else:
            grads[4].wait_recv()
            grads[5].wait_recv()
            product(mates, 0, OWN, gr, mates * OWN)
            relay(0)
            relay(1)
            product(mine_of, 0, PART, gr, mine_of * OWN)
        for copy in copies:
            copy.wait_recv()
        stats += copies
        m, l, p = merge(m, l, p, [sland[stage * 7 + i] for i in range(7)])
        across_rows = jnp.concatenate([m, l, p, jnp.zeros((5, OWN), F32)], axis=0)
    norm = m + jnp.log(l)
    logp = p - norm
    lp_ref[...] = jnp.concatenate([logp[:, 16 * r : 16 * r + 16] for r in range(16)], axis=0)

    tab[own] = jnp.concatenate(
        [weight * jnp.exp(own_m - norm), weight * (1.0 - jnp.exp(logp)), jnp.zeros((6, OWN), F32)], axis=0
    )
    tables = [send(tab.at[own], tab.at[own], ts.at[i], tr.at[i], who) for i, who in enumerate((mate, across, across_mate))]

    def scale(j, t):
        table, at_j = tab[j][:, t * PART : (t + 1) * PART], rows_of(j * OWN + t * PART, PART)
        cols[at_j] = jnp.concatenate([table, jnp.zeros((120, PART), F32)], axis=0).T

        @pl.loop(0, PART // STEP)
        def _(i):
            lo = t * PART + i * STEP
            at, to = rows_of(lo, STEP), rows_of(j * OWN + lo, STEP)
            part[j, at] = cols[to, 1:2] * part[j, at] - cols[to, 0:1] * plain[to, :]

    def turn(lo, hi):
        @pl.loop(lo, hi)
        def _(i):
            at = rows_of(i * STEP, STEP)
            g = jnp.where(vocab == id_ref[at, 0:1], cols[at, 1:2], -cols[at, 0:1] * gr[at, :].astype(F32))
            gr[at] = g.astype(BF16)

    def z_get(half, sub, chunk):
        ylo = me.ylo if half == EARLY else 1 - me.ylo
        return part[2 * ylo, rows_of(sub * PART + chunk * 16, 16), :]

    def x_get(half, sub, chunk):
        ylo = me.ylo if half == EARLY else 1 - me.ylo
        return part[2 * ylo + 1, rows_of(sub * PART + chunk * 32, 32), :]

    zring = Ring(NZ, me.z, z_get, zout, zland, zs, zr, me.peer(z=1), me.peer(z=-1))
    xring = Ring(NX, me.x, x_get, xrout, xrland, xrs, xrr, me.peer(x=1), me.peer(x=-1))
    def begin(half, t):
        zring.step(half, t, 0)
        xring.step(half, t, 0)

    def late(t):
        if t == 0:
            tables[1].wait_recv()
            tables[2].wait_recv()
        for i in (2 * t, 2 * t + 1):
            grads[6 + i].wait_recv()
        product(mates_of, t * PART, PART, gr, mates_of * OWN)

        @pl.loop(0, 2)
        def _(i):
            scale(other + i, t)

        begin(LATE, t)

    scale(own, 0)
    scale(own, 1)
    tables[0].wait_recv()
    scale(mates, 0)
    scale(mates, 1)
    begin(EARLY, 0)
    begin(EARLY, 1)
    late(0)
    relay(2)
    relay(3)
    product(mine_of, PART, PART, gr, mine_of * OWN)
    zring.step(EARLY, 0, 1)
    xring.step(EARLY, 0, 1)
    late(1)
    zring.step(EARLY, 1, 1)
    xring.step(EARLY, 1, 1)
    zring.step(LATE, 0, 1)
    xring.step(LATE, 0, 1)
    zring.step(EARLY, 0, 2)
    zring.step(EARLY, 1, 2)
    zring.step(LATE, 1, 1)
    xring.step(LATE, 1, 1)
    zring.step(LATE, 0, 2)
    zring.step(EARLY, 0, 3)
    zring.step(EARLY, 1, 3)
    for i in range(6, 10):
        grads[i].wait_send()
    own_at = rows_of(own * OWN, OWN)
    gr[own_at] = raw[...]

    def weight_tiles(lo, hi):
        @pl.loop(lo, hi)
        def _(i):
            at = pl.ds(al(i * 128, 128), 128)
            gw_tiles[at, :] = lax.dot_general(
                hd[:, at], gr[...], (((0,), (0,)), ((), ())), preferred_element_type=F32
            ).astype(BF16)

    def cut(ref, at):
        rows = rows_of((at // 2) * 16, 16)
        return ref.at[:, rows, pl.ds(al((at % 2) * 640, 128), 640)]

    later = []
    zring.step(LATE, 1, 2)
    for half, ylo in ((EARLY, me.ylo), (LATE, 1 - me.ylo)):
        for sub in range(2):
            x2[ylo, pl.ds(sub * 32, 32)] = xring.total(half, sub).astype(BF16)
    x_copies = []
    for i in range(1, NZ):
        x_copies.append(
            send(cut(x2, (me.z + i) % NZ), x2land.at[i - 1], x2s.at[i - 1], x2r.at[i - 1], me.peer(z=i))
        )
    zring.step(LATE, 0, 3)
    turn(0, 16)
    zring.step(LATE, 1, 3)
    turn(16, 32)
    weight_tiles(0, 2)
    for half, ylo in ((EARLY, me.ylo), (LATE, 1 - me.ylo)):
        for sub in range(2):
            z2[ylo, pl.ds(sub * 16, 16)] = zring.total(half, sub).astype(BF16)
    z_copies = []
    for i in range(1, NX):
        z_copies.append(
            send(cut(z2, (me.x + i) % NX), z2land.at[i - 1], z2s.at[i - 1], z2r.at[i - 1], me.peer(x=i))
        )
    weight_tiles(2, 6)
    for core, (ours, land, copies) in enumerate(
        ((cut(z2, me.x), z2land, z_copies), (cut(x2, me.z), x2land, x_copies))
    ):
        for copy in copies:
            copy.wait_recv()
        term = ours[...].astype(F32)
        for i in range(len(copies)):
            term = term + land[i].astype(F32)
        ysum[core] = term.astype(BF16)
        later += copies

    def kept_rows(core, x, z):
        return 16 * z + PART * (x // 2) if core == 0 else 32 * x + PART * (z // 4) + 16 * ((z // 2) % 2)

    def kept_cols(core, x, z):
        return (x % 2 if core == 0 else z % 2) * 640

    y_copies = {}
    for i, s in enumerate(Y_PEERS):
        piece = ysum.at[(me.c + s["c"]) % 2, (me.ylo + s["y"]) % 2]
        y_copies[s["y"], s["c"]] = send(piece, yland.at[i], ys.at[i], yr.at[i], me.peer(**s))
    weight_tiles(6, 10)
    gw_out = pltpu.make_async_copy(gw_tiles, gw_ref, loc.at[6])
    gw_out.start()
    row, col = kept_rows(0, me.x, me.z), kept_cols(0, me.x, me.z)
    row = jnp.where(me.c == 0, row, kept_rows(1, me.x, me.z))
    col = jnp.where(me.c == 0, col, kept_cols(1, me.x, me.z))
    for dc in range(2):
        for dy in range(2):
            pair = []
            for y in (dy, dy + 2):
                if (y, dc) == (0, 0):
                    pair.append(ysum[me.c, me.ylo].astype(F32))
                else:
                    mirror = ((NY - y) % NY, dc)
                    y_copies[mirror].wait_recv()
                    pair.append(yland[Y_PEERS.index(dict(y=mirror[0], c=mirror[1]))].astype(F32))
            owner = ((me.ylo + dy) % 2) * 2 + (me.c + dc) % 2
            gather[owner, rows_of(row, 16), pl.ds(al(col, 128), 640)] = (pair[0] + pair[1]).astype(BF16)
    later += list(y_copies.values())

    def piece(core, x, z):
        rows, at = rows_of(kept_rows(core, x, z), 16), pl.ds(al(kept_cols(core, x, z), 128), 640)
        return gather.at[:, rows, at]

    def z_off(i):
        return (me.z + i + NZ) % NZ

    def x_off(i):
        return (me.x + i + NX) % NX

    def put(copies, key, src, who):
        k = len(copies)
        copies[key] = send(src, src, bs.at[k], br.at[k], who)

    @pl.when(me.c == 0)
    def _():
        mine = piece(0, me.x, me.z)
        firsts = {i: send(mine, mine, as_.at[i - 1], ar.at[i - 1], me.peer(x=i)) for i in (2, 1, 3)}
        copies, order = {}, (0, 1, 3, 2)
        for q in order:
            if q:
                firsts[q].wait_recv()
            for away in (2, -2, 1, -1):
                put(copies, (q, away), piece(0, x_off(-q), me.z), me.peer(z=away))
        for q in order:
            for d in (1, -1):
                copies[q, 2 * d].wait_recv()
                came = piece(0, x_off(-q), z_off(-2 * d))
                if (q in (0, 3)) == (d == 1):
                    put(copies, (q, 4), came, me.peer(z=2 * d))
                put(copies, (q, 3 * d), came, me.peer(z=d))
        for q in order:
            for key in (1, -1, 3, -3, 4):
                copies[q, key].wait_recv()
        for copy in list(firsts.values()) + list(copies.values()):
            copy.wait_send()

    @pl.when(me.c == 1)
    def _():
        copies, xcopies = {}, {}
        mine = piece(1, me.x, me.z)

        def along_x(dz):
            at = piece(1, me.x, z_off(dz))
            for d in (1, -1):
                put(xcopies, (dz, d), at, me.peer(x=d))

        firsts = {}
        for i, away in enumerate((2, -2, 1, -1)):
            firsts[away] = send(mine, mine, as_.at[i], ar.at[i], me.peer(z=away))
        along_x(0)
        for d in (1, -1):
            firsts[2 * d].wait_recv()
            came = piece(1, me.x, z_off(-2 * d))
            half = came.at[pl.ds(0 if d == 1 else 2, 2)]
            k = 4 if d == 1 else 6
            firsts[4 * d] = send(half, half, as_.at[k], ar.at[k], me.peer(z=2 * d))
            firsts[3 * d] = send(came, came, as_.at[k + 1], ar.at[k + 1], me.peer(z=d))
        for d in (1, -1):
            firsts[d].wait_recv()
            along_x(-d)
        for d in (1, -1):
            along_x(-2 * d)
        for d in (1, -1):
            firsts[3 * d].wait_recv()
            along_x(-3 * d)
        for d in (1, -1):
            firsts[4 * d].wait_recv()
        along_x(-4)
        for dz in (0, -1, 1, -2, 2, -3, 3, -4):
            d = 1 if dz % 2 == 0 else -1
            xcopies[dz, d].wait_recv()
            put(xcopies, (dz, 2), piece(1, x_off(-d), z_off(dz)), me.peer(x=d))
        for dz in (0, -1, 1, -2, 2, -3, 3, -4):
            d = 1 if dz % 2 == 0 else -1
            xcopies[dz, -d].wait_recv()
            xcopies[dz, 2].wait_recv()
        for copy in list(firsts.values()) + list(xcopies.values()):
            copy.wait_send()

    outs = []
    for s in range(4):
        copy = pltpu.make_async_copy(gather.at[s], gh_ref.at[:, pl.ds(s * WIDE, WIDE)], loc.at[2 + s])
        copy.start()
        outs.append(copy)
    zring.finish()
    xring.finish()
    to_mate.wait_send()
    to_mate_part.wait_send()
    for copy in later + id_copies + exchanged + crossed + stats + tables + list(hidden.values()) + [grads[i] for i in range(6)]:
        copy.wait_send()
    for copy in outs + [gw_out]:
        copy.wait()


def fused(hidden, head_weight, prompt_ids, prompt_counts, sampled_ids, token_mask, rewards):
    vmem = pl.BlockSpec(memory_space=pltpu.VMEM)
    smem = pl.BlockSpec(memory_space=pltpu.SMEM)
    hbm = pl.BlockSpec(memory_space=pl.ANY)
    dma = lambda n: pltpu.SemaphoreType.DMA((n,))
    buf = lambda *shape: pltpu.VMEM(shape, BF16)
    wide = lambda *shape: pltpu.VMEM(shape, F32)
    return pl.pallas_call(
        kernel,
        out_shape=(
            jax.ShapeDtypeStruct((16, 16), F32),
            jax.ShapeDtypeStruct((OWN, 4 * WIDE), BF16),
            jax.ShapeDtypeStruct((WIDE, VOCAB), BF16),
        ),
        in_specs=[hbm, hbm, vmem, vmem, vmem, vmem, smem],
        out_specs=(vmem, hbm, hbm),
        scratch_shapes=[
            buf(WIDE, VOCAB), buf(VOCAB, WIDE), buf(ALL, WIDE), wide(OWN, VOCAB), wide(OWN, VOCAB), wide(OWN, VOCAB),
            wide(STEPS, STEP, VOCAB), wide(STEPS, STEP, VOCAB), wide(STEPS, STEP, VOCAB), wide(STEPS, STEP, VOCAB),
            wide(16, VOCAB), pltpu.VMEM((4, 16, 16), jnp.int32), wide(ALL, 128), wide(OWN, 128), wide(OWN, 128), wide(2, 8, OWN), wide(14, 8, OWN),
            wide(4, 8, OWN), wide(ALL, 128),
            buf(OWN, VOCAB), buf(ALL, VOCAB), wide(4, OWN, WIDE), wide(ALL, WIDE), buf(WIDE, VOCAB),
            buf(28, 16, 1280), buf(28, 16, 1280), buf(12, 32, 1280), buf(12, 32, 1280),
            buf(2, 32, 1280), buf(2, 64, 1280), buf(3, 2, 16, 640), buf(7, 2, 16, 640), buf(2, 2, 16, 640),
            buf(7, 16, 640), buf(4, OWN, WIDE),
            dma(7), dma(3), dma(3), dma(16), dma(16), dma(1), dma(1), dma(1), dma(1), dma(8), dma(8), dma(8), dma(8),
            dma(14), dma(14), dma(10), dma(10), dma(3), dma(3),
            dma(28), dma(28), dma(12), dma(12), dma(3), dma(3), dma(7), dma(7), dma(7), dma(7),
            dma(8), dma(8), dma(28), dma(28),
        ],
        compiler_params=pltpu.CompilerParams(
            collective_id=0, has_side_effects=True, vmem_limit_bytes=56 << 20
        ),
        name="fused",
    )(hidden, head_weight, prompt_ids, prompt_counts, sampled_ids, token_mask, rewards)


def solution(mesh):
    return jax.shard_map(
        fused,
        mesh=mesh,
        in_specs=(
            P("dp", None),
            P("dp", "tensor"),
            P("dp", None),
            P("dp", None),
            P("dp", None),
            P("dp", None),
            P("dp"),
        ),
        out_specs=(P("dp", None), P("dp", None), P("dp", "tensor")),
        check_vma=False,
    )
```

```python
import functools

import jax
import jax.numpy as jnp
from jax import lax
from jax.experimental import pallas as pl
from jax.experimental.pallas import tpu as pltpu
from jax.sharding import PartitionSpec as P

GROUP = 8
NX, NZ, NY = 4, 8, 4
MESH = pl.DeviceIdType.MESH
F32, BF16 = jnp.float32, jnp.bfloat16

recurrence_deduction = 0.4
presence_deduction = 0.6

class Place:
    def __init__(self):
        dp, t = lax.axis_index("dp"), lax.axis_index("tensor")
        self.ylo, self.c = dp // 2, dp % 2
        self.yhi, self.x, self.z = t // 32, (t // 8) % 4, t % 8
        self.dp = dp

    def peer(self, x=0, y=0, z=0, c=0):
        yy = (self.yhi * 2 + self.ylo + y + NY) % NY
        xx, zz, cc = (self.x + x + NX) % NX, (self.z + z + NZ) % NZ, (self.c + c) % 2
        return ((yy % 2) * 2 + cc, (yy // 2) * 32 + xx * 8 + zz)


def arrive(barrier, peers):
    for who in peers:
        pl.semaphore_signal(barrier, inc=1, device_id=who, device_id_type=MESH)


def send(src, dst, ssem, rsem, who):
    copy = pltpu.make_async_remote_copy(
        src_ref=src, dst_ref=dst, send_sem=ssem, recv_sem=rsem, device_id=who, device_id_type=MESH
    )
    copy.start()
    return copy


Z_PEERS = [dict(z=i) for i in range(1, NZ)]
X_PEERS = [dict(x=i) for i in range(1, NX)]
Y_PEERS = [dict(y=i, c=j) for i in range(NY) for j in range(2) if (i, j) != (0, 0)]
XY_PEERS = [dict(x=i, y=j) for i in range(NX) for j in (0, 2) if (i, j) != (0, 0)]
ALL_PEERS = Z_PEERS + X_PEERS + Y_PEERS + [dict(x=i, y=2) for i in range(1, NX)]

WIDE, VOCAB, OWN, ALL = 1280, 1280, 256, 1024
STEP, STEPS = 32, 8
DIRECT = (1, 3)
EARLY, LATE = 0, 1
PART = 128
CHAINS = [(d, half, sub, (d == 1) == (sub == 0)) for half in (EARLY, LATE) for sub in range(2) for d in (1, -1)]


def al(i, n):
    return pl.multiple_of(i, n)


class Ring:
    def __init__(self, n, at, get, out, land, ssem, rsem, ahead, behind):
        self.n, self.at, self.get, self.out, self.land = n, at, get, out, land
        self.ssem, self.rsem, self.toward = ssem, rsem, {1: ahead, -1: behind}
        self.slots, self.copies = {}, {}
        for i in range(len(CHAINS)):
            for h in range(self.hops(i)):
                self.slots[i, h] = len(self.slots)

    def hops(self, i):
        return self.n // 2 - (0 if CHAINS[i][3] else 1)

    def step(self, half, sub, h):
        for i, (d, hf, sb, far) in enumerate(CHAINS):
            if h >= self.hops(i) or (hf, sb) != (half, sub):
                continue
            chunk = (self.at + d * (self.hops(i) - h) + self.n) % self.n
            term = self.get(half, sub, chunk)
            if h:
                self.copies[i, h - 1].wait_recv()
                term = term + self.land[self.slots[i, h - 1]].astype(F32)
            k = self.slots[i, h]
            self.out[k] = term.astype(BF16)
            self.copies[i, h] = send(
                self.out.at[k], self.land.at[k], self.ssem.at[k], self.rsem.at[k], self.toward[d]
            )

    def total(self, half, sub):
        term = self.get(half, sub, self.at)
        for i, (d, hf, sb, far) in enumerate(CHAINS):
            if (hf, sb) == (half, sub):
                self.copies[i, self.hops(i) - 1].wait_recv()
                term = term + self.land[self.slots[i, self.hops(i) - 1]].astype(F32)
        return term

    def finish(self):
        for copy in self.copies.values():
            copy.wait_send()


def merge(m, l, p, others):
    top = m
    for o in others:
        top = jnp.maximum(top, o[0:1])
    l = l * jnp.exp(m - top)
    for o in others:
        l = l + o[1:2] * jnp.exp(o[0:1] - top)
        p = p + o[2:3]
    return top, l, p


def rows_of(i, n):
    return pl.ds(al(i, n), n)


def kernel(
    hid_ref, w_hbm, pid_ref, pc_ref, sid_ref, mask_ref, rew_ref, lp_ref, gh_ref, gw_ref,
    w_ref, wt_ref, hd, lex, pout, pland, xout, xland, lout, lland, prompt, sids, id_ref, tw_ref, st, mine, sland, tab, cols,
    raw, gr, part, plain, gw_tiles, zout, zland, xrout, xrland, z2, x2, z2land, x2land, ysum, yland, gather,
    loc, is_, ir, hs, hr, cs, cr, ps, pr, xs, xr, ls, lr, ss, sr, gs, grs, ts, tr,
    zs, zr, xrs, xrr, z2s, z2r, x2s, x2r, ys, yr, as_, ar, bs, br,
):
    me = Place()
    toward = 1 - 2 * me.ylo
    mate, across, across_mate = me.peer(c=1), me.peer(y=toward), me.peer(y=toward, c=1)
    other = 2 * (1 - me.ylo)
    own, mates = me.dp, 2 * me.ylo + 1 - me.c
    mine_of, mates_of = other + me.c, other + 1 - me.c

    copy_w = pltpu.make_async_copy(w_hbm, w_ref, loc.at[0])
    copy_h = pltpu.make_async_copy(
        hid_ref.at[:, pl.ds(al(own * WIDE, 128), WIDE)], hd.at[rows_of(own * OWN, OWN)], loc.at[1]
    )
    copy_w.start()
    copy_h.start()
    peers = [me.peer(**s) for s in ALL_PEERS]
    barrier = pltpu.get_barrier_semaphore()
    arrive(barrier, peers)

    offset = (me.yhi * 32 + me.x * 8 + me.z) * VOCAB
    column = lax.broadcasted_iota(jnp.int32, (16, VOCAB), 1) + offset
    tile = jnp.zeros((16, VOCAB), F32)
    pid, pc = pid_ref[...], pc_ref[...].astype(F32)
    for j in range(pid.shape[1]):
        tile = tile + jnp.where(pid[:, j : j + 1] == column, pc[:, j : j + 1], 0.0)
    prompt[...] = tile
    its_lane = lax.broadcasted_iota(jnp.int32, (OWN, 16), 1) == lax.broadcasted_iota(jnp.int32, (OWN, 16), 0) % 16

    def as_column(rows):
        wide_rows = jnp.concatenate([jnp.broadcast_to(rows[r : r + 1, :], (16, 16)) for r in range(16)], axis=0)
        return jnp.broadcast_to(jnp.sum(jnp.where(its_lane, wide_rows, 0.0), axis=1, keepdims=True), (OWN, 128))

    which = lax.broadcasted_iota(jnp.int32, (16, 16), 0)
    advantage = jnp.zeros((16, 16), F32)
    for g in range(16 // GROUP):
        rewards = [rew_ref[g * GROUP + r] for r in range(GROUP)]
        mean = sum(rewards[1:], rewards[0]) * (1.0 / GROUP)
        for r in range(GROUP):
            advantage = jnp.where(which == g * GROUP + r, rewards[r] - mean, advantage)
    weight = -(advantage * mask_ref[...].astype(F32)) * 1.25
    sids[own] = sid_ref[...]
    id_ref[rows_of(own * OWN, OWN)] = as_column(sid_ref[...].astype(F32))
    tw_ref[...] = as_column(weight)
    pl.semaphore_wait(barrier, len(peers))

    def hidden_copy(rel, step, way):
        who = me.peer(y=way, c=rel)
        to = other + (me.c + rel) % 2
        k = rel * STEPS + step
        return pltpu.make_async_remote_copy(
            src_ref=hid_ref.at[rows_of(step * STEP, STEP), pl.ds(al(to * WIDE, 128), WIDE)],
            dst_ref=hd.at[rows_of(own * OWN + step * STEP, STEP)],
            send_sem=hs.at[k],
            recv_sem=hr.at[k],
            device_id=who,
            device_id_type=MESH,
        )

    wrapped = [s for s in range(STEPS) if s not in DIRECT]
    hidden = {}
    for s in range(STEPS):
        for rel in range(2):
            hidden[rel, s] = hidden_copy(rel, s, toward if s in DIRECT else -toward)
    ahead = 2
    for s in (wrapped[0],) + DIRECT[:1]:
        for rel in range(2):
            hidden[rel, s].start()
    to_mate = send(
        hid_ref.at[:, pl.ds(al(mates * WIDE, 128), WIDE)], hd.at[rows_of(own * OWN, OWN)],
        cs.at[0], cr.at[0], mate,
    )
    for s in tuple(wrapped[1:ahead]) + DIRECT[1:]:
        for rel in range(2):
            hidden[rel, s].start()

    id_copies = [
        send(sids.at[own], sids.at[own], is_.at[i], ir.at[i], who) for i, who in enumerate((mate, across, across_mate))
    ]
    copy_w.wait()

    @pl.loop(0, 10)
    def _(i):
        at = pl.ds(al(i * 128, 128), 128)
        wt_ref[:, at] = w_ref[at, :].T

    copy_h.wait()
    to_mate.wait_recv()

    pout[...] = jnp.dot(hd[rows_of(mates * OWN, OWN), :], w_ref[...], preferred_element_type=F32)
    to_mate_part = send(pout, pland, ps.at[0], pr.at[0], mate)
    exchanged, crossed = [], []
    vocab = (lax.broadcasted_iota(jnp.int32, (STEP, VOCAB), 1) + offset).astype(F32)
    vocab_wide = (lax.broadcasted_iota(jnp.int32, (OWN, VOCAB), 1) + offset).astype(F32)

    def sampled_rows(j):
        chosen = jnp.where(vocab_wide == id_ref[rows_of(j * OWN, OWN), 0:1], 1.0, 0.0).astype(BF16)
        part[j] = jnp.dot(chosen, wt_ref[...], preferred_element_type=F32)

    for s in range(STEPS):
        for rel in range(2):
            hidden[rel, s].wait_recv()
        both = jnp.concatenate(
            [hd[rows_of(mates_of * OWN + s * STEP, STEP), :], hd[rows_of(mine_of * OWN + s * STEP, STEP), :]], axis=0
        )
        term = jnp.dot(both, w_ref[...], preferred_element_type=F32)
        xout[s] = term[:STEP]
        exchanged.append(send(xout.at[s], xland.at[s], xs.at[s], xr.at[s], mate))
        if s in wrapped:
            i = wrapped.index(s) + ahead
            if i < len(wrapped):
                for rel in range(2):
                    hidden[rel, wrapped[i]].start()
        if s == 1:
            lex[...] = jnp.dot(hd[rows_of(own * OWN, OWN), :], w_ref[...], preferred_element_type=F32)
        if s == 2:
            for copy in id_copies:
                copy.wait_recv()
            for i in range(1, 4):
                j = (own + i) % 4
                id_ref[rows_of(j * OWN, OWN)] = as_column(sids[j].astype(F32))
        if 3 <= s < 7:
            sampled_rows(s - 3)
        exchanged[s].wait_recv()
        lout[s] = term[STEP:] + xland[s]
        crossed.append(send(lout.at[s], lland.at[s], ls.at[s], lr.at[s], across))

    grads = {}

    def grad_send(k, src, j, lo, n, who):
        grads[k] = send(src, gr.at[rows_of(j * OWN + lo, n)], gs.at[k], grs.at[k], who)

    to_mate_part.wait_recv()
    lane = lax.broadcasted_iota(jnp.int32, (STEP, 128), 1)
    k_of = lax.broadcasted_iota(jnp.int32, (STEP, STEP), 0)
    q_of = lax.broadcasted_iota(jnp.int32, (STEP, STEP), 1)
    earlier = jnp.where((q_of < k_of) & (q_of // 16 == k_of // 16), 1.0, 0.0).astype(BF16)
    for s in range(STEPS):
        crossed[s].wait_recv()
        at = pl.ds(s * STEP, STEP)
        ids = id_ref[rows_of(own * OWN + s * STEP, STEP), 0:1]
        chosen = vocab == ids
        tally = jnp.dot(earlier, jnp.where(chosen, 1.0, 0.0).astype(BF16), preferred_element_type=F32)
        tally = tally + jnp.concatenate(
            [jnp.broadcast_to(prompt[2 * s + i : 2 * s + i + 1, :], (16, VOCAB)) for i in range(2)], axis=0
        )
        penalty = recurrence_deduction * tally + jnp.where(tally > 0.0, presence_deduction, 0.0)
        scaled = (lex[at, :] + pland[at, :] + lland[s] - penalty) * 1.25
        m = jnp.max(scaled, axis=1, keepdims=True)
        raised = jnp.exp(scaled - m)
        l = jnp.sum(raised, axis=1, keepdims=True)
        p = jnp.sum(jnp.where(chosen, scaled, 0.0), axis=1, keepdims=True)
        raw[at, :] = jnp.where(chosen, 0.0, raised).astype(BF16)
        table = jnp.zeros((STEP, 128), F32)
        for i, v in enumerate((m, l, p, tw_ref[at, 0:1])):
            table = jnp.where(lane == i, v, table)
        st[at, :] = table
        if s % 2:
            lo, n = (s - 1) * STEP, 2 * STEP
            grad_send(s // 2, raw.at[pl.ds(lo, n)], own, lo, n, across)
        if s % 4 == 3:
            lo, n = (s - 3) * STEP, 4 * STEP
            grad_send(4 + s // 4, raw.at[pl.ds(lo, n)], own, lo, n, mate)
    first = st[...].T[0:8]
    m, l, p, weight = [first[i : i + 1] for i in range(4)]
    own_m, across_rows = m, first
    stats = []

    def product(j, lo, n, src, base):
        plain[rows_of(j * OWN + lo, n)] = jnp.dot(
            src[rows_of(base + lo, n), :], wt_ref[...], preferred_element_type=F32
        )

    def relay(i):
        grads[i].wait_recv()
        grad_send(6 + i, gr.at[rows_of(mine_of * OWN + i * 64, 64)], mine_of, i * 64, 64, mate)

    for stage, where in enumerate((Z_PEERS, XY_PEERS)):
        mine[stage] = across_rows
        copies = []
        for i, s in enumerate(where):
            k = stage * 7 + i
            copies.append(send(mine.at[stage], sland.at[k], ss.at[k], sr.at[k], me.peer(**s)))
        if stage == 0:
            product(own, 0, OWN, raw, 0)
        else:
            grads[4].wait_recv()
            grads[5].wait_recv()
            product(mates, 0, OWN, gr, mates * OWN)
            relay(0)
            relay(1)
            product(mine_of, 0, PART, gr, mine_of * OWN)
        for copy in copies:
            copy.wait_recv()
        stats += copies
        m, l, p = merge(m, l, p, [sland[stage * 7 + i] for i in range(7)])
        across_rows = jnp.concatenate([m, l, p, jnp.zeros((5, OWN), F32)], axis=0)
    norm = m + jnp.log(l)
    logp = p - norm
    lp_ref[...] = jnp.concatenate([logp[:, 16 * r : 16 * r + 16] for r in range(16)], axis=0)

    tab[own] = jnp.concatenate(
        [weight * jnp.exp(own_m - norm), weight * (1.0 - jnp.exp(logp)), jnp.zeros((6, OWN), F32)], axis=0
    )
    tables = [send(tab.at[own], tab.at[own], ts.at[i], tr.at[i], who) for i, who in enumerate((mate, across, across_mate))]

    def scale(j, t):
        table, at_j = tab[j][:, t * PART : (t + 1) * PART], rows_of(j * OWN + t * PART, PART)
        cols[at_j] = jnp.concatenate([table, jnp.zeros((120, PART), F32)], axis=0).T

        @pl.loop(0, PART // STEP)
        def _(i):
            lo = t * PART + i * STEP
            at, to = rows_of(lo, STEP), rows_of(j * OWN + lo, STEP)
            part[j, at] = cols[to, 1:2] * part[j, at] - cols[to, 0:1] * plain[to, :]

    def turn(lo, hi):
        @pl.loop(lo, hi)
        def _(i):
            at = rows_of(i * STEP, STEP)
            g = jnp.where(vocab == id_ref[at, 0:1], cols[at, 1:2], -cols[at, 0:1] * gr[at, :].astype(F32))
            gr[at] = g.astype(BF16)

    def z_get(half, sub, chunk):
        ylo = me.ylo if half == EARLY else 1 - me.ylo
        return part[2 * ylo, rows_of(sub * PART + chunk * 16, 16), :]

    def x_get(half, sub, chunk):
        ylo = me.ylo if half == EARLY else 1 - me.ylo
        return part[2 * ylo + 1, rows_of(sub * PART + chunk * 32, 32), :]

    zring = Ring(NZ, me.z, z_get, zout, zland, zs, zr, me.peer(z=1), me.peer(z=-1))
    xring = Ring(NX, me.x, x_get, xrout, xrland, xrs, xrr, me.peer(x=1), me.peer(x=-1))
    def begin(half, t):
        zring.step(half, t, 0)
        xring.step(half, t, 0)

    def late(t):
        if t == 0:
            tables[1].wait_recv()
            tables[2].wait_recv()
        for i in (2 * t, 2 * t + 1):
            grads[6 + i].wait_recv()
        product(mates_of, t * PART, PART, gr, mates_of * OWN)

        @pl.loop(0, 2)
        def _(i):
            scale(other + i, t)

        begin(LATE, t)

    scale(own, 0)
    scale(own, 1)
    tables[0].wait_recv()
    scale(mates, 0)
    scale(mates, 1)
    begin(EARLY, 0)
    begin(EARLY, 1)
    late(0)
    relay(2)
    relay(3)
    product(mine_of, PART, PART, gr, mine_of * OWN)
    zring.step(EARLY, 0, 1)
    xring.step(EARLY, 0, 1)
    late(1)
    zring.step(EARLY, 1, 1)
    xring.step(EARLY, 1, 1)
    zring.step(LATE, 0, 1)
    xring.step(LATE, 0, 1)
    zring.step(EARLY, 0, 2)
    zring.step(EARLY, 1, 2)
    zring.step(LATE, 1, 1)
    xring.step(LATE, 1, 1)
    zring.step(LATE, 0, 2)
    zring.step(EARLY, 0, 3)
    zring.step(EARLY, 1, 3)
    for i in range(6, 10):
        grads[i].wait_send()
    own_at = rows_of(own * OWN, OWN)
    gr[own_at] = raw[...]

    def weight_tiles(lo, hi):
        @pl.loop(lo, hi)
        def _(i):
            at = pl.ds(al(i * 128, 128), 128)
            gw_tiles[at, :] = lax.dot_general(
                hd[:, at], gr[...], (((0,), (0,)), ((), ())), preferred_element_type=F32
            ).astype(BF16)

    def cut(ref, at):
        rows = rows_of((at // 2) * 16, 16)
        return ref.at[:, rows, pl.ds(al((at % 2) * 640, 128), 640)]

    later = []
    zring.step(LATE, 1, 2)
    for half, ylo in ((EARLY, me.ylo), (LATE, 1 - me.ylo)):
        for sub in range(2):
            x2[ylo, pl.ds(sub * 32, 32)] = xring.total(half, sub).astype(BF16)
    x_copies = []
    for i in range(1, NZ):
        x_copies.append(
            send(cut(x2, (me.z + i) % NZ), x2land.at[i - 1], x2s.at[i - 1], x2r.at[i - 1], me.peer(z=i))
        )
    zring.step(LATE, 0, 3)
    turn(0, 16)
    zring.step(LATE, 1, 3)
    turn(16, 32)
    weight_tiles(0, 2)
    for half, ylo in ((EARLY, me.ylo), (LATE, 1 - me.ylo)):
        for sub in range(2):
            z2[ylo, pl.ds(sub * 16, 16)] = zring.total(half, sub).astype(BF16)
    z_copies = []
    for i in range(1, NX):
        z_copies.append(
            send(cut(z2, (me.x + i) % NX), z2land.at[i - 1], z2s.at[i - 1], z2r.at[i - 1], me.peer(x=i))
        )
    weight_tiles(2, 6)
    for core, (ours, land, copies) in enumerate(
        ((cut(z2, me.x), z2land, z_copies), (cut(x2, me.z), x2land, x_copies))
    ):
        for copy in copies:
            copy.wait_recv()
        term = ours[...].astype(F32)
        for i in range(len(copies)):
            term = term + land[i].astype(F32)
        ysum[core] = term.astype(BF16)
        later += copies

    def kept_rows(core, x, z):
        return 16 * z + PART * (x // 2) if core == 0 else 32 * x + PART * (z // 4) + 16 * ((z // 2) % 2)

    def kept_cols(core, x, z):
        return (x % 2 if core == 0 else z % 2) * 640

    y_copies = {}
    for i, s in enumerate(Y_PEERS):
        piece = ysum.at[(me.c + s["c"]) % 2, (me.ylo + s["y"]) % 2]
        y_copies[s["y"], s["c"]] = send(piece, yland.at[i], ys.at[i], yr.at[i], me.peer(**s))
    weight_tiles(6, 10)
    gw_out = pltpu.make_async_copy(gw_tiles, gw_ref, loc.at[6])
    gw_out.start()
    row, col = kept_rows(0, me.x, me.z), kept_cols(0, me.x, me.z)
    row = jnp.where(me.c == 0, row, kept_rows(1, me.x, me.z))
    col = jnp.where(me.c == 0, col, kept_cols(1, me.x, me.z))
    for dc in range(2):
        for dy in range(2):
            pair = []
            for y in (dy, dy + 2):
                if (y, dc) == (0, 0):
                    pair.append(ysum[me.c, me.ylo].astype(F32))
                else:
                    mirror = ((NY - y) % NY, dc)
                    y_copies[mirror].wait_recv()
                    pair.append(yland[Y_PEERS.index(dict(y=mirror[0], c=mirror[1]))].astype(F32))
            owner = ((me.ylo + dy) % 2) * 2 + (me.c + dc) % 2
            gather[owner, rows_of(row, 16), pl.ds(al(col, 128), 640)] = (pair[0] + pair[1]).astype(BF16)
    later += list(y_copies.values())

    def piece(core, x, z):
        rows, at = rows_of(kept_rows(core, x, z), 16), pl.ds(al(kept_cols(core, x, z), 128), 640)
        return gather.at[:, rows, at]

    def z_off(i):
        return (me.z + i + NZ) % NZ

    def x_off(i):
        return (me.x + i + NX) % NX

    def put(copies, key, src, who):
        k = len(copies)
        copies[key] = send(src, src, bs.at[k], br.at[k], who)

    @pl.when(me.c == 0)
    def _():
        mine = piece(0, me.x, me.z)
        firsts = {i: send(mine, mine, as_.at[i - 1], ar.at[i - 1], me.peer(x=i)) for i in (2, 1, 3)}
        copies, order = {}, (0, 1, 3, 2)
        for q in order:
            if q:
                firsts[q].wait_recv()
            for away in (2, -2, 1, -1):
                put(copies, (q, away), piece(0, x_off(-q), me.z), me.peer(z=away))
        for q in order:
            for d in (1, -1):
                copies[q, 2 * d].wait_recv()
                came = piece(0, x_off(-q), z_off(-2 * d))
                if (q in (0, 3)) == (d == 1):
                    put(copies, (q, 4), came, me.peer(z=2 * d))
                put(copies, (q, 3 * d), came, me.peer(z=d))
        for q in order:
            for key in (1, -1, 3, -3, 4):
                copies[q, key].wait_recv()
        for copy in list(firsts.values()) + list(copies.values()):
            copy.wait_send()

    @pl.when(me.c == 1)
    def _():
        copies, xcopies = {}, {}
        mine = piece(1, me.x, me.z)

        def along_x(dz):
            at = piece(1, me.x, z_off(dz))
            for d in (1, -1):
                put(xcopies, (dz, d), at, me.peer(x=d))

        firsts = {}
        for i, away in enumerate((2, -2, 1, -1)):
            firsts[away] = send(mine, mine, as_.at[i], ar.at[i], me.peer(z=away))
        along_x(0)
        for d in (1, -1):
            firsts[2 * d].wait_recv()
            came = piece(1, me.x, z_off(-2 * d))
            half = came.at[pl.ds(0 if d == 1 else 2, 2)]
            k = 4 if d == 1 else 6
            firsts[4 * d] = send(half, half, as_.at[k], ar.at[k], me.peer(z=2 * d))
            firsts[3 * d] = send(came, came, as_.at[k + 1], ar.at[k + 1], me.peer(z=d))
        for d in (1, -1):
            firsts[d].wait_recv()
            along_x(-d)
        for d in (1, -1):
            along_x(-2 * d)
        for d in (1, -1):
            firsts[3 * d].wait_recv()
            along_x(-3 * d)
        for d in (1, -1):
            firsts[4 * d].wait_recv()
        along_x(-4)
        for dz in (0, -1, 1, -2, 2, -3, 3, -4):
            d = 1 if dz % 2 == 0 else -1
            xcopies[dz, d].wait_recv()
            put(xcopies, (dz, 2), piece(1, x_off(-d), z_off(dz)), me.peer(x=d))
        for dz in (0, -1, 1, -2, 2, -3, 3, -4):
            d = 1 if dz % 2 == 0 else -1
            xcopies[dz, -d].wait_recv()
            xcopies[dz, 2].wait_recv()
        for copy in list(firsts.values()) + list(xcopies.values()):
            copy.wait_send()

    outs = []
    for s in range(4):
        copy = pltpu.make_async_copy(gather.at[s], gh_ref.at[:, pl.ds(s * WIDE, WIDE)], loc.at[2 + s])
        copy.start()
        outs.append(copy)
    zring.finish()
    xring.finish()
    to_mate.wait_send()
    to_mate_part.wait_send()
    for copy in later + id_copies + exchanged + crossed + stats + tables + list(hidden.values()) + [grads[i] for i in range(6)]:
        copy.wait_send()
    for copy in outs + [gw_out]:
        copy.wait()


def fused(hidden, head_weight, prompt_ids, prompt_counts, sampled_ids, token_mask, rewards):
    vmem = pl.BlockSpec(memory_space=pltpu.VMEM)
    smem = pl.BlockSpec(memory_space=pltpu.SMEM)
    hbm = pl.BlockSpec(memory_space=pl.ANY)
    dma = lambda n: pltpu.SemaphoreType.DMA((n,))
    buf = lambda *shape: pltpu.VMEM(shape, BF16)
    wide = lambda *shape: pltpu.VMEM(shape, F32)
    return pl.pallas_call(
        kernel,
        out_shape=(
            jax.ShapeDtypeStruct((16, 16), F32),
            jax.ShapeDtypeStruct((OWN, 4 * WIDE), BF16),
            jax.ShapeDtypeStruct((WIDE, VOCAB), BF16),
        ),
        in_specs=[hbm, hbm, vmem, vmem, vmem, vmem, smem],
        out_specs=(vmem, hbm, hbm),
        scratch_shapes=[
            buf(WIDE, VOCAB), buf(VOCAB, WIDE), buf(ALL, WIDE), wide(OWN, VOCAB), wide(OWN, VOCAB), wide(OWN, VOCAB),
            wide(STEPS, STEP, VOCAB), wide(STEPS, STEP, VOCAB), wide(STEPS, STEP, VOCAB), wide(STEPS, STEP, VOCAB),
            wide(16, VOCAB), pltpu.VMEM((4, 16, 16), jnp.int32), wide(ALL, 128), wide(OWN, 128), wide(OWN, 128), wide(2, 8, OWN), wide(14, 8, OWN),
            wide(4, 8, OWN), wide(ALL, 128),
            buf(OWN, VOCAB), buf(ALL, VOCAB), wide(4, OWN, WIDE), wide(ALL, WIDE), buf(WIDE, VOCAB),
            buf(28, 16, 1280), buf(28, 16, 1280), buf(12, 32, 1280), buf(12, 32, 1280),
            buf(2, 32, 1280), buf(2, 64, 1280), buf(3, 2, 16, 640), buf(7, 2, 16, 640), buf(2, 2, 16, 640),
            buf(7, 16, 640), buf(4, OWN, WIDE),
            dma(7), dma(3), dma(3), dma(16), dma(16), dma(1), dma(1), dma(1), dma(1), dma(8), dma(8), dma(8), dma(8),
            dma(14), dma(14), dma(10), dma(10), dma(3), dma(3),
            dma(28), dma(28), dma(12), dma(12), dma(3), dma(3), dma(7), dma(7), dma(7), dma(7),
            dma(8), dma(8), dma(28), dma(28),
        ],
        compiler_params=pltpu.CompilerParams(
            collective_id=0, has_side_effects=True, vmem_limit_bytes=56 << 20
        ),
        name="fused",
    )(hidden, head_weight, prompt_ids, prompt_counts, sampled_ids, token_mask, rewards)


def solution(mesh):
    return jax.shard_map(
        fused,
        mesh=mesh,
        in_specs=(
            P("dp", None),
            P("dp", "tensor"),
            P("dp", None),
            P("dp", None),
            P("dp", None),
            P("dp", None),
            P("dp"),
        ),
        out_specs=(P("dp", None), P("dp", None), P("dp", "tensor")),
        check_vma=False,
    )
```

```python
import functools

import jax
import jax.numpy as jnp
from jax import lax
from jax.experimental import pallas as pl
from jax.experimental.pallas import tpu as pltpu
from jax.sharding import PartitionSpec as P

GROUP = 8
NX, NZ, NY = 4, 8, 4
MESH = pl.DeviceIdType.MESH
F32, BF16 = jnp.float32, jnp.bfloat16

recurrence_deduction = 0.4
presence_deduction = 0.6

class Place:
    def __init__(self):
        dp, t = lax.axis_index("dp"), lax.axis_index("tensor")
        self.ylo, self.c = dp // 2, dp % 2
        self.yhi, self.x, self.z = t // 32, (t // 8) % 4, t % 8
        self.dp = dp

    def peer(self, x=0, y=0, z=0, c=0):
        yy = (self.yhi * 2 + self.ylo + y + NY) % NY
        xx, zz, cc = (self.x + x + NX) % NX, (self.z + z + NZ) % NZ, (self.c + c) % 2
        return ((yy % 2) * 2 + cc, (yy // 2) * 32 + xx * 8 + zz)


def arrive(barrier, peers):
    for who in peers:
        pl.semaphore_signal(barrier, inc=1, device_id=who, device_id_type=MESH)


def send(src, dst, ssem, rsem, who):
    copy = pltpu.make_async_remote_copy(
        src_ref=src, dst_ref=dst, send_sem=ssem, recv_sem=rsem, device_id=who, device_id_type=MESH
    )
    copy.start()
    return copy


Z_PEERS = [dict(z=i) for i in range(1, NZ)]
X_PEERS = [dict(x=i) for i in range(1, NX)]
Y_PEERS = [dict(y=i, c=j) for i in range(NY) for j in range(2) if (i, j) != (0, 0)]
XY_PEERS = [dict(x=i, y=j) for i in range(NX) for j in (0, 2) if (i, j) != (0, 0)]
ALL_PEERS = Z_PEERS + X_PEERS + Y_PEERS + [dict(x=i, y=2) for i in range(1, NX)]

WIDE, VOCAB, OWN, ALL = 1280, 1280, 256, 1024
STEP, STEPS = 32, 8
DIRECT = (1, 3)
EARLY, LATE = 0, 1
PART = 128
CHAINS = [(d, half, sub, (d == 1) == (sub == 0)) for half in (EARLY, LATE) for sub in range(2) for d in (1, -1)]


def al(i, n):
    return pl.multiple_of(i, n)


class Ring:
    def __init__(self, n, at, get, out, land, ssem, rsem, ahead, behind):
        self.n, self.at, self.get, self.out, self.land = n, at, get, out, land
        self.ssem, self.rsem, self.toward = ssem, rsem, {1: ahead, -1: behind}
        self.slots, self.copies = {}, {}
        for i in range(len(CHAINS)):
            for h in range(self.hops(i)):
                self.slots[i, h] = len(self.slots)

    def hops(self, i):
        return self.n // 2 - (0 if CHAINS[i][3] else 1)

    def step(self, half, sub, h):
        for i, (d, hf, sb, far) in enumerate(CHAINS):
            if h >= self.hops(i) or (hf, sb) != (half, sub):
                continue
            chunk = (self.at + d * (self.hops(i) - h) + self.n) % self.n
            term = self.get(half, sub, chunk)
            if h:
                self.copies[i, h - 1].wait_recv()
                term = term + self.land[self.slots[i, h - 1]].astype(F32)
            k = self.slots[i, h]
            self.out[k] = term.astype(BF16)
            self.copies[i, h] = send(
                self.out.at[k], self.land.at[k], self.ssem.at[k], self.rsem.at[k], self.toward[d]
            )

    def total(self, half, sub):
        term = self.get(half, sub, self.at)
        for i, (d, hf, sb, far) in enumerate(CHAINS):
            if (hf, sb) == (half, sub):
                self.copies[i, self.hops(i) - 1].wait_recv()
                term = term + self.land[self.slots[i, self.hops(i) - 1]].astype(F32)
        return term

    def finish(self):
        for copy in self.copies.values():
            copy.wait_send()


def merge(m, l, p, others):
    top = m
    for o in others:
        top = jnp.maximum(top, o[0:1])
    l = l * jnp.exp(m - top)
    for o in others:
        l = l + o[1:2] * jnp.exp(o[0:1] - top)
        p = p + o[2:3]
    return top, l, p


def rows_of(i, n):
    return pl.ds(al(i, n), n)


def kernel(
    hid_ref, w_hbm, pid_ref, pc_ref, sid_ref, mask_ref, rew_ref, lp_ref, gh_ref, gw_ref,
    w_ref, wt_ref, hd, lex, pout, pland, xout, xland, lout, lland, prompt, sids, id_ref, tw_ref, st, mine, sland, tab, cols,
    raw, gr, part, plain, gw_tiles, zout, zland, xrout, xrland, z2, x2, z2land, x2land, ysum, yland, gather,
    loc, is_, ir, hs, hr, cs, cr, ps, pr, xs, xr, ls, lr, ss, sr, gs, grs, ts, tr,
    zs, zr, xrs, xrr, z2s, z2r, x2s, x2r, ys, yr, as_, ar, bs, br,
):
    me = Place()
    toward = 1 - 2 * me.ylo
    mate, across, across_mate = me.peer(c=1), me.peer(y=toward), me.peer(y=toward, c=1)
    other = 2 * (1 - me.ylo)
    own, mates = me.dp, 2 * me.ylo + 1 - me.c
    mine_of, mates_of = other + me.c, other + 1 - me.c

    copy_w = pltpu.make_async_copy(w_hbm, w_ref, loc.at[0])
    copy_h = pltpu.make_async_copy(
        hid_ref.at[:, pl.ds(al(own * WIDE, 128), WIDE)], hd.at[rows_of(own * OWN, OWN)], loc.at[1]
    )
    copy_w.start()
    copy_h.start()
    peers = [me.peer(**s) for s in ALL_PEERS]
    barrier = pltpu.get_barrier_semaphore()
    arrive(barrier, peers)

    offset = (me.yhi * 32 + me.x * 8 + me.z) * VOCAB
    column = lax.broadcasted_iota(jnp.int32, (16, VOCAB), 1) + offset
    tile = jnp.zeros((16, VOCAB), F32)
    pid, pc = pid_ref[...], pc_ref[...].astype(F32)
    for j in range(pid.shape[1]):
        tile = tile + jnp.where(pid[:, j : j + 1] == column, pc[:, j : j + 1], 0.0)
    prompt[...] = tile
    its_lane = lax.broadcasted_iota(jnp.int32, (OWN, 16), 1) == lax.broadcasted_iota(jnp.int32, (OWN, 16), 0) % 16

    def as_column(rows):
        wide_rows = jnp.concatenate([jnp.broadcast_to(rows[r : r + 1, :], (16, 16)) for r in range(16)], axis=0)
        return jnp.broadcast_to(jnp.sum(jnp.where(its_lane, wide_rows, 0.0), axis=1, keepdims=True), (OWN, 128))

    which = lax.broadcasted_iota(jnp.int32, (16, 16), 0)
    advantage = jnp.zeros((16, 16), F32)
    for g in range(16 // GROUP):
        rewards = [rew_ref[g * GROUP + r] for r in range(GROUP)]
        mean = sum(rewards[1:], rewards[0]) * (1.0 / GROUP)
        for r in range(GROUP):
            advantage = jnp.where(which == g * GROUP + r, rewards[r] - mean, advantage)
    weight = -(advantage * mask_ref[...].astype(F32)) * 1.25
    sids[own] = sid_ref[...]
    id_ref[rows_of(own * OWN, OWN)] = as_column(sid_ref[...].astype(F32))
    tw_ref[...] = as_column(weight)
    pl.semaphore_wait(barrier, len(peers))

    def hidden_copy(rel, step, way):
        who = me.peer(y=way, c=rel)
        to = other + (me.c + rel) % 2
        k = rel * STEPS + step
        return pltpu.make_async_remote_copy(
            src_ref=hid_ref.at[rows_of(step * STEP, STEP), pl.ds(al(to * WIDE, 128), WIDE)],
            dst_ref=hd.at[rows_of(own * OWN + step * STEP, STEP)],
            send_sem=hs.at[k],
            recv_sem=hr.at[k],
            device_id=who,
            device_id_type=MESH,
        )

    wrapped = [s for s in range(STEPS) if s not in DIRECT]
    hidden = {}
    for s in range(STEPS):
        for rel in range(2):
            hidden[rel, s] = hidden_copy(rel, s, toward if s in DIRECT else -toward)
    ahead = 3
    for s in (wrapped[0],) + DIRECT[:1]:
        for rel in range(2):
            hidden[rel, s].start()
    to_mate = send(
        hid_ref.at[:, pl.ds(al(mates * WIDE, 128), WIDE)], hd.at[rows_of(own * OWN, OWN)],
        cs.at[0], cr.at[0], mate,
    )
    for s in tuple(wrapped[1:ahead]) + DIRECT[1:]:
        for rel in range(2):
            hidden[rel, s].start()

    id_copies = [
        send(sids.at[own], sids.at[own], is_.at[i], ir.at[i], who) for i, who in enumerate((mate, across, across_mate))
    ]
    copy_w.wait()

    @pl.loop(0, 10)
    def _(i):
        at = pl.ds(al(i * 128, 128), 128)
        wt_ref[:, at] = w_ref[at, :].T

    copy_h.wait()
    to_mate.wait_recv()

    pout[...] = jnp.dot(hd[rows_of(mates * OWN, OWN), :], w_ref[...], preferred_element_type=F32)
    to_mate_part = send(pout, pland, ps.at[0], pr.at[0], mate)
    exchanged, crossed = [], []
    vocab = (lax.broadcasted_iota(jnp.int32, (STEP, VOCAB), 1) + offset).astype(F32)
    vocab_wide = (lax.broadcasted_iota(jnp.int32, (OWN, VOCAB), 1) + offset).astype(F32)

    def sampled_rows(j):
        chosen = jnp.where(vocab_wide == id_ref[rows_of(j * OWN, OWN), 0:1], 1.0, 0.0).astype(BF16)
        part[j] = jnp.dot(chosen, wt_ref[...], preferred_element_type=F32)

    sampled_rows(own)
    for s in range(STEPS):
        for rel in range(2):
            hidden[rel, s].wait_recv()
        both = jnp.concatenate(
            [hd[rows_of(mates_of * OWN + s * STEP, STEP), :], hd[rows_of(mine_of * OWN + s * STEP, STEP), :]], axis=0
        )
        term = jnp.dot(both, w_ref[...], preferred_element_type=F32)
        xout[s] = term[:STEP]
        exchanged.append(send(xout.at[s], xland.at[s], xs.at[s], xr.at[s], mate))
        if s in wrapped:
            i = wrapped.index(s) + ahead
            if i < len(wrapped):
                for rel in range(2):
                    hidden[rel, wrapped[i]].start()
        if s == 1:
            lex[...] = jnp.dot(hd[rows_of(own * OWN, OWN), :], w_ref[...], preferred_element_type=F32)
        if s == 2:
            for copy in id_copies:
                copy.wait_recv()
            for i in range(1, 4):
                j = (own + i) % 4
                id_ref[rows_of(j * OWN, OWN)] = as_column(sids[j].astype(F32))
        if 3 <= s < 6:
            sampled_rows((own + s - 2) % 4)
        exchanged[s].wait_recv()
        lout[s] = term[STEP:] + xland[s]
        crossed.append(send(lout.at[s], lland.at[s], ls.at[s], lr.at[s], across))

    grads = {}

    def grad_send(k, src, j, lo, n, who):
        grads[k] = send(src, gr.at[rows_of(j * OWN + lo, n)], gs.at[k], grs.at[k], who)

    to_mate_part.wait_recv()
    lane = lax.broadcasted_iota(jnp.int32, (STEP, 128), 1)
    k_of = lax.broadcasted_iota(jnp.int32, (STEP, STEP), 0)
    q_of = lax.broadcasted_iota(jnp.int32, (STEP, STEP), 1)
    earlier = jnp.where((q_of < k_of) & (q_of // 16 == k_of // 16), 1.0, 0.0).astype(BF16)
    for s in range(STEPS):
        crossed[s].wait_recv()
        at = pl.ds(s * STEP, STEP)
        ids = id_ref[rows_of(own * OWN + s * STEP, STEP), 0:1]
        chosen = vocab == ids
        tally = jnp.dot(earlier, jnp.where(chosen, 1.0, 0.0).astype(BF16), preferred_element_type=F32)
        tally = tally + jnp.concatenate(
            [jnp.broadcast_to(prompt[2 * s + i : 2 * s + i + 1, :], (16, VOCAB)) for i in range(2)], axis=0
        )
        penalty = recurrence_deduction * tally + jnp.where(tally > 0.0, presence_deduction, 0.0)
        scaled = (lex[at, :] + pland[at, :] + lland[s] - penalty) * 1.25
        m = jnp.max(scaled, axis=1, keepdims=True)
        raised = jnp.exp(scaled - m)
        l = jnp.sum(raised, axis=1, keepdims=True)
        p = jnp.sum(jnp.where(chosen, scaled, 0.0), axis=1, keepdims=True)
        raw[at, :] = jnp.where(chosen, 0.0, raised).astype(BF16)
        table = jnp.zeros((STEP, 128), F32)
        for i, v in enumerate((m, l, p, tw_ref[at, 0:1])):
            table = jnp.where(lane == i, v, table)
        st[at, :] = table
        if s % 2:
            lo, n = (s - 1) * STEP, 2 * STEP
            grad_send(s // 2, raw.at[pl.ds(lo, n)], own, lo, n, across)
        if s % 4 == 3:
            lo, n = (s - 3) * STEP, 4 * STEP
            grad_send(4 + s // 4, raw.at[pl.ds(lo, n)], own, lo, n, mate)
    first = st[...].T[0:8]
    m, l, p, weight = [first[i : i + 1] for i in range(4)]
    own_m, across_rows = m, first
    stats = []

    def product(j, lo, n, src, base):
        plain[rows_of(j * OWN + lo, n)] = jnp.dot(
            src[rows_of(base + lo, n), :], wt_ref[...], preferred_element_type=F32
        )

    def relay(i):
        grads[i].wait_recv()
        grad_send(6 + i, gr.at[rows_of(mine_of * OWN + i * 64, 64)], mine_of, i * 64, 64, mate)

    for stage, where in enumerate((Z_PEERS, XY_PEERS)):
        mine[stage] = across_rows
        copies = []
        for i, s in enumerate(where):
            k = stage * 7 + i
            copies.append(send(mine.at[stage], sland.at[k], ss.at[k], sr.at[k], me.peer(**s)))
        if stage == 0:
            product(own, 0, OWN, raw, 0)
        else:
            grads[4].wait_recv()
            grads[5].wait_recv()
            product(mates, 0, OWN, gr, mates * OWN)
            relay(0)
            relay(1)
            product(mine_of, 0, PART, gr, mine_of * OWN)
        for copy in copies:
            copy.wait_recv()
        stats += copies
        m, l, p = merge(m, l, p, [sland[stage * 7 + i] for i in range(7)])
        across_rows = jnp.concatenate([m, l, p, jnp.zeros((5, OWN), F32)], axis=0)
    norm = m + jnp.log(l)
    logp = p - norm
    lp_ref[...] = jnp.concatenate([logp[:, 16 * r : 16 * r + 16] for r in range(16)], axis=0)

    tab[own] = jnp.concatenate(
        [weight * jnp.exp(own_m - norm), weight * (1.0 - jnp.exp(logp)), jnp.zeros((6, OWN), F32)], axis=0
    )
    tables = [send(tab.at[own], tab.at[own], ts.at[i], tr.at[i], who) for i, who in enumerate((mate, across, across_mate))]

    def scale(j, t):
        table, at_j = tab[j][:, t * PART : (t + 1) * PART], rows_of(j * OWN + t * PART, PART)
        cols[at_j] = jnp.concatenate([table, jnp.zeros((120, PART), F32)], axis=0).T

        @pl.loop(0, PART // STEP)
        def _(i):
            lo = t * PART + i * STEP
            at, to = rows_of(lo, STEP), rows_of(j * OWN + lo, STEP)
            part[j, at] = cols[to, 1:2] * part[j, at] - cols[to, 0:1] * plain[to, :]

    def turn(lo, hi):
        @pl.loop(lo, hi)
        def _(i):
            at = rows_of(i * STEP, STEP)
            g = jnp.where(vocab == id_ref[at, 0:1], cols[at, 1:2], -cols[at, 0:1] * gr[at, :].astype(F32))
            gr[at] = g.astype(BF16)

    def z_get(half, sub, chunk):
        ylo = me.ylo if half == EARLY else 1 - me.ylo
        return part[2 * ylo, rows_of(sub * PART + chunk * 16, 16), :]

    def x_get(half, sub, chunk):
        ylo = me.ylo if half == EARLY else 1 - me.ylo
        return part[2 * ylo + 1, rows_of(sub * PART + chunk * 32, 32), :]

    zring = Ring(NZ, me.z, z_get, zout, zland, zs, zr, me.peer(z=1), me.peer(z=-1))
    xring = Ring(NX, me.x, x_get, xrout, xrland, xrs, xrr, me.peer(x=1), me.peer(x=-1))
    def begin(half, t):
        zring.step(half, t, 0)
        xring.step(half, t, 0)

    def late(t):
        if t == 0:
            tables[1].wait_recv()
            tables[2].wait_recv()
        for i in (2 * t, 2 * t + 1):
            grads[6 + i].wait_recv()
        product(mates_of, t * PART, PART, gr, mates_of * OWN)

        @pl.loop(0, 2)
        def _(i):
            scale(other + i, t)

        begin(LATE, t)

    scale(own, 0)
    scale(own, 1)
    tables[0].wait_recv()
    scale(mates, 0)
    scale(mates, 1)
    begin(EARLY, 0)
    begin(EARLY, 1)
    late(0)
    relay(2)
    relay(3)
    product(mine_of, PART, PART, gr, mine_of * OWN)
    zring.step(EARLY, 0, 1)
    xring.step(EARLY, 0, 1)
    late(1)
    zring.step(EARLY, 1, 1)
    xring.step(EARLY, 1, 1)
    zring.step(LATE, 0, 1)
    xring.step(LATE, 0, 1)
    zring.step(EARLY, 0, 2)
    zring.step(EARLY, 1, 2)
    zring.step(LATE, 1, 1)
    xring.step(LATE, 1, 1)
    zring.step(LATE, 0, 2)
    zring.step(EARLY, 0, 3)
    zring.step(EARLY, 1, 3)
    for i in range(6, 10):
        grads[i].wait_send()
    own_at = rows_of(own * OWN, OWN)
    gr[own_at] = raw[...]

    def weight_tiles(lo, hi):
        @pl.loop(lo, hi)
        def _(i):
            at = pl.ds(al(i * 128, 128), 128)
            gw_tiles[at, :] = lax.dot_general(
                hd[:, at], gr[...], (((0,), (0,)), ((), ())), preferred_element_type=F32
            ).astype(BF16)

    def cut(ref, at):
        rows = rows_of((at // 2) * 16, 16)
        return ref.at[:, rows, pl.ds(al((at % 2) * 640, 128), 640)]

    later = []
    zring.step(LATE, 1, 2)
    for half, ylo in ((EARLY, me.ylo), (LATE, 1 - me.ylo)):
        for sub in range(2):
            x2[ylo, pl.ds(sub * 32, 32)] = xring.total(half, sub).astype(BF16)
    x_copies = []
    for i in range(1, NZ):
        x_copies.append(
            send(cut(x2, (me.z + i) % NZ), x2land.at[i - 1], x2s.at[i - 1], x2r.at[i - 1], me.peer(z=i))
        )
    zring.step(LATE, 0, 3)
    turn(0, 8)
    zring.step(LATE, 1, 3)
    turn(8, 16)
    for half, ylo in ((EARLY, me.ylo), (LATE, 1 - me.ylo)):
        for sub in range(2):
            z2[ylo, pl.ds(sub * 16, 16)] = zring.total(half, sub).astype(BF16)
    z_copies = []
    for i in range(1, NX):
        z_copies.append(
            send(cut(z2, (me.x + i) % NX), z2land.at[i - 1], z2s.at[i - 1], z2r.at[i - 1], me.peer(x=i))
        )
    turn(16, 32)
    for core, (ours, land, copies) in enumerate(
        ((cut(z2, me.x), z2land, z_copies), (cut(x2, me.z), x2land, x_copies))
    ):
        for copy in copies:
            copy.wait_recv()
        term = ours[...].astype(F32)
        for i in range(len(copies)):
            term = term + land[i].astype(F32)
        ysum[core] = term.astype(BF16)
        later += copies

    def kept_rows(core, x, z):
        return 16 * z + PART * (x // 2) if core == 0 else 32 * x + PART * (z // 4) + 16 * ((z // 2) % 2)

    def kept_cols(core, x, z):
        return (x % 2 if core == 0 else z % 2) * 640

    y_copies = {}
    for i, s in enumerate(Y_PEERS):
        piece = ysum.at[(me.c + s["c"]) % 2, (me.ylo + s["y"]) % 2]
        y_copies[s["y"], s["c"]] = send(piece, yland.at[i], ys.at[i], yr.at[i], me.peer(**s))
    weight_tiles(0, 3)
    gw_out = pltpu.make_async_copy(gw_tiles, gw_ref, loc.at[6])
    row, col = kept_rows(0, me.x, me.z), kept_cols(0, me.x, me.z)
    row = jnp.where(me.c == 0, row, kept_rows(1, me.x, me.z))
    col = jnp.where(me.c == 0, col, kept_cols(1, me.x, me.z))
    for dc in range(2):
        for dy in range(2):
            pair = []
            for y in (dy, dy + 2):
                if (y, dc) == (0, 0):
                    pair.append(ysum[me.c, me.ylo].astype(F32))
                else:
                    mirror = ((NY - y) % NY, dc)
                    y_copies[mirror].wait_recv()
                    pair.append(yland[Y_PEERS.index(dict(y=mirror[0], c=mirror[1]))].astype(F32))
            owner = ((me.ylo + dy) % 2) * 2 + (me.c + dc) % 2
            gather[owner, rows_of(row, 16), pl.ds(al(col, 128), 640)] = (pair[0] + pair[1]).astype(BF16)
    later += list(y_copies.values())

    def piece(core, x, z):
        rows, at = rows_of(kept_rows(core, x, z), 16), pl.ds(al(kept_cols(core, x, z), 128), 640)
        return gather.at[:, rows, at]

    def z_off(i):
        return (me.z + i + NZ) % NZ

    def x_off(i):
        return (me.x + i + NX) % NX

    def put(copies, key, src, who):
        k = len(copies)
        copies[key] = send(src, src, bs.at[k], br.at[k], who)

    @pl.when(me.c == 0)
    def _():
        mine = piece(0, me.x, me.z)
        firsts = {i: send(mine, mine, as_.at[i - 1], ar.at[i - 1], me.peer(x=i)) for i in (2, 1, 3)}
        copies, order = {}, (0, 1, 3, 2)
        hops = lambda q, d: NZ // 2 - (0 if (d == 1) == (q in (0, 3)) else 1)
        for h in range(NZ // 2):
            for q in order:
                if h == 0 and q:
                    firsts[q].wait_recv()
                for d in (1, -1):
                    if h >= hops(q, d):
                        continue
                    if h:
                        copies[q, d, h - 1].wait_recv()
                    put(copies, (q, d, h), piece(0, x_off(-q), z_off(-d * h)), me.peer(z=d))
                if h == 0 and q == 0:
                    weight_tiles(3, 7)
            if h == 0:
                weight_tiles(7, 10)
                gw_out.start()
        for q in order:
            for d in (1, -1):
                copies[q, d, hops(q, d) - 1].wait_recv()
        for copy in list(firsts.values()) + list(copies.values()):
            copy.wait_send()

    @pl.when(me.c == 1)
    def _():
        copies, xcopies = {}, {}
        mine = piece(1, me.x, me.z)

        def along_x(dz):
            at = piece(1, me.x, z_off(dz))
            for d in (1, -1):
                put(xcopies, (dz, d), at, me.peer(x=d))

        firsts = {}
        for i, away in enumerate((2, -2, 1, -1)):
            firsts[away] = send(mine, mine, as_.at[i], ar.at[i], me.peer(z=away))
        along_x(0)
        weight_tiles(3, 7)
        for d in (1, -1):
            firsts[2 * d].wait_recv()
            came = piece(1, me.x, z_off(-2 * d))
            half = came.at[pl.ds(0 if d == 1 else 2, 2)]
            k = 4 if d == 1 else 6
            firsts[4 * d] = send(half, half, as_.at[k], ar.at[k], me.peer(z=2 * d))
            firsts[3 * d] = send(came, came, as_.at[k + 1], ar.at[k + 1], me.peer(z=d))
        for d in (1, -1):
            firsts[d].wait_recv()
            along_x(-d)
        for d in (1, -1):
            along_x(-2 * d)
        for d in (1, -1):
            firsts[3 * d].wait_recv()
            along_x(-3 * d)
        weight_tiles(7, 10)
        gw_out.start()
        for d in (1, -1):
            firsts[4 * d].wait_recv()
        along_x(-4)
        for dz in (0, -1, 1, -2, 2, -3, 3, -4):
            d = 1 if dz % 2 == 0 else -1
            xcopies[dz, d].wait_recv()
            put(xcopies, (dz, 2), piece(1, x_off(-d), z_off(dz)), me.peer(x=d))
        for dz in (0, -1, 1, -2, 2, -3, 3, -4):
            d = 1 if dz % 2 == 0 else -1
            xcopies[dz, -d].wait_recv()
            xcopies[dz, 2].wait_recv()
        for copy in list(firsts.values()) + list(xcopies.values()):
            copy.wait_send()

    outs = []
    for s in range(4):
        copy = pltpu.make_async_copy(gather.at[s], gh_ref.at[:, pl.ds(s * WIDE, WIDE)], loc.at[2 + s])
        copy.start()
        outs.append(copy)
    zring.finish()
    xring.finish()
    to_mate.wait_send()
    to_mate_part.wait_send()
    for copy in later + id_copies + exchanged + crossed + stats + tables + list(hidden.values()) + [grads[i] for i in range(6)]:
        copy.wait_send()
    for copy in outs + [gw_out]:
        copy.wait()


def fused(hidden, head_weight, prompt_ids, prompt_counts, sampled_ids, token_mask, rewards):
    vmem = pl.BlockSpec(memory_space=pltpu.VMEM)
    smem = pl.BlockSpec(memory_space=pltpu.SMEM)
    hbm = pl.BlockSpec(memory_space=pl.ANY)
    dma = lambda n: pltpu.SemaphoreType.DMA((n,))
    buf = lambda *shape: pltpu.VMEM(shape, BF16)
    wide = lambda *shape: pltpu.VMEM(shape, F32)
    return pl.pallas_call(
        kernel,
        out_shape=(
            jax.ShapeDtypeStruct((16, 16), F32),
            jax.ShapeDtypeStruct((OWN, 4 * WIDE), BF16),
            jax.ShapeDtypeStruct((WIDE, VOCAB), BF16),
        ),
        in_specs=[hbm, hbm, vmem, vmem, vmem, vmem, smem],
        out_specs=(vmem, hbm, hbm),
        scratch_shapes=[
            buf(WIDE, VOCAB), buf(VOCAB, WIDE), buf(ALL, WIDE), wide(OWN, VOCAB), wide(OWN, VOCAB), wide(OWN, VOCAB),
            wide(STEPS, STEP, VOCAB), wide(STEPS, STEP, VOCAB), wide(STEPS, STEP, VOCAB), wide(STEPS, STEP, VOCAB),
            wide(16, VOCAB), pltpu.VMEM((4, 16, 16), jnp.int32), wide(ALL, 128), wide(OWN, 128), wide(OWN, 128), wide(2, 8, OWN), wide(14, 8, OWN),
            wide(4, 8, OWN), wide(ALL, 128),
            buf(OWN, VOCAB), buf(ALL, VOCAB), wide(4, OWN, WIDE), wide(ALL, WIDE), buf(WIDE, VOCAB),
            buf(28, 16, 1280), buf(28, 16, 1280), buf(12, 32, 1280), buf(12, 32, 1280),
            buf(2, 32, 1280), buf(2, 64, 1280), buf(3, 2, 16, 640), buf(7, 2, 16, 640), buf(2, 2, 16, 640),
            buf(7, 16, 640), buf(4, OWN, WIDE),
            dma(7), dma(3), dma(3), dma(16), dma(16), dma(1), dma(1), dma(1), dma(1), dma(8), dma(8), dma(8), dma(8),
            dma(14), dma(14), dma(10), dma(10), dma(3), dma(3),
            dma(28), dma(28), dma(12), dma(12), dma(3), dma(3), dma(7), dma(7), dma(7), dma(7),
            dma(8), dma(8), dma(28), dma(28),
        ],
        compiler_params=pltpu.CompilerParams(
            collective_id=0, has_side_effects=True, vmem_limit_bytes=56 << 20
        ),
        name="fused",
    )(hidden, head_weight, prompt_ids, prompt_counts, sampled_ids, token_mask, rewards)


def solution(mesh):
    return jax.shard_map(
        fused,
        mesh=mesh,
        in_specs=(
            P("dp", None),
            P("dp", "tensor"),
            P("dp", None),
            P("dp", None),
            P("dp", None),
            P("dp", None),
            P("dp"),
        ),
        out_specs=(P("dp", None), P("dp", None), P("dp", "tensor")),
        check_vma=False,
    )
```

```python
import functools

import jax
import jax.numpy as jnp
from jax import lax
from jax.experimental import pallas as pl
from jax.experimental.pallas import tpu as pltpu
from jax.sharding import PartitionSpec as P

GROUP = 8
NX, NZ, NY = 4, 8, 4
MESH = pl.DeviceIdType.MESH
F32, BF16 = jnp.float32, jnp.bfloat16

recurrence_deduction = 0.4
presence_deduction = 0.6

class Place:
    def __init__(self):
        dp, t = lax.axis_index("dp"), lax.axis_index("tensor")
        self.ylo, self.c = dp // 2, dp % 2
        self.yhi, self.x, self.z = t // 32, (t // 8) % 4, t % 8
        self.dp = dp

    def peer(self, x=0, y=0, z=0, c=0):
        yy = (self.yhi * 2 + self.ylo + y + NY) % NY
        xx, zz, cc = (self.x + x + NX) % NX, (self.z + z + NZ) % NZ, (self.c + c) % 2
        return ((yy % 2) * 2 + cc, (yy // 2) * 32 + xx * 8 + zz)


def arrive(barrier, peers):
    for who in peers:
        pl.semaphore_signal(barrier, inc=1, device_id=who, device_id_type=MESH)


def send(src, dst, ssem, rsem, who):
    copy = pltpu.make_async_remote_copy(
        src_ref=src, dst_ref=dst, send_sem=ssem, recv_sem=rsem, device_id=who, device_id_type=MESH
    )
    copy.start()
    return copy


Z_PEERS = [dict(z=i) for i in range(1, NZ)]
X_PEERS = [dict(x=i) for i in range(1, NX)]
Y_PEERS = [dict(y=i, c=j) for i in range(NY) for j in range(2) if (i, j) != (0, 0)]
XY_PEERS = [dict(x=i, y=j) for i in range(NX) for j in (0, 2) if (i, j) != (0, 0)]
ALL_PEERS = Z_PEERS + X_PEERS + Y_PEERS + [dict(x=i, y=2) for i in range(1, NX)]

WIDE, VOCAB, OWN, ALL = 1280, 1280, 256, 1024
STEP, STEPS = 32, 8
DIRECT = (1, 3)
EARLY, LATE = 0, 1
PART = 128
CHAINS = [(d, half, sub, (d == 1) == (sub == 0)) for half in (EARLY, LATE) for sub in range(2) for d in (1, -1)]


def al(i, n):
    return pl.multiple_of(i, n)


class Ring:
    def __init__(self, n, at, get, out, land, ssem, rsem, ahead, behind):
        self.n, self.at, self.get, self.out, self.land = n, at, get, out, land
        self.ssem, self.rsem, self.toward = ssem, rsem, {1: ahead, -1: behind}
        self.slots, self.copies = {}, {}
        for i in range(len(CHAINS)):
            for h in range(self.hops(i)):
                self.slots[i, h] = len(self.slots)

    def hops(self, i):
        return self.n // 2 - (0 if CHAINS[i][3] else 1)

    def step(self, half, sub, h):
        for i, (d, hf, sb, far) in enumerate(CHAINS):
            if h >= self.hops(i) or (hf, sb) != (half, sub):
                continue
            chunk = (self.at + d * (self.hops(i) - h) + self.n) % self.n
            term = self.get(half, sub, chunk)
            if h:
                self.copies[i, h - 1].wait_recv()
                term = term + self.land[self.slots[i, h - 1]].astype(F32)
            k = self.slots[i, h]
            self.out[k] = term.astype(BF16)
            self.copies[i, h] = send(
                self.out.at[k], self.land.at[k], self.ssem.at[k], self.rsem.at[k], self.toward[d]
            )

    def total(self, half, sub):
        term = self.get(half, sub, self.at)
        for i, (d, hf, sb, far) in enumerate(CHAINS):
            if (hf, sb) == (half, sub):
                self.copies[i, self.hops(i) - 1].wait_recv()
                term = term + self.land[self.slots[i, self.hops(i) - 1]].astype(F32)
        return term

    def finish(self):
        for copy in self.copies.values():
            copy.wait_send()


def merge(m, l, p, others):
    top = m
    for o in others:
        top = jnp.maximum(top, o[0:1])
    l = l * jnp.exp(m - top)
    for o in others:
        l = l + o[1:2] * jnp.exp(o[0:1] - top)
        p = p + o[2:3]
    return top, l, p


def rows_of(i, n):
    return pl.ds(al(i, n), n)


def kernel(
    hid_ref, w_hbm, pid_ref, pc_ref, sid_ref, mask_ref, rew_ref, lp_ref, gh_ref, gw_ref,
    w_ref, wt_ref, hd, lex, pout, pland, xout, xland, lout, lland, prompt, sids, id_ref, tw_ref, st, mine, sland, tab, cols,
    raw, gr, part, plain, gw_tiles, zout, zland, xrout, xrland, z2, x2, z2land, x2land, ysum, yland, gather,
    loc, is_, ir, hs, hr, cs, cr, ps, pr, xs, xr, ls, lr, ss, sr, gs, grs, ts, tr,
    zs, zr, xrs, xrr, z2s, z2r, x2s, x2r, ys, yr, as_, ar, bs, br,
):
    me = Place()
    toward = 1 - 2 * me.ylo
    mate, across, across_mate = me.peer(c=1), me.peer(y=toward), me.peer(y=toward, c=1)
    other = 2 * (1 - me.ylo)
    own, mates = me.dp, 2 * me.ylo + 1 - me.c
    mine_of, mates_of = other + me.c, other + 1 - me.c

    copy_w = pltpu.make_async_copy(w_hbm, w_ref, loc.at[0])
    copy_h = pltpu.make_async_copy(
        hid_ref.at[:, pl.ds(al(own * WIDE, 128), WIDE)], hd.at[rows_of(own * OWN, OWN)], loc.at[1]
    )
    copy_w.start()
    copy_h.start()
    peers = [me.peer(**s) for s in ALL_PEERS]
    barrier = pltpu.get_barrier_semaphore()
    arrive(barrier, peers)

    offset = (me.yhi * 32 + me.x * 8 + me.z) * VOCAB
    column = lax.broadcasted_iota(jnp.int32, (16, VOCAB), 1) + offset
    tile = jnp.zeros((16, VOCAB), F32)
    pid, pc = pid_ref[...], pc_ref[...].astype(F32)
    for j in range(pid.shape[1]):
        tile = tile + jnp.where(pid[:, j : j + 1] == column, pc[:, j : j + 1], 0.0)
    prompt[...] = tile
    its_lane = lax.broadcasted_iota(jnp.int32, (OWN, 16), 1) == lax.broadcasted_iota(jnp.int32, (OWN, 16), 0) % 16

    def as_column(rows):
        wide_rows = jnp.concatenate([jnp.broadcast_to(rows[r : r + 1, :], (16, 16)) for r in range(16)], axis=0)
        return jnp.broadcast_to(jnp.sum(jnp.where(its_lane, wide_rows, 0.0), axis=1, keepdims=True), (OWN, 128))

    which = lax.broadcasted_iota(jnp.int32, (16, 16), 0)
    advantage = jnp.zeros((16, 16), F32)
    for g in range(16 // GROUP):
        rewards = [rew_ref[g * GROUP + r] for r in range(GROUP)]
        mean = sum(rewards[1:], rewards[0]) * (1.0 / GROUP)
        for r in range(GROUP):
            advantage = jnp.where(which == g * GROUP + r, rewards[r] - mean, advantage)
    weight = -(advantage * mask_ref[...].astype(F32)) * 1.25
    sids[own] = sid_ref[...]
    id_ref[rows_of(own * OWN, OWN)] = as_column(sid_ref[...].astype(F32))
    tw_ref[...] = as_column(weight)
    pl.semaphore_wait(barrier, len(peers))

    def hidden_copy(rel, step, way):
        who = me.peer(y=way, c=rel)
        to = other + (me.c + rel) % 2
        k = rel * STEPS + step
        return pltpu.make_async_remote_copy(
            src_ref=hid_ref.at[rows_of(step * STEP, STEP), pl.ds(al(to * WIDE, 128), WIDE)],
            dst_ref=hd.at[rows_of(own * OWN + step * STEP, STEP)],
            send_sem=hs.at[k],
            recv_sem=hr.at[k],
            device_id=who,
            device_id_type=MESH,
        )

    wrapped = [s for s in range(STEPS) if s not in DIRECT]
    hidden = {}
    for s in range(STEPS):
        for rel in range(2):
            hidden[rel, s] = hidden_copy(rel, s, toward if s in DIRECT else -toward)
    ahead = 3
    for s in (wrapped[0],) + DIRECT[:1]:
        for rel in range(2):
            hidden[rel, s].start()
    to_mate = send(
        hid_ref.at[:, pl.ds(al(mates * WIDE, 128), WIDE)], hd.at[rows_of(own * OWN, OWN)],
        cs.at[0], cr.at[0], mate,
    )
    for s in tuple(wrapped[1:ahead]) + DIRECT[1:]:
        for rel in range(2):
            hidden[rel, s].start()

    id_copies = [
        send(sids.at[own], sids.at[own], is_.at[i], ir.at[i], who) for i, who in enumerate((mate, across, across_mate))
    ]
    copy_w.wait()

    @pl.loop(0, 10)
    def _(i):
        at = pl.ds(al(i * 128, 128), 128)
        wt_ref[:, at] = w_ref[at, :].T

    copy_h.wait()
    to_mate.wait_recv()

    pout[...] = jnp.dot(hd[rows_of(mates * OWN, OWN), :], w_ref[...], preferred_element_type=F32)
    to_mate_part = send(pout, pland, ps.at[0], pr.at[0], mate)
    exchanged, crossed = [], []
    vocab = (lax.broadcasted_iota(jnp.int32, (STEP, VOCAB), 1) + offset).astype(F32)
    vocab_wide = (lax.broadcasted_iota(jnp.int32, (OWN, VOCAB), 1) + offset).astype(F32)

    def sampled_rows(j):
        chosen = jnp.where(vocab_wide == id_ref[rows_of(j * OWN, OWN), 0:1], 1.0, 0.0).astype(BF16)
        part[j] = jnp.dot(chosen, wt_ref[...], preferred_element_type=F32)

    sampled_rows(own)
    for s in range(STEPS):
        for rel in range(2):
            hidden[rel, s].wait_recv()
        both = jnp.concatenate(
            [hd[rows_of(mates_of * OWN + s * STEP, STEP), :], hd[rows_of(mine_of * OWN + s * STEP, STEP), :]], axis=0
        )
        term = jnp.dot(both, w_ref[...], preferred_element_type=F32)
        xout[s] = term[:STEP]
        exchanged.append(send(xout.at[s], xland.at[s], xs.at[s], xr.at[s], mate))
        if s in wrapped:
            i = wrapped.index(s) + ahead
            if i < len(wrapped):
                for rel in range(2):
                    hidden[rel, wrapped[i]].start()
        if s == 1:
            lex[...] = jnp.dot(hd[rows_of(own * OWN, OWN), :], w_ref[...], preferred_element_type=F32)
        if s == 2:
            for copy in id_copies:
                copy.wait_recv()
            for i in range(1, 4):
                j = (own + i) % 4
                id_ref[rows_of(j * OWN, OWN)] = as_column(sids[j].astype(F32))
        if 3 <= s < 6:
            sampled_rows((own + s - 2) % 4)
        exchanged[s].wait_recv()
        lout[s] = term[STEP:] + xland[s]
        crossed.append(send(lout.at[s], lland.at[s], ls.at[s], lr.at[s], across))

    grads = {}

    def grad_send(k, src, j, lo, n, who):
        grads[k] = send(src, gr.at[rows_of(j * OWN + lo, n)], gs.at[k], grs.at[k], who)

    to_mate_part.wait_recv()
    lane = lax.broadcasted_iota(jnp.int32, (STEP, 128), 1)
    k_of = lax.broadcasted_iota(jnp.int32, (STEP, STEP), 0)
    q_of = lax.broadcasted_iota(jnp.int32, (STEP, STEP), 1)
    earlier = jnp.where((q_of < k_of) & (q_of // 16 == k_of // 16), 1.0, 0.0).astype(BF16)
    for s in range(STEPS):
        crossed[s].wait_recv()
        at = pl.ds(s * STEP, STEP)
        ids = id_ref[rows_of(own * OWN + s * STEP, STEP), 0:1]
        chosen = vocab == ids
        tally = jnp.dot(earlier, jnp.where(chosen, 1.0, 0.0).astype(BF16), preferred_element_type=F32)
        tally = tally + jnp.concatenate(
            [jnp.broadcast_to(prompt[2 * s + i : 2 * s + i + 1, :], (16, VOCAB)) for i in range(2)], axis=0
        )
        penalty = recurrence_deduction * tally + jnp.where(tally > 0.0, presence_deduction, 0.0)
        scaled = (lex[at, :] + pland[at, :] + lland[s] - penalty) * 1.25
        m = jnp.max(scaled, axis=1, keepdims=True)
        raised = jnp.exp(scaled - m)
        l = jnp.sum(raised, axis=1, keepdims=True)
        p = jnp.sum(jnp.where(chosen, scaled, 0.0), axis=1, keepdims=True)
        raw[at, :] = jnp.where(chosen, 0.0, raised).astype(BF16)
        table = jnp.zeros((STEP, 128), F32)
        for i, v in enumerate((m, l, p, tw_ref[at, 0:1])):
            table = jnp.where(lane == i, v, table)
        st[at, :] = table
        if s % 2:
            lo, n = (s - 1) * STEP, 2 * STEP
            grad_send(s // 2, raw.at[pl.ds(lo, n)], own, lo, n, across)
        if s % 4 == 3:
            lo, n = (s - 3) * STEP, 4 * STEP
            grad_send(4 + s // 4, raw.at[pl.ds(lo, n)], own, lo, n, mate)
    first = st[...].T[0:8]
    m, l, p, weight = [first[i : i + 1] for i in range(4)]
    own_m, across_rows = m, first
    stats = []

    def product(j, lo, n, src, base):
        plain[rows_of(j * OWN + lo, n)] = jnp.dot(
            src[rows_of(base + lo, n), :], wt_ref[...], preferred_element_type=F32
        )

    def relay(i):
        grads[i].wait_recv()
        grad_send(6 + i, gr.at[rows_of(mine_of * OWN + i * 64, 64)], mine_of, i * 64, 64, mate)

    for stage, where in enumerate((Z_PEERS, XY_PEERS)):
        mine[stage] = across_rows
        copies = []
        for i, s in enumerate(where):
            k = stage * 7 + i
            copies.append(send(mine.at[stage], sland.at[k], ss.at[k], sr.at[k], me.peer(**s)))
        if stage == 0:
            product(own, 0, OWN, raw, 0)
        else:
            grads[4].wait_recv()
            grads[5].wait_recv()
            product(mates, 0, OWN, gr, mates * OWN)
            relay(0)
            relay(1)
            product(mine_of, 0, PART, gr, mine_of * OWN)
        for copy in copies:
            copy.wait_recv()
        stats += copies
        m, l, p = merge(m, l, p, [sland[stage * 7 + i] for i in range(7)])
        across_rows = jnp.concatenate([m, l, p, jnp.zeros((5, OWN), F32)], axis=0)
    norm = m + jnp.log(l)
    logp = p - norm
    lp_ref[...] = jnp.concatenate([logp[:, 16 * r : 16 * r + 16] for r in range(16)], axis=0)

    tab[own] = jnp.concatenate(
        [weight * jnp.exp(own_m - norm), weight * (1.0 - jnp.exp(logp)), jnp.zeros((6, OWN), F32)], axis=0
    )
    tables = [send(tab.at[own], tab.at[own], ts.at[i], tr.at[i], who) for i, who in enumerate((mate, across, across_mate))]

    def scale(j, t):
        table, at_j = tab[j][:, t * PART : (t + 1) * PART], rows_of(j * OWN + t * PART, PART)
        cols[at_j] = jnp.concatenate([table, jnp.zeros((120, PART), F32)], axis=0).T

        @pl.loop(0, PART // STEP)
        def _(i):
            lo = t * PART + i * STEP
            at, to = rows_of(lo, STEP), rows_of(j * OWN + lo, STEP)
            part[j, at] = cols[to, 1:2] * part[j, at] - cols[to, 0:1] * plain[to, :]

    def turn(lo, hi):
        @pl.loop(lo, hi)
        def _(i):
            at = rows_of(i * STEP, STEP)
            g = jnp.where(vocab == id_ref[at, 0:1], cols[at, 1:2], -cols[at, 0:1] * gr[at, :].astype(F32))
            gr[at] = g.astype(BF16)

    def z_get(half, sub, chunk):
        ylo = me.ylo if half == EARLY else 1 - me.ylo
        return part[2 * ylo, rows_of(sub * PART + chunk * 16, 16), :]

    def x_get(half, sub, chunk):
        ylo = me.ylo if half == EARLY else 1 - me.ylo
        return part[2 * ylo + 1, rows_of(sub * PART + chunk * 32, 32), :]

    zring = Ring(NZ, me.z, z_get, zout, zland, zs, zr, me.peer(z=1), me.peer(z=-1))
    xring = Ring(NX, me.x, x_get, xrout, xrland, xrs, xrr, me.peer(x=1), me.peer(x=-1))
    def begin(half, t):
        zring.step(half, t, 0)
        xring.step(half, t, 0)

    def late(t):
        if t == 0:
            tables[1].wait_recv()
            tables[2].wait_recv()
        for i in (2 * t, 2 * t + 1):
            grads[6 + i].wait_recv()
        product(mates_of, t * PART, PART, gr, mates_of * OWN)

        @pl.loop(0, 2)
        def _(i):
            scale(other + i, t)

        begin(LATE, t)

    scale(own, 0)
    scale(own, 1)
    tables[0].wait_recv()
    scale(mates, 0)
    scale(mates, 1)
    begin(EARLY, 0)
    relay(2)
    begin(EARLY, 1)
    relay(3)
    late(0)
    product(mine_of, PART, PART, gr, mine_of * OWN)
    zring.step(EARLY, 0, 1)
    xring.step(EARLY, 0, 1)
    late(1)
    zring.step(EARLY, 1, 1)
    xring.step(EARLY, 1, 1)
    zring.step(LATE, 0, 1)
    xring.step(LATE, 0, 1)
    zring.step(EARLY, 0, 2)
    zring.step(EARLY, 1, 2)
    zring.step(LATE, 1, 1)
    xring.step(LATE, 1, 1)
    zring.step(LATE, 0, 2)
    zring.step(EARLY, 0, 3)
    zring.step(EARLY, 1, 3)
    for i in range(6, 10):
        grads[i].wait_send()
    own_at = rows_of(own * OWN, OWN)
    gr[own_at] = raw[...]

    def weight_tiles(lo, hi):
        @pl.loop(lo, hi)
        def _(i):
            at = pl.ds(al(i * 128, 128), 128)
            gw_tiles[at, :] = lax.dot_general(
                hd[:, at], gr[...], (((0,), (0,)), ((), ())), preferred_element_type=F32
            ).astype(BF16)

    def cut(ref, at):
        rows = rows_of((at // 2) * 16, 16)
        return ref.at[:, rows, pl.ds(al((at % 2) * 640, 128), 640)]

    later = []
    zring.step(LATE, 1, 2)
    for half, ylo in ((EARLY, me.ylo), (LATE, 1 - me.ylo)):
        for sub in range(2):
            x2[ylo, pl.ds(sub * 32, 32)] = xring.total(half, sub).astype(BF16)
    x_copies = []
    for i in range(1, NZ):
        x_copies.append(
            send(cut(x2, (me.z + i) % NZ), x2land.at[i - 1], x2s.at[i - 1], x2r.at[i - 1], me.peer(z=i))
        )
    zring.step(LATE, 0, 3)
    turn(0, 8)
    zring.step(LATE, 1, 3)
    turn(8, 16)
    for half, ylo in ((EARLY, me.ylo), (LATE, 1 - me.ylo)):
        for sub in range(2):
            z2[ylo, pl.ds(sub * 16, 16)] = zring.total(half, sub).astype(BF16)
    z_copies = []
    for i in range(1, NX):
        z_copies.append(
            send(cut(z2, (me.x + i) % NX), z2land.at[i - 1], z2s.at[i - 1], z2r.at[i - 1], me.peer(x=i))
        )
    turn(16, 32)
    for core, (ours, land, copies) in enumerate(
        ((cut(z2, me.x), z2land, z_copies), (cut(x2, me.z), x2land, x_copies))
    ):
        for copy in copies:
            copy.wait_recv()
        term = ours[...].astype(F32)
        for i in range(len(copies)):
            term = term + land[i].astype(F32)
        ysum[core] = term.astype(BF16)
        later += copies

    def kept_rows(core, x, z):
        return 16 * z + PART * (x // 2) if core == 0 else 32 * x + PART * (z // 4) + 16 * ((z // 2) % 2)

    def kept_cols(core, x, z):
        return (x % 2 if core == 0 else z % 2) * 640

    y_copies = {}
    for i, s in enumerate(Y_PEERS):
        piece = ysum.at[(me.c + s["c"]) % 2, (me.ylo + s["y"]) % 2]
        y_copies[s["y"], s["c"]] = send(piece, yland.at[i], ys.at[i], yr.at[i], me.peer(**s))
    weight_tiles(0, 3)
    gw_out = pltpu.make_async_copy(gw_tiles, gw_ref, loc.at[6])
    row, col = kept_rows(0, me.x, me.z), kept_cols(0, me.x, me.z)
    row = jnp.where(me.c == 0, row, kept_rows(1, me.x, me.z))
    col = jnp.where(me.c == 0, col, kept_cols(1, me.x, me.z))
    for dc in range(2):
        for dy in range(2):
            pair = []
            for y in (dy, dy + 2):
                if (y, dc) == (0, 0):
                    pair.append(ysum[me.c, me.ylo].astype(F32))
                else:
                    mirror = ((NY - y) % NY, dc)
                    y_copies[mirror].wait_recv()
                    pair.append(yland[Y_PEERS.index(dict(y=mirror[0], c=mirror[1]))].astype(F32))
            owner = ((me.ylo + dy) % 2) * 2 + (me.c + dc) % 2
            gather[owner, rows_of(row, 16), pl.ds(al(col, 128), 640)] = (pair[0] + pair[1]).astype(BF16)
    later += list(y_copies.values())

    def piece(core, x, z):
        rows, at = rows_of(kept_rows(core, x, z), 16), pl.ds(al(kept_cols(core, x, z), 128), 640)
        return gather.at[:, rows, at]

    def z_off(i):
        return (me.z + i + NZ) % NZ

    def x_off(i):
        return (me.x + i + NX) % NX

    def put(copies, key, src, who):
        k = len(copies)
        copies[key] = send(src, src, bs.at[k], br.at[k], who)

    @pl.when(me.c == 0)
    def _():
        mine = piece(0, me.x, me.z)
        firsts = {i: send(mine, mine, as_.at[i - 1], ar.at[i - 1], me.peer(x=i)) for i in (2, 1, 3)}
        copies, order = {}, (0, 1, 3, 2)
        hops = lambda q, d: NZ // 2 - (0 if (d == 1) == (q in (0, 3)) else 1)
        for h in range(NZ // 2):
            for q in order:
                if h == 0 and q:
                    firsts[q].wait_recv()
                for d in (1, -1):
                    if h >= hops(q, d):
                        continue
                    if h:
                        copies[q, d, h - 1].wait_recv()
                    put(copies, (q, d, h), piece(0, x_off(-q), z_off(-d * h)), me.peer(z=d))
                if h == 0 and q == 0:
                    weight_tiles(3, 7)
            if h == 0:
                weight_tiles(7, 10)
                gw_out.start()
        for q in order:
            for d in (1, -1):
                copies[q, d, hops(q, d) - 1].wait_recv()
        for copy in list(firsts.values()) + list(copies.values()):
            copy.wait_send()

    @pl.when(me.c == 1)
    def _():
        copies, xcopies = {}, {}
        mine = piece(1, me.x, me.z)

        def along_x(dz):
            at = piece(1, me.x, z_off(dz))
            for d in (1, -1):
                put(xcopies, (dz, d), at, me.peer(x=d))

        firsts = {}
        for i, away in enumerate((2, -2, 1, -1)):
            firsts[away] = send(mine, mine, as_.at[i], ar.at[i], me.peer(z=away))
        along_x(0)
        weight_tiles(3, 7)
        for d in (1, -1):
            firsts[2 * d].wait_recv()
            came = piece(1, me.x, z_off(-2 * d))
            half = came.at[pl.ds(0 if d == 1 else 2, 2)]
            k = 4 if d == 1 else 6
            firsts[4 * d] = send(half, half, as_.at[k], ar.at[k], me.peer(z=2 * d))
            firsts[3 * d] = send(came, came, as_.at[k + 1], ar.at[k + 1], me.peer(z=d))
        for d in (1, -1):
            firsts[d].wait_recv()
            along_x(-d)
        for d in (1, -1):
            along_x(-2 * d)
        for d in (1, -1):
            firsts[3 * d].wait_recv()
            along_x(-3 * d)
        weight_tiles(7, 10)
        gw_out.start()
        for d in (1, -1):
            firsts[4 * d].wait_recv()
        along_x(-4)
        for dz in (0, -1, 1, -2, 2, -3, 3, -4):
            d = 1 if dz % 2 == 0 else -1
            xcopies[dz, d].wait_recv()
            put(xcopies, (dz, 2), piece(1, x_off(-d), z_off(dz)), me.peer(x=d))
        for dz in (0, -1, 1, -2, 2, -3, 3, -4):
            d = 1 if dz % 2 == 0 else -1
            xcopies[dz, -d].wait_recv()
            xcopies[dz, 2].wait_recv()
        for copy in list(firsts.values()) + list(xcopies.values()):
            copy.wait_send()

    outs = []
    for s in range(4):
        copy = pltpu.make_async_copy(gather.at[s], gh_ref.at[:, pl.ds(s * WIDE, WIDE)], loc.at[2 + s])
        copy.start()
        outs.append(copy)
    zring.finish()
    xring.finish()
    to_mate.wait_send()
    to_mate_part.wait_send()
    for copy in later + id_copies + exchanged + crossed + stats + tables + list(hidden.values()) + [grads[i] for i in range(6)]:
        copy.wait_send()
    for copy in outs + [gw_out]:
        copy.wait()


def fused(hidden, head_weight, prompt_ids, prompt_counts, sampled_ids, token_mask, rewards):
    vmem = pl.BlockSpec(memory_space=pltpu.VMEM)
    smem = pl.BlockSpec(memory_space=pltpu.SMEM)
    hbm = pl.BlockSpec(memory_space=pl.ANY)
    dma = lambda n: pltpu.SemaphoreType.DMA((n,))
    buf = lambda *shape: pltpu.VMEM(shape, BF16)
    wide = lambda *shape: pltpu.VMEM(shape, F32)
    return pl.pallas_call(
        kernel,
        out_shape=(
            jax.ShapeDtypeStruct((16, 16), F32),
            jax.ShapeDtypeStruct((OWN, 4 * WIDE), BF16),
            jax.ShapeDtypeStruct((WIDE, VOCAB), BF16),
        ),
        in_specs=[hbm, hbm, vmem, vmem, vmem, vmem, smem],
        out_specs=(vmem, hbm, hbm),
        scratch_shapes=[
            buf(WIDE, VOCAB), buf(VOCAB, WIDE), buf(ALL, WIDE), wide(OWN, VOCAB), wide(OWN, VOCAB), wide(OWN, VOCAB),
            wide(STEPS, STEP, VOCAB), wide(STEPS, STEP, VOCAB), wide(STEPS, STEP, VOCAB), wide(STEPS, STEP, VOCAB),
            wide(16, VOCAB), pltpu.VMEM((4, 16, 16), jnp.int32), wide(ALL, 128), wide(OWN, 128), wide(OWN, 128), wide(2, 8, OWN), wide(14, 8, OWN),
            wide(4, 8, OWN), wide(ALL, 128),
            buf(OWN, VOCAB), buf(ALL, VOCAB), wide(4, OWN, WIDE), wide(ALL, WIDE), buf(WIDE, VOCAB),
            buf(28, 16, 1280), buf(28, 16, 1280), buf(12, 32, 1280), buf(12, 32, 1280),
            buf(2, 32, 1280), buf(2, 64, 1280), buf(3, 2, 16, 640), buf(7, 2, 16, 640), buf(2, 2, 16, 640),
            buf(7, 16, 640), buf(4, OWN, WIDE),
            dma(7), dma(3), dma(3), dma(16), dma(16), dma(1), dma(1), dma(1), dma(1), dma(8), dma(8), dma(8), dma(8),
            dma(14), dma(14), dma(10), dma(10), dma(3), dma(3),
            dma(28), dma(28), dma(12), dma(12), dma(3), dma(3), dma(7), dma(7), dma(7), dma(7),
            dma(8), dma(8), dma(28), dma(28),
        ],
        compiler_params=pltpu.CompilerParams(
            collective_id=0, has_side_effects=True, vmem_limit_bytes=56 << 20
        ),
        name="fused",
    )(hidden, head_weight, prompt_ids, prompt_counts, sampled_ids, token_mask, rewards)


def solution(mesh):
    return jax.shard_map(
        fused,
        mesh=mesh,
        in_specs=(
            P("dp", None),
            P("dp", "tensor"),
            P("dp", None),
            P("dp", None),
            P("dp", None),
            P("dp", None),
            P("dp"),
        ),
        out_specs=(P("dp", None), P("dp", None), P("dp", "tensor")),
        check_vma=False,
    )
```
